32 devices in a mesh: fsdp: 8 (over z, x), expert: 4 (over y, core).
Axes of the slice: x: 2, y: 2, z: 4, core: 2. Of those that a mesh axis runs over, the one named last changes fastest.
Arguments:
- inputs: bfloat16 [2, 32, 197, 512], P(None, ('fsdp', 'expert')), may hold values from -6 to 6
- gain_attn: bfloat16 [512], P('fsdp'), may hold values from 0.5 to 1.5
- qkv_weight: bfloat16 [512, 1536], P('fsdp'), may hold values from -0.25 to 0.25
- out_weight: bfloat16 [512, 512], P('fsdp'), may hold values from -2 to 2
- gain_moe: bfloat16 [512], P('fsdp'), may hold values from 0.5 to 1.5
- router_weight: bfloat16 [512, 8], P('fsdp'), may hold values from -0.1875 to 0.1875
- expert_in: bfloat16 [8, 512, 2048], P('expert', 'fsdp'), may hold values from -0.25 to 0.25
- expert_out: bfloat16 [8, 2048, 512], P('expert', 'fsdp'), may hold values from -2 to 2
- routes: int32 [2, 32, 197, 2], P(None, ('fsdp', 'expert')), may hold values from 0 to 7, all different within a row; in each aligned block of 197 rows (0 to 196, 197 to 393, ..., all dimensions but the last counted through in order) at most 62 rows name the same one
- cotangent: bfloat16 [2, 32, 197, 512], P(None, ('fsdp', 'expert')), may hold values from -6 to 6
Outputs:
- activations: bfloat16 [2, 32, 197, 512], P(None, ('fsdp', 'expert'))
- input_grad: float32 [2, 32, 197, 512], P(None, ('fsdp', 'expert'))
- grad_gain_attn: float32 [512], P('fsdp')
- grad_qkv: float32 [512, 1536], P('fsdp')
- grad_out: float32 [512, 512], P('fsdp')
- grad_gain_moe: float32 [512], P('fsdp')
- grad_router: float32 [512, 8], P('fsdp')
- grad_expert_in: float32 [8, 512, 2048], P('expert', 'fsdp')
- grad_expert_out: float32 [8, 2048, 512], P('expert', 'fsdp')
The draws below stay inside these ranges and needn't reach their ends.
Inputs may be any that keep to these rules, and one draw needn't show every extreme that they name: `routes`: each token names two different experts; among the 197 tokens of one device in one micro-batch no expert is named more than 62 times, a bound that some block reaches.
All inputs are finite; a program needn't handle non-finite values.
Results may differ from the reference program's by a relative error of at most 0.023.
Values may be sent and summed in bfloat16 or wider, within the bound.
A program may use at most 128 MiB of HBM per device.

```python
import math
import jax
import jax.numpy as jnp
import numpy as np
from jax import lax

D = 512
HEADS = 8
HEAD_DIM = 64
FF = 2048
SEQ = 197
EXPERTS = 8
IMG_DEV = 1
MICRO = 2
IMAGES = 32
ROWS = 197
CAP = 62
N_FSDP = 8
N_EXPERT = 4


def shard_levels(own_key, shape, shards, low, high):
    level, own = 1.0, jax.random.fold_in(own_key, 6)
    for axis_at, blocks in shards:
        steps = jnp.exp(jax.random.uniform(jax.random.fold_in(own, axis_at), (blocks,), jnp.float32, low / len(shards), high / len(shards)))
        level = level * jnp.repeat(steps, shape[axis_at] // blocks).reshape([-1 if axis == axis_at else 1 for axis in range(len(shape))])
    return level


def shared_out(key, own, number, rows, number_of, top, most, lean):
    sequence = jax.random.permutation(key, number_of)
    packed, usual = portions_of(number_of, rows * top, most, lean, True), portions_of(number_of, rows * top, most, lean, False)
    places = jnp.arange(number_of)

    def named(lengths, rotation):
        used = int((lengths > 0).sum())
        fixed = max(1, used // 4)
        moved = fixed + (places - fixed + rotation * (used - fixed)) % max(1, number_of - fixed)
        return jnp.zeros((number_of,), jnp.int32).at[sequence[jnp.where(places < fixed, places, moved)]].set(jnp.asarray(lengths, jnp.int32))

    lengths = jnp.where(number % 4 == 0, named(packed, number // 4), named(usual, number - number // 4 - 1))
    mixed = jax.random.permutation(jax.random.fold_in(own, 3), number_of)
    donor, taker = mixed[0:number_of // 2 * 2:2], mixed[1:number_of // 2 * 2:2]
    margin = jnp.minimum(lengths[donor] - 1, most - lengths[taker]) // 2
    margin = jnp.where((donor == sequence[0]) | (taker == sequence[0]) | (lengths[taker] == 0), 0, jnp.maximum(margin, 0))
    moved = jax.random.randint(jax.random.fold_in(own, 4), (number_of // 2,), 0, 1 << 20) % (margin + 1)
    lengths = lengths.at[donor].add(-moved).at[taker].add(moved)
    items = jnp.searchsorted(jnp.cumsum(lengths), jnp.arange(rows * top), side="right").astype(jnp.int32)
    table = items.reshape(top, rows).T
    table = table[jax.random.permutation(jax.random.fold_in(own, 1), rows)]
    rotation = jax.random.randint(jax.random.fold_in(own, 2), (rows, 1), 0, top)
    return jnp.take_along_axis(table, (jnp.arange(top)[None, :] + rotation) % top, axis=1)


def portions_of(number_of, total, limit, skew, full):
    loads = [(1 << 20) // math.isqrt(standing ** skew) + 1 for standing in range(1, number_of + 1)]
    largest = limit if full else min(limit, max(-(-total // number_of), total * loads[0] // sum(loads)))
    least = 1 if total - largest >= number_of - 1 else 0
    given, spare = [largest] + [least] * (number_of - 1), total - largest - least * (number_of - 1)
    while spare > 0:
        free = [i for i in range(1, number_of) if given[i] < largest] or [i for i in range(1, number_of) if given[i] < limit]
        mass, remaining = sum([loads[i] for i in free]), spare
        for i in free:
            extra = min(limit - given[i], max(1, remaining * loads[i] // mass), spare)
            given[i] = given[i] + extra
            spare = spare - extra
    return np.array(given)


def noise(rng, extent, scale, limit, shards=(), held_as=jnp.bfloat16):
    entries = scale * jax.random.normal(rng, extent, jnp.float32)
    if shards:
        entries = entries * shard_levels(rng, extent, shards, -0.22, 0.18)
    return jnp.clip(entries, -limit, limit).astype(held_as)


def setup_inputs(seed: int = 0) -> dict:
    splits = jax.random.split(jax.random.key(seed), 11)
    inputs = noise(splits[0], (MICRO, IMAGES, SEQ, D), 1.0, 6.0, ((1, 32),))
    gain_attn = jnp.clip(1.0 + 0.1 * jax.random.normal(splits[1], (D,), jnp.float32), 0.5, 1.5).astype(jnp.bfloat16)
    qkv_weight = noise(splits[2], (D, 3 * D), D ** -0.5, 0.25, ((0, 8),))
    out_weight = noise(splits[3], (D, D), (D // 64) ** -0.5, 2.0, ((0, 8),))
    gain_moe = jnp.clip(1.0 + 0.1 * jax.random.normal(splits[4], (D,), jnp.float32), 0.5, 1.5).astype(jnp.bfloat16)
    router_weight = noise(splits[5], (D, EXPERTS), (2 * D) ** -0.5, 0.1875, ((0, 8),))
    expert_in = noise(splits[6], (EXPERTS, D, FF), D ** -0.5, 0.25, ((0, 4), (1, 8)))
    expert_out = noise(splits[7], (EXPERTS, FF, D), (max(FF // 256, 1)) ** -0.5, 2.0, ((0, 4), (1, 8)))
    routes_keys = jax.random.split(jax.random.fold_in(splits[8], 1), MICRO * IMAGES * SEQ // ROWS)
    routes_turns = jax.random.permutation(jax.random.fold_in(splits[8], 3), MICRO * IMAGES * SEQ // ROWS)
    routes = jax.vmap(lambda own, number: shared_out(jax.random.fold_in(splits[8], 2), own, number, ROWS, EXPERTS, 2, CAP, 0))(routes_keys, routes_turns).reshape((MICRO, IMAGES, SEQ, 2))
    cotangent = noise(splits[9], (MICRO, IMAGES, SEQ, D), 1.0, 6.0, ((1, 32),))
    return dict(inputs=inputs, gain_attn=gain_attn, qkv_weight=qkv_weight, out_weight=out_weight, gain_moe=gain_moe, router_weight=router_weight, expert_in=expert_in, expert_out=expert_out, routes=routes, cotangent=cotangent)


@jax.custom_vjp
def low(v):
    return lax.optimization_barrier(v.astype(jnp.bfloat16)).astype(jnp.float32)

@jax.custom_vjp
def low_back(v):
    return v

def low_keep(v):
    return (low(v), None)

def low_pass(kept, grad):
    return (grad,)

def back_keep(v):
    return (v, None)

def back_low(kept, grad):
    return (low(grad),)
low.defvjp(low_keep, low_pass)
low_back.defvjp(back_keep, back_low)
EPS = 1e-06

def layer_norm(values, gain):
    center = lax.optimization_barrier(jnp.mean(values, axis=-1, keepdims=True))
    shifted = values - center
    spread = lax.optimization_barrier(jnp.mean(shifted * shifted, axis=-1, keepdims=True))
    return shifted * lax.rsqrt(spread + EPS) * gain

def slot_table(routed, count):
    order = jnp.transpose(routed).reshape(-1)
    onehot = (order[:, None] == jnp.arange(count, dtype=jnp.int32)[None, :]).astype(jnp.int32)
    ranks = (jnp.cumsum(onehot, axis=0) - 1).astype(jnp.int32)
    placed = lax.optimization_barrier(jnp.sum(onehot * ranks, axis=1)).astype(jnp.int32)
    return jnp.transpose(placed.reshape(2, -1)).astype(jnp.int32)

def block_forward(tokens, gain_one, qkv_w, out_w, gain_two, router_w, first_w, second_w, routed, places):
    exact = lax.Precision.HIGHEST
    scale = 1.0 / math.sqrt(HEAD_DIM)
    normed = low(layer_norm(tokens, gain_one))
    joined = low(low_back(jnp.dot(normed, qkv_w, precision=exact)))
    split = joined.reshape(IMG_DEV, SEQ, 3, HEADS, HEAD_DIM)
    query, keys, values = (split[:, :, 0], split[:, :, 1], split[:, :, 2])
    scores = low_back(jnp.einsum('bqhd,bkhd->bhqk', query, keys, precision=exact) * scale)
    probs = low(jax.nn.softmax(scores, axis=-1))
    attended = jnp.einsum('bhqk,bkhd->bqhd', probs, values, precision=exact).reshape(ROWS, D)
    attended = low(low_back(attended))
    middle = tokens + low_back(jnp.dot(attended, out_w, precision=exact))
    normed_two = low(layer_norm(middle, gain_two))
    logits = low_back(jnp.dot(normed_two, router_w, precision=exact))
    gates = jax.nn.softmax(logits, axis=-1)
    chosen = jnp.take_along_axis(gates, routed, axis=1)
    buffer = jnp.zeros((EXPERTS * CAP, D), jnp.float32).at[places.reshape(-1)].set(jnp.repeat(normed_two, 2, axis=0))
    buffer = low_back(buffer).reshape(EXPERTS, CAP, D)
    hidden = low_back(jnp.einsum('ecd,edf->ecf', buffer, first_w, precision=exact))
    acted = low(jax.nn.gelu(hidden))
    results = low(low_back(jnp.einsum('ecf,efd->ecd', acted, second_w, precision=exact)))
    picked = results.reshape(EXPERTS * CAP, D)[places]
    return middle + lax.optimization_barrier(jnp.sum(chosen[..., None] * picked, axis=1))

def reference(inputs, gain_attn, qkv_weight, out_weight, gain_moe, router_weight, expert_in, expert_out, routes, cotangent):
    blocks = MICRO * N_FSDP * N_EXPERT
    token_blocks = inputs.reshape(blocks, ROWS, D)
    route_blocks = routes.reshape(blocks, ROWS, 2)
    grad_blocks = cotangent.reshape(blocks, ROWS, D)
    params = (gain_attn.astype(jnp.float32), qkv_weight.astype(jnp.float32), out_weight.astype(jnp.float32), gain_moe.astype(jnp.float32), router_weight.astype(jnp.float32), expert_in.astype(jnp.float32), expert_out.astype(jnp.float32))

    def advance(carry, item):
        tokens, routed, upstream = item
        places = (routed * CAP + slot_table(routed, EXPERTS)).astype(jnp.int32)

        def forward(tok, gain_one, qkv_w, out_w, gain_two, router_w, first_w, second_w):
            return block_forward(tok, gain_one, qkv_w, out_w, gain_two, router_w, first_w, second_w, routed, places)
        result, pullback = jax.vjp(forward, tokens.astype(jnp.float32), *params)
        grads = pullback(upstream.astype(jnp.float32))
        updated = tuple((c + g for c, g in zip(carry, grads[1:])))
        return (updated, (result.astype(jnp.bfloat16), grads[0]))
    zeros = tuple((jnp.zeros_like(p) for p in params))
    totals, (results, token_grads) = lax.scan(advance, zeros, (token_blocks, route_blocks, grad_blocks))
    return (results.reshape(inputs.shape), token_grads.reshape(inputs.shape), totals[0], totals[1], totals[2], totals[3], totals[4], totals[5], totals[6])
```

```python
import functools
import math

import jax
import jax.numpy as jnp
from jax import lax
from jax.experimental import pallas as pl
from jax.experimental.pallas import tpu as pltpu
from jax.sharding import PartitionSpec as P

HEADS = 8
EPS = 1e-06
MESH = pl.DeviceIdType.MESH
F32 = jnp.float32
BF16 = jnp.bfloat16


def nn(a, b):
    return lax.dot_general(a, b, (((1,), (0,)), ((), ())), preferred_element_type=F32)


def nt(a, b):
    return lax.dot_general(a, b, (((1,), (1,)), ((), ())), preferred_element_type=F32)


def tn(a, b):
    return lax.dot_general(a, b, (((0,), (0,)), ((), ())), preferred_element_type=F32)


def normalize(values):
    center = jnp.mean(values, axis=-1, keepdims=True)
    shifted = values - center
    spread = jnp.mean(shifted * shifted, axis=-1, keepdims=True)
    rstd = lax.rsqrt(spread + EPS)
    return shifted * rstd, rstd


def normalize_back(grad, hat, rstd):
    return rstd * (
        grad
        - jnp.mean(grad, axis=-1, keepdims=True)
        - hat * jnp.mean(grad * hat, axis=-1, keepdims=True)
    )


class Semaphores:
    def __init__(self):
        self.used = 0

    def take(self, count):
        start = self.used
        self.used += count
        return start


def layout(mesh_shape, micro, seq, width, ff_width):
    fsdp, peers = mesh_shape["fsdp"], mesh_shape["expert"]
    c = {}
    c["nz"] = fsdp // 2
    c["E"] = peers
    c["G"] = peers // 2
    c["NE"] = 2 * peers
    c["T"] = seq
    c["TP"] = -(-seq // 16) * 16
    c["CP"] = -(-max(2, 10 * seq // (4 * 2 * peers) + 1) // 16) * 16
    c["S"] = c["NE"] * c["CP"]
    c["D"] = width
    c["FF"] = ff_width
    c["RF"] = width // fsdp
    c["CF"] = ff_width // fsdp
    c["TW"] = 4 * width // peers
    c["M"] = micro
    return c


def scratch_of(c):
    nz, E, G, NE, TP, CP, S, D, FF, RF, CF, TW, M = (
        c[k] for k in ("nz", "E", "G", "NE", "TP", "CP", "S", "D", "FF", "RF", "CF", "TW", "M")
    )
    h = nz // 2
    v = {
        "XP": ((M, TP, D), BF16),
        "CT": ((M, TP, D), BF16),
        "RT": ((M, TP, 128), jnp.int32),
        "DW": ((E, nz, 2, RF, TW), BF16),
        "SM": ((nz, 2, RF, 128), BF16),
        "WIN": ((nz, 2, RF, FF), BF16),
        "WOUT": ((nz, 2, CF, D), BF16),
        "N1": ((M, TP, D), BF16),
        "J": ((M, TP, 3 * D), BF16),
        "ATT": ((M, TP, D), BF16),
        "MID": ((M, TP, D), F32),
        "N2": ((M, TP, D), BF16),
        "GATES": ((M, TP, 128), F32),
        "PM": ((M, 2, TP, S), BF16),
        "XGS": ((M, 2, NE, CP, D), BF16),
        "XG": ((M, 2, NE, CP, D), BF16),
        "YD": ((M, 2, NE, CP, D), BF16),
        "RET": ((M, 2, NE, CP, D), BF16),
        "YACC": ((M, S, D), F32),
        "DXACC": ((M, S, D), F32),
        "AS": ((M, S, CF), BF16),
        "GHS": ((M, S, CF), BF16),
        "DWI": ((nz, 2, RF, FF), BF16),
        "DWO": ((nz, 2, CF, D), BF16),
        "UPI": ((nz, 2, RF, FF), BF16),
        "UPO": ((nz, 2, CF, D), BF16),
        "DNI": ((nz, 2, RF, FF), BF16),
        "DNO": ((nz, 2, CF, D), BF16),
        "FXI": ((RF, FF), BF16),
        "FXO": ((CF, D), BF16),
        "FYI": ((RF, FF), BF16),
        "FYO": ((CF, D), BF16),
        "GM": ((M, TP, D), F32),
        "GA": ((M, TP, D), BF16),
        "GJ": ((M, TP, 3 * D), BF16),
        "GR": ((8, D), F32),
        "PR": ((D, 128), F32),
        "DG": ((E, nz, 2, RF, TW), BF16),
        "SG": ((nz, 2, RF, 128), BF16),
        "RB1": ((G, nz, 2, RF, TW), BF16),
        "RY1": ((G, h, 2, RF, TW), BF16),
        "RX1": ((G, nz - h, RF, TW), BF16),
        "RX2": ((h, RF, TW), BF16),
        "RY2": ((G, nz - h, RF, TW), BF16),
        "RZ": ((nz, RF, TW), BF16),
        "FIN": ((E, RF, TW), BF16),
        "SH": ((nz, 2, RF, 128), BF16),
        "SB1": ((nz, 2, RF, 128), BF16),
        "SB2": ((G, nz, 2, RF, 128), BF16),
        "SB3": ((nz, RF, 128), BF16),
        "SB4": ((nz, RF, 128), BF16),
    }
    return v


def kernel(c, names, sem_count, *refs):
    nz, E, G, NE, T, TP, CP, S, D, FF, RF, CF, TW, M = (
        c[k]
        for k in ("nz", "E", "G", "NE", "T", "TP", "CP", "S", "D", "FF", "RF", "CF", "TW", "M")
    )
    (xin, cot, routes, qkv_s, out_s, small_s, ein, eout) = refs[:8]
    (act, igrad, gqkv, gout, gsmall, gein, geout) = refs[8:15]
    b = dict(zip(names, refs[15:]))
    SS, RS = refs[-2:]
    h = nz // 2
    nb = D // TW
    nq = 3 * nb
    head = D // HEADS
    pair = 2 * head
    scale = 1.0 / math.sqrt(head)
    sems = Semaphores()
    pending = []

    f = lax.axis_index("fsdp")
    e = lax.axis_index("expert")
    z, x = f // 2, f % 2
    y, core = e // 2, e % 2
    pme = 2 * e + x

    def at(zz, xx, ee):
        return (zz * 2 + xx, ee)

    sibling = at(z, x, y * 2 + (1 - core))
    across = at(z, 1 - x, e)

    def copy_of(src, dst, sem, device):
        return pltpu.make_async_remote_copy(
            src_ref=src,
            dst_ref=dst,
            send_sem=SS.at[sem],
            recv_sem=RS.at[sem],
            device_id=device,
            device_id_type=MESH,
        )

    def when(cond, run):
        if cond is None:
            run()
        else:
            pl.when(cond)(run)

    def send(src, dst, sem, device, cond=None, late=True):
        copy = copy_of(src, dst, sem, device)
        when(cond, copy.start)
        if late:
            pending.append((cond, copy))

    def arrived(dst, sem, cond=None):
        copy = copy_of(dst, dst, sem, sibling)
        when(cond, copy.wait_recv)

    def sent(src, sem, cond=None):
        copy = copy_of(src, src, sem, sibling)
        when(cond, copy.wait_send)

    DW, SM, WIN, WOUT = b["DW"], b["SM"], b["WIN"], b["WOUT"]
    for k in range(nq + nb):

        @pl.when(e == k)
        def _():
            shard = qkv_s if k < nq else out_s
            start = (k % nq) * TW
            DW[k, z, x] = shard[:, start : start + TW]

    SM[z, x] = small_s[...]
    WIN[z, x] = ein[x]
    WOUT[z, x] = eout[x]

    barrier = pltpu.get_barrier_semaphore()
    for dz in range(1, nz):
        pl.semaphore_signal(
            barrier, inc=1, device_id=at((z + dz) % nz, x, e), device_id_type=MESH
        )

    def greet(d, carry):
        p = (pme + d) % NE
        pl.semaphore_signal(barrier, inc=1, device_id=at(z, p % 2, p // 2), device_id_type=MESH)
        return carry

    lax.fori_loop(1, NE, greet, 0)
    pl.semaphore_wait(barrier, nz - 1 + NE - 1)

    s_dz, s_sz = sems.take(nz), sems.take(nz)
    for dz in range(1, nz):
        to = at((z + dz) % nz, x, e)
        send(DW.at[e, z, x], DW.at[e, z, x], s_dz + dz, to)
        send(SM.at[z, x], SM.at[z, x], s_sz + dz, to)

    s_xi, s_xo = sems.take(1), sems.take(1)
    send(ein.at[1 - x], WIN.at[z, x], s_xi, across)

    XP, CT, RT, PM = b["XP"], b["CT"], b["RT"], b["PM"]
    lane = lax.broadcasted_iota(jnp.int32, (TP, 128), 1)
    for m in range(M):
        XP[m] = jnp.zeros((TP, D), BF16)
        CT[m] = jnp.zeros((TP, D), BF16)
        RT[m] = jnp.full((TP, 128), -1, jnp.int32)
        XP[m, 0:T] = xin[m]
        CT[m, 0:T] = cot[m]
        RT[m, 0:T, 0:2] = routes[m]

    def onehot(m, j):
        return RT[m][:, j : j + 1] == lane

    before = (
        lax.broadcasted_iota(jnp.int32, (TP, TP), 1) < lax.broadcasted_iota(jnp.int32, (TP, TP), 0)
    ).astype(BF16)
    place = lax.broadcasted_iota(jnp.int32, (TP, S), 1)
    for m in range(M):
        first = onehot(m, 0).astype(F32)
        second = onehot(m, 1).astype(F32)
        rank0 = nn(before, first.astype(BF16))
        rank1 = nn(before, second.astype(BF16)) + jnp.sum(first, axis=0, keepdims=True)
        for j, (hot, rank) in enumerate(((first, rank0), (second, rank1))):
            slot = jnp.sum(hot * rank, axis=-1, keepdims=True).astype(jnp.int32)
            route = RT[m][:, j : j + 1]
            spot = jnp.where(route >= 0, route * CP + slot, -1)
            PM[m, j] = (place == spot).astype(BF16)

    s_zi = [sems.take(2 * nz), sems.take(2 * nz)]
    s_zo = [sems.take(2 * nz), sems.take(2 * nz)]

    def chain(kind, d, xs=(0, 1)):
        ref, base = (WIN, s_zi) if kind == "in" else (WOUT, s_zo)
        for i in xs:
            xx = x if i == 0 else 1 - x
            up_at, dn_at = z - d, z + d
            if d > 0:
                arrived(ref.at[up_at, xx], base[0] + 2 * d + i, up_at >= 0)
                arrived(ref.at[dn_at, xx], base[1] + 2 * d + i, dn_at < nz)
            if d < nz - 1:
                up_ok = (up_at >= 0) & (z < nz - 1)
                dn_ok = (dn_at < nz) & (z > 0)
                send(
                    ref.at[up_at, xx],
                    ref.at[up_at, xx],
                    base[0] + 2 * (d + 1) + i,
                    at((z + 1) % nz, x, e),
                    up_ok,
                )
                send(
                    ref.at[dn_at, xx],
                    ref.at[dn_at, xx],
                    base[1] + 2 * (d + 1) + i,
                    at((z + nz - 1) % nz, x, e),
                    dn_ok,
                )

    for dz in range(1, nz):
        zz = (z + nz - dz) % nz
        arrived(DW.at[e, zz, x], s_dz + dz)
        arrived(SM.at[zz, x], s_sz + dz)

    s_px, s_psm = sems.take(1), sems.take(1)
    s_py, s_f1, s_f2 = sems.take(G), sems.take(G), sems.take(G)
    s_c = sems.take(2 * G)
    send(DW.at[e, :, x], DW.at[e, :, x], s_px, across)
    send(SM.at[:, x], SM.at[:, x], s_psm, across)
    for d in range(1, G):
        send(DW.at[e, :, x], DW.at[e, :, x], s_py + d, at(z, x, ((y + d) % G) * 2 + core))

    def to_sibling(d, i):
        ee = ((y + G - d) % G) * 2 + core
        xx = x if i == 0 else 1 - x
        send(DW.at[ee, :, xx], DW.at[ee, :, xx], s_c + 2 * d + i, sibling)

    to_sibling(0, 0)
    chain("in", 0, (0,))
    arrived(WIN.at[z, 1 - x], s_xi)
    chain("in", 0, (1,))
    arrived(DW.at[e, :, 1 - x], s_px)
    for d in range(1, G):
        to = at(z, x, ((y + d) % G) * 2 + core)
        send(DW.at[e, 0:h, 1 - x], DW.at[e, 0:h, 1 - x], s_f1 + d, to)
    to_sibling(0, 1)
    for d in range(1, G):
        ee = ((y + G - d) % G) * 2 + core
        arrived(DW.at[ee, :, x], s_py + d)
        send(DW.at[ee, h:nz, x], DW.at[ee, h:nz, x], s_f2 + d, across)
        to_sibling(d, 0)
    for d in range(1, G):
        ee = ((y + G - d) % G) * 2 + core
        arrived(DW.at[ee, 0:h, 1 - x], s_f1 + d)
        arrived(DW.at[ee, h:nz, 1 - x], s_f2 + d)
        to_sibling(d, 1)
    send(eout.at[1 - x], WOUT.at[z, x], s_xo, across)
    arrived(SM.at[:, 1 - x], s_psm)
    for d in range(G):
        ee = ((y + G - d) % G) * 2 + (1 - core)
        arrived(DW.at[ee, :, x], s_c + 2 * d)
        arrived(DW.at[ee, :, 1 - x], s_c + 2 * d + 1)

    chain("in", 1)

    def dense(k):
        return DW[k].reshape(D, TW)

    small = SM[...].reshape(D, 128)
    row = lax.broadcasted_iota(jnp.int32, (8, 128), 0)
    col = lax.broadcasted_iota(jnp.int32, (8, 128), 1)
    pick = (((row == 0) & (col == 126)) | ((row == 1) & (col == 127))).astype(BF16)
    gains = nt(pick, small)
    gain_one, gain_two = gains[0:1], gains[1:2]
    key_ok = lax.broadcasted_iota(jnp.int32, (1, TP), 1) < T
    low_half = lax.broadcasted_iota(jnp.int32, (1, pair), 1) < head
    N1, J, ATT, MID, N2 = b["N1"], b["J"], b["ATT"], b["MID"], b["N2"]
    GATES, XGS, XG = b["GATES"], b["XGS"], b["XG"]

    def half_of(value, i):
        keep = low_half if i == 0 else jnp.logical_not(low_half)
        return jnp.where(keep, value, jnp.zeros_like(value))

    def softmax_scores(query, keys):
        scores = jnp.where(key_ok, nt(query, keys) * scale, -1e30)
        raised = jnp.exp(scores - jnp.max(scores, axis=-1, keepdims=True))
        return raised * (1.0 / jnp.sum(raised, axis=-1, keepdims=True))

    def columns(base, hp):
        return pl.ds(pl.multiple_of(base + hp * pair, 128), pair)

    def chosen_of(m, j):
        gates = GATES[m]
        return jnp.sum(jnp.where(onehot(m, j), gates, 0.0), axis=-1, keepdims=True)

    def forward(m):
        tokens = XP[m].astype(F32)
        hat, _ = normalize(tokens)
        N1[m] = (hat * gain_one).astype(BF16)
        for k in range(nq):
            J[m, :, k * TW : (k + 1) * TW] = nn(N1[m], dense(k)).astype(BF16)

        def attend(hp, carry):
            query, keys, values = (J[m, :, columns(i * D, hp)] for i in range(3))
            total = jnp.zeros((TP, pair), F32)
            for i in range(2):
                probs = softmax_scores(half_of(query, i), keys).astype(BF16)
                total = total + nn(probs, half_of(values, i))
            ATT[m, :, columns(0, hp)] = total.astype(BF16)
            return carry

        lax.fori_loop(0, D // pair, attend, 0)
        for k in range(nb):
            cols = slice(k * TW, (k + 1) * TW)
            MID[m, :, cols] = XP[m, :, cols].astype(F32) + nn(ATT[m], dense(nq + k))
        hat, _ = normalize(MID[m])
        N2[m] = (hat * gain_two).astype(BF16)
        logits = jnp.where(lane < NE, nn(N2[m], small), -1e30)
        raised = jnp.exp(logits - jnp.max(logits, axis=-1, keepdims=True))
        GATES[m] = raised / jnp.sum(raised, axis=-1, keepdims=True)
        upstream = CT[m].astype(F32)
        XGS[m, 0] = tn(PM[m, 0] + PM[m, 1], N2[m]).astype(BF16).reshape(NE, CP, D)
        placed = tn(PM[m, 0], (chosen_of(m, 0) * upstream).astype(BF16))
        placed = placed + tn(PM[m, 1], (chosen_of(m, 1) * upstream).astype(BF16))
        XGS[m, 1] = placed.astype(BF16).reshape(NE, CP, D)

    def exchange(src, dst, m, base):
        def one(d, carry):
            p = (pme + d) % NE
            copy_of(
                src.at[m, :, p], dst.at[m, :, pme], base + d, at(z, p % 2, p // 2)
            ).start()
            return carry

        lax.fori_loop(1, NE, one, 0)
        dst[m, :, pme] = src[m, :, pme]

    def exchanged(src, dst, m, base):
        def one(d, carry):
            p = (pme + NE - d) % NE
            copy_of(dst.at[m, :, p], dst.at[m, :, p], base + d, sibling).wait_recv()
            return carry

        lax.fori_loop(1, NE, one, 0)

    def exchange_sent(src, m, base):
        def one(d, carry):
            p = (pme + d) % NE
            copy_of(src.at[m, :, p], src.at[m, :, p], base + d, sibling).wait_send()
            return carry

        lax.fori_loop(1, NE, one, 0)

    s_go = [sems.take(NE) for _ in range(M)]
    s_back = [sems.take(NE) for _ in range(M)]
    for m in range(M):
        forward(m)
        exchange(XGS, XG, m, s_go[m])
        if m == 0:
            chain("in", 2) if nz > 2 else None
            chain("out", 0, (0,))
            arrived(WOUT.at[z, 1 - x], s_xo)
            chain("out", 0, (1,))
    for d in range(3, nz):
        chain("in", d)
    chain("out", 1)
    for m in range(M):
        exchanged(XGS, XG, m, s_go[m])

    YACC, DXACC, AS, GHS = b["YACC"], b["DXACC"], b["AS"], b["GHS"]
    DWI, DWO = b["DWI"], b["DWO"]
    YACC[...] = jnp.zeros_like(YACC)
    DXACC[...] = jnp.zeros_like(DXACC)
    c0, c1 = math.sqrt(2.0 / math.pi), 0.044715

    def expert_block(zc):
        for xx in range(2):
            cols = pl.ds(pl.multiple_of((2 * zc + xx) * CF, CF), CF)
            w_in = WIN[:, :, :, cols].reshape(D, CF)
            w_out = WOUT[zc, xx]

            def part(m, carry):
                tokens = XG[m, 0].reshape(S, D)
                grads = XG[m, 1].reshape(S, D)
                hidden = nn(tokens, w_in)
                grad_acted = nt(grads, w_out)
                square = hidden * hidden
                bent = jnp.tanh(c0 * hidden * (1.0 + c1 * square))
                acted = (0.5 * hidden * (1.0 + bent)).astype(BF16)
                slope = 0.5 * (1.0 + bent) + 0.5 * c0 * hidden * (1.0 - bent * bent) * (
                    1.0 + 3.0 * c1 * square
                )
                grad_hidden = (grad_acted * slope).astype(BF16)
                AS[m] = acted
                GHS[m] = grad_hidden
                YACC[m] = YACC[m] + nn(acted, w_out)
                DXACC[m] = DXACC[m] + nt(grad_hidden, w_in)
                return carry

            lax.fori_loop(0, M, part, 0)
            grads = XG[:, 1].reshape(M * S, D)
            tokens = XG[:, 0].reshape(M * S, D)
            DWO[zc, xx] = tn(AS[...].reshape(M * S, CF), grads).astype(BF16)
            DWI[:, :, :, cols] = (
                tn(tokens, GHS[...].reshape(M * S, CF)).astype(BF16).reshape(nz, 2, RF, CF)
            )

    turn = 1 - 2 * (z // h)
    for i in range(nz):
        if i >= 1:
            if i + 1 < nz:
                chain("out", i + 1)
        expert_block((z + turn * i + nz) % nz)

    YD, RET = b["YD"], b["RET"]
    for m in range(M):
        YD[m, 0] = YACC[m].astype(BF16).reshape(NE, CP, D)
        YD[m, 1] = DXACC[m].astype(BF16).reshape(NE, CP, D)
        exchange(YD, RET, m, s_back[m])

    UP, DN = (b["UPI"], b["UPO"]), (b["DNI"], b["DNO"])
    OWN = (DWI, DWO)
    s_up, s_dn = sems.take(4 * nz), sems.take(4 * nz)
    rounds = 2 * (nz - 1)

    def sums(r0, r1):
        def step(r, carry):
            for side, (got, base) in enumerate(((UP, s_up), (DN, s_dn))):
                place_z = z if side == 0 else nz - 1 - z
                j = r - place_z
                goal = nz - 1 - (j + 2 * nz) // 2 + nz
                ok = (j >= 0) & (goal > place_z)
                goal = goal if side == 0 else nz - 1 - goal
                goal = jnp.clip(goal, 0, nz - 1)
                xx = (1 - x + j + 2 * nz) % 2
                to = at((z + 1) % nz if side == 0 else (z + nz - 1) % nz, x, e)

                @pl.when(ok)
                def _():
                    for kind in range(2):
                        sem = base + 4 * goal + 2 * kind + xx

                        @pl.when(place_z > 0)
                        def _():
                            arrived(got[kind].at[goal, xx], sem)
                            OWN[kind][goal, xx] = OWN[kind][goal, xx] + got[kind][goal, xx]

                        copy_of(
                            OWN[kind].at[goal, xx], got[kind].at[goal, xx], sem, to
                        ).start()

            return carry

        lax.fori_loop(r0, r1, step, 0)

    s_fin = sems.take(2)
    FX, FY = (b["FXI"], b["FXO"]), (b["FYI"], b["FYO"])
    GE = (gein, geout)

    def sums_end():
        for kind in range(2):
            for i in range(2):
                xx = 1 - x if i == 0 else x
                up_sem = s_up + 4 * z + 2 * kind + xx
                dn_sem = s_dn + 4 * z + 2 * kind + xx
                arrived(UP[kind].at[z, xx], up_sem, z > 0)
                arrived(DN[kind].at[z, xx], dn_sem, z < nz - 1)

                @pl.when(z == 0)
                def _():
                    UP[kind][z, xx] = jnp.zeros(UP[kind].shape[2:], BF16)

                @pl.when(z == nz - 1)
                def _():
                    DN[kind][z, xx] = jnp.zeros(DN[kind].shape[2:], BF16)

                total = (
                    OWN[kind][z, xx].astype(F32)
                    + UP[kind][z, xx].astype(F32)
                    + DN[kind][z, xx].astype(F32)
                )
                if i == 0:
                    FX[kind][...] = total.astype(BF16)
                    send(FX[kind], FY[kind], s_fin + kind, across)
                else:
                    GE[kind][x] = total
        for kind in range(2):
            arrived(FY[kind], s_fin + kind)
            GE[kind][1 - x] = FY[kind][...].astype(F32)

        def clear(r, carry):
            for side, (got, base) in enumerate(((UP, s_up), (DN, s_dn))):
                place_z = z if side == 0 else nz - 1 - z
                goal = r // 2
                ok = (goal > z) if side == 0 else (goal < z)

                @pl.when(ok)
                def _():
                    for kind in range(2):
                        sent(OWN[kind].at[goal, r % 2], base + 4 * goal + 2 * kind + r % 2)

            return carry

        lax.fori_loop(0, 2 * nz, clear, 0)

    GM, GA, GJ, GR, PR = b["GM"], b["GA"], b["GJ"], b["GR"], b["PR"]
    DG, SG = b["DG"], b["SG"]
    GR[...] = jnp.zeros_like(GR)

    def backward_top(m):
        result = RET[m, 0].reshape(S, D)
        picked0 = nn(PM[m, 0], result)
        picked1 = nn(PM[m, 1], result)
        out = MID[m] + chosen_of(m, 0) * picked0 + chosen_of(m, 1) * picked1
        act[m] = out[0:T].astype(BF16)
        upstream = CT[m].astype(F32)
        gates = GATES[m]
        grad_gates = jnp.where(
            onehot(m, 0), jnp.sum(upstream * picked0, axis=-1, keepdims=True), 0.0
        ) + jnp.where(onehot(m, 1), jnp.sum(upstream * picked1, axis=-1, keepdims=True), 0.0)
        grad_logits = (
            gates * (grad_gates - jnp.sum(grad_gates * gates, axis=-1, keepdims=True))
        ).astype(BF16)
        router_part = tn(N2[m], grad_logits)
        PR[...] = router_part if m == 0 else PR[...] + router_part
        grad = nn(PM[m, 0] + PM[m, 1], RET[m, 1].reshape(S, D)) + nt(grad_logits, small)
        hat, rstd = normalize(MID[m])
        GR[1:2] = GR[1:2] + jnp.sum(grad * hat, axis=0, keepdims=True)
        grad_middle = upstream + normalize_back(grad * gain_two, hat, rstd)
        GM[m] = grad_middle
        branch = grad_middle.astype(BF16)
        N2[m] = branch
        back = None
        for k in range(nb):
            term = nt(branch[:, k * TW : (k + 1) * TW], dense(nq + k))
            back = term if back is None else back + term
        GA[m] = back.astype(BF16)

    def backward_heads(m):
        def attend(hp, carry):
            query, keys, values = (J[m, :, columns(i * D, hp)] for i in range(3))
            grads = GA[m, :, columns(0, hp)]
            grad_query = jnp.zeros((TP, pair), F32)
            grad_keys = jnp.zeros((TP, pair), F32)
            grad_values = jnp.zeros((TP, pair), F32)
            for i in range(2):
                part = half_of(query, i)
                upstream = half_of(grads, i)
                probs = softmax_scores(part, keys)
                grad_probs = nt(upstream, values)
                grad_values = grad_values + tn(probs.astype(BF16), upstream)
                grad_scores = (
                    probs
                    * (grad_probs - jnp.sum(grad_probs * probs, axis=-1, keepdims=True))
                ).astype(BF16)
                grad_query = grad_query + nn(grad_scores, half_of(keys, i))
                grad_keys = grad_keys + tn(grad_scores, part)
            GJ[m, :, columns(0, hp)] = (grad_query * scale).astype(BF16)
            GJ[m, :, columns(D, hp)] = (grad_keys * scale).astype(BF16)
            GJ[m, :, columns(2 * D, hp)] = grad_values.astype(BF16)
            return carry

        lax.fori_loop(0, D // pair, attend, 0)

    def backward_end(m):
        grad = None
        for k in range(nq):
            term = nt(GJ[m, :, k * TW : (k + 1) * TW], dense(k))
            grad = term if grad is None else grad + term
        hat, rstd = normalize(XP[m].astype(F32))
        GR[0:1] = GR[0:1] + jnp.sum(grad * hat, axis=0, keepdims=True)
        full = GM[m] + normalize_back(grad * gain_one, hat, rstd)
        igrad[m] = full[0:T]

    for m in range(M):
        exchanged(YD, RET, m, s_back[m])
        backward_top(m)
        sums(m, m + 1)
    for k in range(nb):
        part = tn(
            ATT[...].reshape(M * TP, D), N2[:, :, k * TW : (k + 1) * TW].reshape(M * TP, TW)
        )
        DG[nq + k] = part.astype(BF16).reshape(nz, 2, RF, TW)
    for m in range(M):
        backward_heads(m)
        sums(M + m, M + m + 1)
    for k in range(nq):
        part = tn(
            N1[...].reshape(M * TP, D), GJ[:, :, k * TW : (k + 1) * TW].reshape(M * TP, TW)
        )
        DG[k] = part.astype(BF16).reshape(nz, 2, RF, TW)
    for m in range(M):
        backward_end(m)
    gain_part = tn(GR[...].astype(BF16), pick)
    SG[...] = (PR[...] + gain_part).astype(BF16).reshape(nz, 2, RF, 128)

    RB1, RY1, RX1, RX2, RY2, RZ, FIN = (
        b[k] for k in ("RB1", "RY1", "RX1", "RX2", "RY2", "RZ", "FIN")
    )
    SH, SB1, SB2, SB3, SB4 = (b[k] for k in ("SH", "SB1", "SB2", "SB3", "SB4"))
    s_r1, s_ry1, s_rx1 = sems.take(G), sems.take(G), sems.take(G)
    s_rx2, s_ry2, s_rz, s_fe = sems.take(1), sems.take(G), sems.take(nz), sems.take(E)
    s_b1, s_b2, s_b3, s_b4 = sems.take(1), sems.take(G), sems.take(1), sems.take(nz)
    for j in range(G):
        send(DG.at[2 * j + 1 - core], RB1.at[j], s_r1 + j, sibling)
    send(SG, SB1, s_b1, sibling)
    for j in range(G):
        arrived(RB1.at[j], s_r1 + j)
        DG[2 * j + core] = DG[2 * j + core] + RB1[j]
    arrived(SB1, s_b1)
    SB2[y] = SG[...] + SB1[...]
    for d in range(1, G):
        q = (y + d) % G
        send(DG.at[2 * q + core, 0:h], RY1.at[y], s_ry1 + d, at(z, x, 2 * q + core))
        send(SB2.at[y], SB2.at[y], s_b2 + d, at(z, x, 2 * q + core))
    for j in range(G):
        send(DG.at[2 * j + core, h:nz, 1 - x], RX1.at[j], s_rx1 + j, across)
    sums(2 * M, 2 * M + 1) if rounds > 2 * M else None
    for d in range(1, G):
        q = (y + G - d) % G
        arrived(RY1.at[q], s_ry1 + d)
        DG[e, 0:h] = DG[e, 0:h] + RY1[q]
    send(DG.at[e, 0:h, 1 - x], RX2, s_rx2, across)
    for j in range(G):
        arrived(RX1.at[j], s_rx1 + j)
        DG[2 * j + core, h:nz, x] = DG[2 * j + core, h:nz, x] + RX1[j]
    for d in range(1, G):
        q = (y + d) % G
        send(DG.at[2 * q + core, h:nz, x], RY2.at[y], s_ry2 + d, at(z, x, 2 * q + core))
    for d in range(1, G):
        arrived(SB2.at[(y + G - d) % G], s_b2 + d)
    total = SB2[0].astype(F32)
    for j in range(1, G):
        total = total + SB2[j].astype(F32)
    SH[...] = total.astype(BF16)
    send(SH.at[:, 1 - x], SB3, s_b3, across)
    arrived(RX2, s_rx2)
    DG[e, 0:h, x] = DG[e, 0:h, x] + RX2[...]
    for d in range(1, G):
        q = (y + G - d) % G
        arrived(RY2.at[q], s_ry2 + d)
        DG[e, h:nz, x] = DG[e, h:nz, x] + RY2[q]
    for dz in range(1, nz):
        zz = (z + dz) % nz
        send(DG.at[e, zz, x], RZ.at[z], s_rz + dz, at(zz, x, e))
    arrived(SB3, s_b3)
    SH[:, x] = SH[:, x] + SB3[...]
    for dz in range(1, nz):
        zz = (z + dz) % nz
        send(SH.at[zz, x], SB4.at[z], s_b4 + dz, at(zz, x, e))
    for r in range(2 * M + 1, rounds):
        sums(r, r + 1)
    RZ[z] = DG[e, z, x]
    for dz in range(1, nz):
        arrived(RZ.at[(z + nz - dz) % nz], s_rz + dz)
    total = RZ[0].astype(F32)
    for k in range(1, nz):
        total = total + RZ[k].astype(F32)
    FIN[e] = total.astype(BF16)

    def spread(d, carry):
        copy_of(FIN.at[e], FIN.at[e], s_fe + d, at(z, x, (e + d) % E)).start()
        return carry

    lax.fori_loop(1, E, spread, 0)
    SB4[z] = SH[z, x]
    for dz in range(1, nz):
        arrived(SB4.at[(z + nz - dz) % nz], s_b4 + dz)
    total = SB4[0].astype(F32)
    for k in range(1, nz):
        total = total + SB4[k].astype(F32)
    gsmall[...] = total
    sums_end()

    def spread_done(d, carry):
        ee = (e + E - d) % E
        copy_of(FIN.at[ee], FIN.at[ee], s_fe + d, sibling).wait_recv()
        return carry

    lax.fori_loop(1, E, spread_done, 0)
    for k in range(nq):
        gqkv[:, k * TW : (k + 1) * TW] = FIN[k].astype(F32)
    for k in range(nb):
        gout[:, k * TW : (k + 1) * TW] = FIN[nq + k].astype(F32)

    for m in range(M):
        exchange_sent(XGS, m, s_go[m])
        exchange_sent(YD, m, s_back[m])

    def spread_sent(d, carry):
        copy_of(FIN.at[e], FIN.at[e], s_fe + d, sibling).wait_send()
        return carry

    lax.fori_loop(1, E, spread_sent, 0)
    for cond, copy in pending:
        when(cond, copy.wait_send)
    assert sems.used <= sem_count, sems.used


def body(
    mesh_shape,
    inputs,
    gain_attn,
    qkv_weight,
    out_weight,
    gain_moe,
    router_weight,
    expert_in,
    expert_out,
    routes,
    cotangent,
):
    micro, images, seq, width = inputs.shape
    c = layout(mesh_shape, micro, images * seq, width, expert_in.shape[2])
    rows, columns = images * seq, c["NE"]
    small = jnp.concatenate(
        [
            router_weight,
            jnp.zeros((c["RF"], 126 - columns), BF16),
            gain_attn[:, None],
            gain_moe[:, None],
        ],
        axis=1,
    )
    scratch = scratch_of(c)
    names = list(scratch)
    sem_count = 40 + 20 * c["nz"] + 8 * c["G"] + 4 * c["NE"] + c["E"]
    vmem = pl.BlockSpec(memory_space=pltpu.VMEM)
    shapes = (
        ((micro, rows, width), BF16),
        ((micro, rows, width), F32),
        (qkv_weight.shape, F32),
        (out_weight.shape, F32),
        ((c["RF"], 128), F32),
        (expert_in.shape, F32),
        (expert_out.shape, F32),
    )
    act, igrad, gqkv, gout, gsmall, gein, geout = pl.pallas_call(
        functools.partial(kernel, c, names, sem_count),
        out_shape=[jax.ShapeDtypeStruct(s, t) for s, t in shapes],
        in_specs=[vmem] * 8,
        out_specs=[vmem] * 7,
        scratch_shapes=[pltpu.VMEM(s, t) for s, t in scratch.values()]
        + [pltpu.SemaphoreType.DMA((sem_count,)), pltpu.SemaphoreType.DMA((sem_count,))],
        compiler_params=pltpu.CompilerParams(
            collective_id=0, has_side_effects=True, vmem_limit_bytes=60 * 1024 * 1024
        ),
    )(
        inputs.reshape(micro, rows, width),
        cotangent.reshape(micro, rows, width),
        routes.reshape(micro, rows, 2),
        qkv_weight,
        out_weight,
        small,
        expert_in,
        expert_out,
    )
    return (
        act.reshape(inputs.shape),
        igrad.reshape(inputs.shape),
        gsmall[:, 126],
        gqkv,
        gout,
        gsmall[:, 127],
        gsmall[:, :columns],
        gein,
        geout,
    )


def solution(mesh):
    return jax.shard_map(
        functools.partial(body, dict(mesh.shape)),
        mesh=mesh,
        in_specs=(
            P(None, ("fsdp", "expert"), None, None),
            P("fsdp"),
            P("fsdp", None),
            P("fsdp", None),
            P("fsdp"),
            P("fsdp", None),
            P("expert", "fsdp", None),
            P("expert", "fsdp", None),
            P(None, ("fsdp", "expert"), None, None),
            P(None, ("fsdp", "expert"), None, None),
        ),
        out_specs=(
            P(None, ("fsdp", "expert"), None, None),
            P(None, ("fsdp", "expert"), None, None),
            P("fsdp"),
            P("fsdp", None),
            P("fsdp", None),
            P("fsdp"),
            P("fsdp", None),
            P("expert", "fsdp", None),
            P("expert", "fsdp", None),
        ),
        check_vma=False,
    )
```

```python
import functools
import math

import jax
import jax.numpy as jnp
from jax import lax
from jax.experimental import pallas as pl
from jax.experimental.pallas import tpu as pltpu
from jax.sharding import PartitionSpec as P

HEADS = 8
EPS = 1e-06
MESH = pl.DeviceIdType.MESH
F32 = jnp.float32
BF16 = jnp.bfloat16


def nn(a, b):
    return lax.dot_general(a, b, (((1,), (0,)), ((), ())), preferred_element_type=F32)


def nt(a, b):
    return lax.dot_general(a, b, (((1,), (1,)), ((), ())), preferred_element_type=F32)


def tn(a, b):
    return lax.dot_general(a, b, (((0,), (0,)), ((), ())), preferred_element_type=F32)


def normalize(values):
    center = jnp.mean(values, axis=-1, keepdims=True)
    shifted = values - center
    spread = jnp.mean(shifted * shifted, axis=-1, keepdims=True)
    rstd = lax.rsqrt(spread + EPS)
    return shifted * rstd, rstd


def normalize_back(grad, hat, rstd):
    return rstd * (
        grad
        - jnp.mean(grad, axis=-1, keepdims=True)
        - hat * jnp.mean(grad * hat, axis=-1, keepdims=True)
    )


class Semaphores:
    def __init__(self):
        self.used = 0

    def take(self, count):
        start = self.used
        self.used += count
        return start


SIZES = ("nz", "E", "G", "NE", "NR", "T", "TP", "CP", "S", "D", "FC", "RF", "CF", "TW", "M")


def layout(mesh_shape, micro, seq, width, ff_width):
    fsdp, peers = mesh_shape["fsdp"], mesh_shape["expert"]
    c = {}
    c["nz"] = fsdp // 2
    c["E"] = peers
    c["G"] = peers // 2
    c["NE"] = 2 * peers
    c["T"] = seq
    c["TP"] = -(-seq // 16) * 16
    c["CP"] = -(-max(2, 10 * seq // (4 * 2 * peers) + 1) // 16) * 16
    c["S"] = c["NE"] * c["CP"]
    c["NR"] = -(-(c["NE"] + 2) // 16) * 16
    c["D"] = width
    c["FF"] = ff_width
    c["RF"] = width // fsdp
    c["CF"] = ff_width // fsdp
    c["FC"] = 2 * c["CF"]
    c["TW"] = 4 * width // peers
    c["M"] = micro
    return c


def scratch_of(c):
    nz, E, G, NE, NR, T, TP, CP, S, D, FC, RF, CF, TW, M = (c[k] for k in SIZES)
    h = nz // 2
    v = {
        "XP": ((M, TP, D), BF16),
        "CT": ((M, TP, D), BF16),
        "XR": ((T, M, D), BF16),
        "CR": ((T, M, D), BF16),
        "AR": ((T, M, D), F32),
        "AO": ((T, M, D), BF16),
        "IG": ((M, T, 1, D), F32),
        "RR": ((M, 2, T), jnp.int32),
        "RT": ((M, TP, 128), F32),
        "SR": ((nz, 2, NR, RF), BF16),
        "G1": ((1, RF), BF16),
        "G2": ((1, RF), BF16),
        "RW": ((NE, RF), BF16),
        "GQ": ((RF, 3 * D), F32),
        "GO": ((RF, D), F32),
        "GI": ((2, RF, nz * FC), F32),
        "GT": ((2, CF, D), F32),
        "GS": ((NR, RF), F32),
        "DW": ((E, nz, 2, RF, TW), BF16),
        "SM": ((nz, 2, RF, 128), BF16),
        "WIN": ((nz, nz, 2, RF, FC), BF16),
        "WOUT": ((nz, 2, CF, D), BF16),
        "N1": ((M, TP, D), BF16),
        "J": ((M, TP, 3 * D), BF16),
        "ATT": ((M, TP, D), BF16),
        "MID": ((M, TP, D), F32),
        "N2": ((M, TP, D), BF16),
        "GATES": ((M, TP, 128), F32),
        "PM": ((M, 2, TP, S), BF16),
        "XGS": ((M, 2, NE, CP, D), BF16),
        "XG": ((M, 2, NE, CP, D), BF16),
        "YD": ((M, 2, NE, CP, D), BF16),
        "RET": ((M, 2, NE, CP, D), BF16),
        "YACC": ((M, S, D), F32),
        "DXACC": ((M, S, D), F32),
        "AS": ((M, S, FC), BF16),
        "GHS": ((M, S, FC), BF16),
        "DWI": ((nz, nz, 2, RF, FC), BF16),
        "DWO": ((nz, 2, CF, D), BF16),
        "UPI": ((nz, nz, 2, RF, FC), BF16),
        "UPO": ((nz, 2, CF, D), BF16),
        "DNI": ((nz, nz, 2, RF, FC), BF16),
        "DNO": ((nz, 2, CF, D), BF16),
        "FXI": ((nz, RF, FC), BF16),
        "FXO": ((CF, D), BF16),
        "FYI": ((nz, RF, FC), BF16),
        "FYO": ((CF, D), BF16),
        "GM": ((M, TP, D), F32),
        "GA": ((M, TP, D), BF16),
        "GJ": ((M, TP, 3 * D), BF16),
        "GR": ((NR, D), F32),
        "DG": ((E, nz, 2, RF, TW), BF16),
        "RB1": ((G, nz, 2, RF, TW), BF16),
        "RY1": ((G, h, 2, RF, TW), BF16),
        "RX1": ((G, nz - h, RF, TW), BF16),
        "RX2": ((h, RF, TW), BF16),
        "RY2": ((G, nz - h, RF, TW), BF16),
        "RZ": ((nz, RF, TW), BF16),
        "FIN": ((E, RF, TW), BF16),
        "GB": ((NR, D), BF16),
        "SB1": ((NR, D), BF16),
        "SB2": ((G, NR, D), BF16),
        "SB3": ((2, NR, D), BF16),
        "SB4": ((nz, NR, D), BF16),
    }
    return v


def kernel(c, names, counts, *refs):
    nz, E, G, NE, NR, T, TP, CP, S, D, FC, RF, CF, TW, M = (c[k] for k in SIZES)
    (xin, cot, routes, qkv_s, out_s, gain1, gain2, router, ein, eout) = refs[:10]
    (act, igrad, gqkv, gout, ggain1, ggain2, grouter, gein, geout) = refs[10:19]
    b = dict(zip(names, refs[19:]))
    SS, RS, LS = refs[-3:]
    h = nz // 2
    nb = D // TW
    nq = 3 * nb
    head = D // HEADS
    pair = 2 * head
    scale = 1.0 / math.sqrt(head)
    sems, sends, locals_ = Semaphores(), Semaphores(), Semaphores()
    pending = []

    f = lax.axis_index("fsdp")
    e = lax.axis_index("expert")
    z, x = f // 2, f % 2
    y, core = e // 2, e % 2
    pme = 2 * e + x

    def at(zz, xx, ee):
        return (zz * 2 + xx, ee)

    sibling = at(z, x, y * 2 + (1 - core))
    across = at(z, 1 - x, e)

    def copy_of(src, dst, ssem, rsem, device):
        return pltpu.make_async_remote_copy(
            src_ref=src,
            dst_ref=dst,
            send_sem=SS.at[ssem],
            recv_sem=RS.at[rsem],
            device_id=device,
            device_id_type=MESH,
        )

    def when(cond, run):
        if cond is None:
            run()
        else:
            pl.when(cond)(run)

    def send(src, dst, ssem, rsem, device, cond=None):
        when(cond, copy_of(src, dst, ssem, rsem, device).start)

    def arrived(dst, rsem, cond=None):
        when(cond, copy_of(dst, dst, 0, rsem, sibling).wait_recv)

    def sent_later(ssem, src, cond=None):
        pending.append((cond, copy_of(src, src, ssem, 0, sibling)))

    def one_send(src, dst, device):
        ssem, rsem = sends.take(1), sems.take(1)
        send(src, dst, ssem, rsem, device)
        sent_later(ssem, src)
        return rsem

    barrier = pltpu.get_barrier_semaphore()
    for dz in range(1, nz):
        pl.semaphore_signal(
            barrier, inc=1, device_id=at((z + dz) % nz, x, e), device_id_type=MESH
        )

    def greet(d, carry):
        p = (pme + d) % NE
        pl.semaphore_signal(barrier, inc=1, device_id=at(z, p % 2, p // 2), device_id_type=MESH)
        return carry

    lax.fori_loop(1, NE, greet, 0)

    DW, SM, WIN, WOUT = b["DW"], b["SM"], b["WIN"], b["WOUT"]
    UP, DN = (b["UPI"], b["UPO"]), (b["DNI"], b["DNO"])

    def fetch(src, dst):
        copy = pltpu.make_async_copy(src, dst, LS.at[locals_.take(1)])
        copy.start()
        return copy

    def columns_of_shard(k):
        shard = qkv_s if k < nq else out_s
        return shard.at[:, (k % nq) * TW : (k % nq + 1) * TW]

    own_dense = locals_.take(1)
    for k in range(nq + nb):

        @pl.when(e == k)
        def _():
            pltpu.make_async_copy(
                columns_of_shard(k), DW.at[k, z, x], LS.at[own_dense]
            ).start()

    SR = b["SR"]
    SR[z, x] = jnp.zeros((NR, RF), BF16)
    small_in = [
        fetch(gain1, b["G1"]),
        fetch(gain2, b["G2"]),
        fetch(router, b["RW"]),
    ]
    token_in = [fetch(routes, b["RR"]), fetch(xin, b["XR"]), fetch(cot, b["CR"])]
    own_in = locals_.take(1)
    for k in range(nz):
        pltpu.make_async_copy(
            ein.at[x, :, k * FC : (k + 1) * FC], WIN.at[k, z, x], LS.at[own_in]
        ).start()
    own_out = fetch(eout.at[x], WOUT.at[z, x])

    for copy in small_in:
        copy.wait()
    SR[z, x, 0:NE] = b["RW"][...]
    SR[z, x, NE : NE + 1] = b["G1"][...]
    SR[z, x, NE + 1 : NE + 2] = b["G2"][...]
    entry = lax.broadcasted_iota(jnp.int32, (NR, 128), 0)
    place = lax.broadcasted_iota(jnp.int32, (NR, 128), 1)
    pick = (
        ((entry < NE) & (entry == place))
        | ((entry >= NE) & (entry < NE + 2) & (place == entry - NE + 126))
    ).astype(BF16)
    pltpu.make_async_copy(DW.at[e, z, x], DW.at[e, z, x], LS.at[own_dense]).wait()
    pl.semaphore_wait(barrier, nz - 1 + NE - 1)

    far_first = [d for k in range(1, nz) for d in (k, nz - k) if 2 * k <= nz]
    orders = list(dict.fromkeys(far_first))
    r_dz, r_sz, s_dz, s_sz = sems.take(nz), sems.take(1), sends.take(1), sends.take(1)
    for dz in orders:
        to = at((z + dz) % nz, x, e)
        send(DW.at[e, z, x], DW.at[e, z, x], s_dz, r_dz + dz, to)
    for dz in orders:
        to = at((z + dz) % nz, x, e)
        send(SR.at[z, x], SR.at[z, x], s_sz, r_sz, to)
    sent_later(s_dz, DW.at[e, 0 : nz - 1, x])
    sent_later(s_sz, SR.at[0 : nz - 1, x])

    s_px, r_px = sends.take(1), sems.take(nz)
    s_py, r_py = sends.take(G), sems.take(G * nz)
    s_c, r_c = sends.take(1), sems.take(1)

    def spread_shard(dz):
        zz = (z + nz - dz) % nz
        piece = DW.at[e, zz, x]
        send(piece, piece, s_px, r_px + dz, across)
        for d in range(1, G):
            send(piece, piece, s_py + d, r_py + d * nz + dz, at(z, x, ((y + d) % G) * 2 + core))
        send(piece, piece, s_c, r_c, sibling)

    spread_shard(0)
    sent_later(s_px, DW.at[e, :, x])
    for d in range(1, G):
        sent_later(s_py + d, DW.at[e, :, x])
    sent_later(s_c, DW.at[0:G])

    s_xi, r_xi = sends.take(1), sems.take(1)
    for k in range(nz):
        send(ein.at[1 - x, :, k * FC : (k + 1) * FC], WIN.at[k, z, x], s_xi, r_xi, across)
    sent_later(s_xi, WIN.at[:, z, x])

    XP, CT, RT, PM = b["XP"], b["CT"], b["RT"], b["PM"]

    @pl.when(z == 0)
    def _():
        UP[0][:, 0] = jnp.zeros((nz, 2, RF, FC), BF16)
        UP[1][0] = jnp.zeros((2, CF, D), BF16)

    @pl.when(z == nz - 1)
    def _():
        DN[0][:, nz - 1] = jnp.zeros((nz, 2, RF, FC), BF16)
        DN[1][nz - 1] = jnp.zeros((2, CF, D), BF16)

    for copy in token_in:
        copy.wait()
    lane = lax.broadcasted_iota(jnp.int32, (TP, 128), 1)
    lane_f = lane.astype(F32)
    swap = (
        lax.broadcasted_iota(jnp.int32, (2, 128), 0) == lax.broadcasted_iota(jnp.int32, (2, 128), 1)
    ).astype(BF16)
    for m in range(M):
        XP[m] = jnp.zeros((TP, D), BF16)
        CT[m] = jnp.zeros((TP, D), BF16)
        RT[m] = jnp.full((TP, 128), -1.0, F32)
        XP[m, 0:T] = b["XR"][:, m, :]
        CT[m, 0:T] = b["CR"][:, m, :]
        RT[m, 0:T] = tn(b["RR"][m].astype(BF16), swap)

    def onehot(m, j):
        return RT[m][:, j : j + 1] == lane_f

    before = (
        lax.broadcasted_iota(jnp.int32, (TP, TP), 1) < lax.broadcasted_iota(jnp.int32, (TP, TP), 0)
    ).astype(BF16)
    spots = lax.broadcasted_iota(jnp.int32, (TP, S), 1).astype(F32)
    for m in range(M):
        first = onehot(m, 0).astype(F32)
        second = onehot(m, 1).astype(F32)
        rank0 = nn(before, first.astype(BF16))
        rank1 = nn(before, second.astype(BF16)) + jnp.sum(first, axis=0, keepdims=True)
        for j, (hot, rank) in enumerate(((first, rank0), (second, rank1))):
            slot = jnp.sum(hot * rank, axis=-1, keepdims=True)
            route = RT[m][:, j : j + 1]
            spot = jnp.where(route >= 0, route * CP + slot, -1.0)
            PM[m, j] = (spots == spot).astype(BF16)

    def turn_of(i):
        return 0 if i == 0 else i % (nz - 1) + 1

    groups = (range(0, 2), range(2, nz))
    s_zi = [[sends.take(1) for _ in groups] for _ in range(2)]
    s_zo = [sends.take(1) for _ in range(2)]
    r_zi = [[sems.take(nz) for _ in groups] for _ in range(2)]
    r_zo = [sems.take(2 * nz) for _ in range(2)]
    for zz in range(nz):
        for side in range(2):
            count = zz + 1 if side == 0 else nz - zz
            if count < nz:
                for g, turns in enumerate(groups):
                    sent_later(s_zi[side][g], WIN.at[0 : len(turns), 0:count], z == zz)
                sent_later(s_zo[side], WOUT.at[0:count], z == zz)

    def reach(side, d, some=None):
        begun = z - d if side == 0 else z + d
        there = (begun >= 0) if side == 0 else (begun < nz)
        last = (z == nz - 1) if side == 0 else (z == 0)
        if some is not None:
            there = there & some(begun)
        return begun, there, there & jnp.logical_not(last)

    def onward(side):
        return at((z + 1) % nz if side == 0 else (z + nz - 1) % nz, x, e)

    def pass_in(g, d, halves=(0, 1)):
        for side in range(2):
            begun, there, goes = reach(side, d)
            r = r_zi[side][g]
            if d > 0:
                arrived(WIN.at[0 : len(groups[g]), begun], r + d, there)
            if d < nz - 1:

                @pl.when(goes)
                def _():
                    for i in groups[g]:
                        k = turn_of(i) if side == 1 else nz - 1 - turn_of(i)
                        for half in halves:
                            piece = WIN.at[k, begun, x if half == 0 else 1 - x]
                            send(piece, piece, s_zi[side][g], r + d + 1, onward(side))

    def pass_out(d, half, late=None):
        xx = x if half == 0 else 1 - x
        for side in range(2):
            odd = nz - 2 if side == 0 else 1
            some = None
            if late is not None:
                some = (lambda begun: begun == odd) if late else (lambda begun: begun != odd)
            begun, there, goes = reach(side, d, some)
            r = r_zo[side] + 2 * d + half
            piece = WOUT.at[begun, xx]
            if d > 0:
                arrived(piece, r, there)
            if d < nz - 1:
                send(piece, piece, s_zo[side], r + 2, onward(side), goes)

    early, others = 0, 1
    for dz in orders:
        arrived(DW.at[e, (z + nz - dz) % nz, x], r_dz + dz)
        spread_shard(dz)
    arrived(SR.at[0 : nz - 1, x], r_sz)
    r_sx = one_send(SR.at[:, x], SR.at[:, x], across)
    pltpu.make_async_copy(WIN.at[:, z, x], WIN.at[:, z, x], LS.at[own_in]).wait()
    pass_in(early, 0, (0,))
    arrived(WIN.at[:, z, 1 - x], r_xi)
    pass_in(early, 0, (1,))
    own_out.wait()
    pass_out(0, 0)
    pass_in(others, 0)

    s_f1, r_f1 = sends.take(G), sems.take(G)
    s_f2, r_f2 = sends.take(G), sems.take(G)
    for d in range(1, G):
        sent_later(s_f1 + d, DW.at[e, 0:h, x])
        sent_later(s_f2 + d, DW.at[e, h:nz, x])

    def forward_shard(dz):
        zz = (z + nz - dz) % nz
        piece = DW.at[e, zz, 1 - x]
        arrived(piece, r_px + dz)
        for d in range(1, G):
            to = at(z, x, ((y + d) % G) * 2 + core)
            send(piece, piece, s_f1 + d, r_f1 + d, to, zz < h)
        send(piece, piece, s_c, r_c, sibling)
        for d in range(1, G):
            piece = DW.at[((y + G - d) % G) * 2 + core, zz, x]
            arrived(piece, r_py + d * nz + dz)
            send(piece, piece, s_f2 + d, r_f2 + d, across, zz >= h)
            send(piece, piece, s_c, r_c, sibling)

    for dz in [0] + orders:
        forward_shard(dz)
    for d in range(1, G):
        ee = ((y + G - d) % G) * 2 + core
        arrived(DW.at[ee, 0:h, 1 - x], r_f1 + d)
        arrived(DW.at[ee, h:nz, 1 - x], r_f2 + d)
        send(DW.at[ee, :, 1 - x], DW.at[ee, :, 1 - x], s_c, r_c, sibling)
    r_xo = one_send(eout.at[1 - x], WOUT.at[z, x], across)
    arrived(SR.at[:, 1 - x], r_sx)
    for zz in range(nz):
        for xx in range(2):
            SM[zz, xx] = tn(SR[zz, xx], pick).astype(BF16)
    arrived(DW.at[0:G], r_c)

    pass_in(early, 1)

    def dense(k):
        return DW[k].reshape(D, TW)

    small = SM[...].reshape(D, 128)
    gains = nt(pick, small)
    gain_one, gain_two = gains[NE : NE + 1], gains[NE + 1 : NE + 2]
    key_ok = lax.broadcasted_iota(jnp.int32, (1, TP), 1) < T
    low_half = lax.broadcasted_iota(jnp.int32, (1, pair), 1) < head
    N1, J, ATT, MID, N2 = b["N1"], b["J"], b["ATT"], b["MID"], b["N2"]
    GATES, XGS, XG = b["GATES"], b["XGS"], b["XG"]

    def half_of(value, i):
        keep = low_half if i == 0 else jnp.logical_not(low_half)
        return jnp.where(keep, value, jnp.zeros_like(value))

    def softmax_scores(query, keys):
        scores = jnp.where(key_ok, nt(query, keys) * scale, -1e30)
        raised = jnp.exp(scores - jnp.max(scores, axis=-1, keepdims=True))
        return raised * (1.0 / jnp.sum(raised, axis=-1, keepdims=True))

    def columns(base, hp):
        return pl.ds(pl.multiple_of(base + hp * pair, 128), pair)

    def chosen_of(m, j):
        gates = GATES[m]
        return jnp.sum(jnp.where(onehot(m, j), gates, 0.0), axis=-1, keepdims=True)

    def forward(m):
        tokens = XP[m].astype(F32)
        hat, _ = normalize(tokens)
        N1[m] = (hat * gain_one).astype(BF16)
        for k in range(nq):
            J[m, :, k * TW : (k + 1) * TW] = nn(N1[m], dense(k)).astype(BF16)

        def attend(hp, carry):
            query, keys, values = (J[m, :, columns(i * D, hp)] for i in range(3))
            total = jnp.zeros((TP, pair), F32)
            for i in range(2):
                probs = softmax_scores(half_of(query, i), keys).astype(BF16)
                total = total + nn(probs, half_of(values, i))
            ATT[m, :, columns(0, hp)] = total.astype(BF16)
            return carry

        lax.fori_loop(0, D // pair, attend, 0)
        for k in range(nb):
            cols = slice(k * TW, (k + 1) * TW)
            MID[m, :, cols] = XP[m, :, cols].astype(F32) + nn(ATT[m], dense(nq + k))
        hat, _ = normalize(MID[m])
        N2[m] = (hat * gain_two).astype(BF16)
        logits = jnp.where(lane < NE, nn(N2[m], small), -1e30)
        raised = jnp.exp(logits - jnp.max(logits, axis=-1, keepdims=True))
        GATES[m] = raised / jnp.sum(raised, axis=-1, keepdims=True)
        upstream = CT[m].astype(F32)
        XGS[m, 0] = tn(PM[m, 0] + PM[m, 1], N2[m]).astype(BF16).reshape(NE, CP, D)
        placed = tn(PM[m, 0], (chosen_of(m, 0) * upstream).astype(BF16))
        placed = placed + tn(PM[m, 1], (chosen_of(m, 1) * upstream).astype(BF16))
        XGS[m, 1] = placed.astype(BF16).reshape(NE, CP, D)

    def exchange(src, dst, m, sem):
        def one(d, carry):
            p = (pme + d) % NE
            send(src.at[m, :, p], dst.at[m, :, pme], *sem, at(z, p % 2, p // 2))
            return carry

        lax.fori_loop(1, NE, one, 0)
        sent_later(sem[0], src.at[m, :, 0 : NE - 1])
        dst[m, :, pme] = src[m, :, pme]

    def exchanged(dst, m, sem):
        arrived(dst.at[m, :, 0 : NE - 1], sem[1])

    s_go = [(sends.take(1), sems.take(1)) for _ in range(M)]
    s_back = [(sends.take(1), sems.take(1)) for _ in range(M)]
    for m in range(M):
        forward(m)
        exchange(XGS, XG, m, s_go[m])
        if m == 0:
            pass_in(early, 2) if nz <= 4 else None
    arrived(WOUT.at[z, 1 - x], r_xo)
    pass_out(0, 1, False)
    for d in range(3 if nz <= 4 else 2, nz):
        pass_in(early, d)
    pass_out(1, 0)
    pass_in(others, 1)
    pass_out(1, 1, False)
    for m in range(M):
        exchanged(XG, m, s_go[m])

    YACC, DXACC, AS, GHS = b["YACC"], b["DXACC"], b["AS"], b["GHS"]
    DWI, DWO = b["DWI"], b["DWO"]
    YACC[...] = jnp.zeros_like(YACC)
    DXACC[...] = jnp.zeros_like(DXACC)
    c0, c1 = math.sqrt(2.0 / math.pi), 0.044715

    YD, RET = b["YD"], b["RET"]
    OWN = (DWI, DWO)
    s_up = [(sends.take(1), sends.take(1)) for _ in range(2)]
    r_up = [(sems.take(nz * nz), sems.take(2 * nz)) for _ in range(2)]

    def expert_block(k, done):
        def part(m):
            tokens = XG[m, 0].reshape(S, D)
            grads = XG[m, 1].reshape(S, D)
            for xx in range(2):
                cols = slice(xx * CF, (xx + 1) * CF)
                w_in = WIN[k, :, :, :, cols].reshape(D, CF)
                w_out = WOUT[k, xx]
                hidden = nn(tokens, w_in)
                grad_acted = nt(grads, w_out)
                square = hidden * hidden
                bent = jnp.tanh(c0 * hidden * (1.0 + c1 * square))
                acted = (0.5 * hidden * (1.0 + bent)).astype(BF16)
                slope = 0.5 * (1.0 + bent) + 0.5 * c0 * hidden * (1.0 - bent * bent) * (
                    1.0 + 3.0 * c1 * square
                )
                grad_hidden = (grad_acted * slope).astype(BF16)
                AS[m, :, cols] = acted
                GHS[m, :, cols] = grad_hidden
                YACC[m] = YACC[m] + nn(acted, w_out)
                DXACC[m] = DXACC[m] + nt(grad_hidden, w_in)

        for m in range(M):
            part(m)
            if done is not None:
                done(m)
        grads = XG[:, 1].reshape(M * S, D)
        tokens = XG[:, 0].reshape(M * S, D)
        for xx in range(2):
            cols = slice(xx * CF, (xx + 1) * CF)
            DWO[k, xx] = tn(AS[:, :, cols].reshape(M * S, CF), grads).astype(BF16)
            DWI[k, :, :, :, cols] = (
                tn(tokens, GHS[:, :, cols].reshape(M * S, CF))
                .astype(BF16)
                .reshape(nz, 2, RF, CF)
            )

    def sum_step(side, i, begins):
        far = z if side == 0 else nz - 1 - z
        GOT = UP if side == 0 else DN
        turn = ((i % (nz - 1)) + 1) * jnp.minimum(i, 1)
        k = turn if side == 0 else nz - 1 - turn

        def one(j, carry):
            goal = nz - 1 - j
            t = goal if side == 0 else nz - 1 - goal
            rsem = r_up[side][0] + k * nz + t

            @pl.when(goal > far)
            def _():
                if not begins:
                    arrived(GOT[0].at[k, t], rsem)
                    DWI[k, t] = DWI[k, t] + GOT[0][k, t]
                send(DWI.at[k, t], GOT[0].at[k, t], s_up[side][0], rsem, onward(side))

            return carry

        lax.fori_loop(0, nz - 1, one, 0)

        @pl.when(turn > far)
        def _():
            for xx in (1 - x, x):
                rsem = r_up[side][1] + 2 * k + xx
                if not begins:
                    arrived(GOT[1].at[k, xx], rsem)
                    DWO[k, xx] = DWO[k, xx] + GOT[1][k, xx]
                send(DWO.at[k, xx], GOT[1].at[k, xx], s_up[side][1], rsem, onward(side))

    def sums_begin(i):
        for side in range(2):
            far = z if side == 0 else nz - 1 - z
            pl.when(far == 0)(functools.partial(sum_step, side, jnp.int32(i), True))

    def sums_pass(far_at, i):
        for side in range(2):
            far = z if side == 0 else nz - 1 - z
            pl.when(far == far_at)(functools.partial(sum_step, side, jnp.int32(i), False))

    passes = [
        (slot - i + 1, i)
        for slot in range(2 * nz - 3)
        for i in range(nz)
        if 0 < slot - i + 1 < nz - 1
    ]

    def sums_next(count):
        for _ in range(min(count, len(passes))):
            sums_pass(*passes.pop(0))

    def sums_rest():
        if len(passes) <= 2:
            return sums_next(2)

        def slot_of(slot, carry):
            for side in range(2):
                far = z if side == 0 else nz - 1 - z
                i = slot - far + 1
                ok = (far > 0) & (far < nz - 1) & (i >= 0) & (i < nz)
                pl.when(ok)(functools.partial(sum_step, side, jnp.clip(i, 0, nz - 1), False))
            return carry

        first = sum(passes[0]) - 1
        lax.fori_loop(first, 2 * nz - 3, slot_of, 0)

    for zz in range(nz):
        for side in range(2):
            count = nz - 1 - zz if side == 0 else zz
            if count > 0:
                sent_later(s_up[side][0], DWI.at[:, 0:count], z == zz)
                sent_later(s_up[side][1], DWO.at[0:count], z == zz)

    def give_back(m):
        YD[m, 0] = YACC[m].astype(BF16).reshape(NE, CP, D)
        YD[m, 1] = DXACC[m].astype(BF16).reshape(NE, CP, D)
        exchange(YD, RET, m, s_back[m])

    when_two, when_far, when_late = (1, 2, nz - 1) if nz <= 4 else (0, 0, 0)
    for i in range(nz):
        if i == when_two:
            pass_in(others, 2)
            pass_out(2, 0)
            pass_out(2, 1, False)
        if i == when_far:
            pass_out(0, 1, True)
            for d in range(3, nz):
                pass_in(others, d)
                pass_out(d, 0)
                pass_out(d, 1, False)
        if i == when_late:
            for d in range(1, nz):
                pass_out(d, 1, True)
        block = turn_of(i) + (z // h) * (nz - 1 - 2 * turn_of(i))
        expert_block(block, give_back if i == nz - 1 else None)
        sums_begin(i)

    r_fin, s_fin = (sems.take(nz), sems.take(1)), (sends.take(1), sends.take(1))
    FX, FY = (b["FXI"], b["FXO"]), (b["FYI"], b["FYO"])
    GI, GT = b["GI"], b["GT"]
    sent_later(s_fin[0], FX[0])
    sent_later(s_fin[1], FX[1])
    kept = []

    def total_of(kind, place):
        return (
            OWN[kind][place].astype(F32)
            + UP[kind][place].astype(F32)
            + DN[kind][place].astype(F32)
        )

    def sums_end_in(k):
        for side, ref, ok in ((0, UP, z > 0), (1, DN, z < nz - 1)):
            arrived(ref[0].at[k, z], r_up[side][0] + k * nz + z, ok)
        FX[0][k] = total_of(0, (k, z, 1 - x)).astype(BF16)
        send(FX[0].at[k], FY[0].at[k], s_fin[0], r_fin[0] + k, across)
        GI[x, :, k * FC : (k + 1) * FC] = total_of(0, (k, z, x))

    def sums_end_out():
        for xx, mine in ((1 - x, False), (x, True)):
            for side, ref, ok in ((0, UP, z > 0), (1, DN, z < nz - 1)):
                arrived(ref[1].at[z, xx], r_up[side][1] + 2 * z + xx, ok)
            if mine:
                GT[x] = total_of(1, (z, xx))
            else:
                FX[1][...] = total_of(1, (z, xx)).astype(BF16)
                send(FX[1], FY[1], s_fin[1], r_fin[1], across)

    def sums_close():
        kept.append(fetch(GI.at[x], gein.at[x]))
        kept.append(fetch(GT.at[x], geout.at[x]))
        for k in range(nz):
            arrived(FY[0].at[k], r_fin[0] + k)
            GI[1 - x, :, k * FC : (k + 1) * FC] = FY[0][k].astype(F32)
        kept.append(fetch(GI.at[1 - x], gein.at[1 - x]))
        arrived(FY[1], r_fin[1])
        GT[1 - x] = FY[1][...].astype(F32)
        kept.append(fetch(GT.at[1 - x], geout.at[1 - x]))

    GM, GA, GJ, GR = b["GM"], b["GA"], b["GJ"], b["GR"]
    DG = b["DG"]
    GR[...] = jnp.zeros_like(GR)

    def backward_top(m):
        result = RET[m, 0].reshape(S, D)
        picked0 = nn(PM[m, 0], result)
        picked1 = nn(PM[m, 1], result)
        out = MID[m] + chosen_of(m, 0) * picked0 + chosen_of(m, 1) * picked1
        b["AR"][:, m, :] = out[0:T]
        upstream = CT[m].astype(F32)
        gates = GATES[m]
        grad_gates = jnp.where(
            onehot(m, 0), jnp.sum(upstream * picked0, axis=-1, keepdims=True), 0.0
        ) + jnp.where(onehot(m, 1), jnp.sum(upstream * picked1, axis=-1, keepdims=True), 0.0)
        grad_logits = (
            gates * (grad_gates - jnp.sum(grad_gates * gates, axis=-1, keepdims=True))
        ).astype(BF16)
        GR[0:NE] = GR[0:NE] + tn(grad_logits, N2[m])[0:NE]
        grad = nn(PM[m, 0] + PM[m, 1], RET[m, 1].reshape(S, D)) + nt(grad_logits, small)
        hat, rstd = normalize(MID[m])
        GR[NE + 1 : NE + 2] = GR[NE + 1 : NE + 2] + jnp.sum(grad * hat, axis=0, keepdims=True)
        grad_middle = upstream + normalize_back(grad * gain_two, hat, rstd)
        GM[m] = grad_middle
        branch = grad_middle.astype(BF16)
        N2[m] = branch
        back = None
        for k in range(nb):
            term = nt(branch[:, k * TW : (k + 1) * TW], dense(nq + k))
            back = term if back is None else back + term
        GA[m] = back.astype(BF16)

    def backward_heads(m):
        def attend(hp, carry):
            query, keys, values = (J[m, :, columns(i * D, hp)] for i in range(3))
            grads = GA[m, :, columns(0, hp)]
            grad_query = jnp.zeros((TP, pair), F32)
            grad_keys = jnp.zeros((TP, pair), F32)
            grad_values = jnp.zeros((TP, pair), F32)
            for i in range(2):
                part = half_of(query, i)
                upstream = half_of(grads, i)
                probs = softmax_scores(part, keys)
                grad_probs = nt(upstream, values)
                grad_values = grad_values + tn(probs.astype(BF16), upstream)
                grad_scores = (
                    probs
                    * (grad_probs - jnp.sum(grad_probs * probs, axis=-1, keepdims=True))
                ).astype(BF16)
                grad_query = grad_query + nn(grad_scores, half_of(keys, i))
                grad_keys = grad_keys + tn(grad_scores, part)
            GJ[m, :, columns(0, hp)] = (grad_query * scale).astype(BF16)
            GJ[m, :, columns(D, hp)] = (grad_keys * scale).astype(BF16)
            GJ[m, :, columns(2 * D, hp)] = grad_values.astype(BF16)
            return carry

        lax.fori_loop(0, D // pair, attend, 0)

    def backward_end(m):
        grad = None
        for k in range(nq):
            term = nt(GJ[m, :, k * TW : (k + 1) * TW], dense(k))
            grad = term if grad is None else grad + term
        hat, rstd = normalize(XP[m].astype(F32))
        GR[NE : NE + 1] = GR[NE : NE + 1] + jnp.sum(grad * hat, axis=0, keepdims=True)
        full = GM[m] + normalize_back(grad * gain_one, hat, rstd)
        b["IG"][m, :, 0, :] = full[0:T]

    sums_next(1)
    for m in range(M):
        exchanged(RET, m, s_back[m])
        backward_top(m)
        backward_heads(m)
        sums_next(2)
    for k in range(nb):
        part = tn(
            ATT[...].reshape(M * TP, D), N2[:, :, k * TW : (k + 1) * TW].reshape(M * TP, TW)
        )
        DG[nq + k] = part.astype(BF16).reshape(nz, 2, RF, TW)
    for k in range(nq):
        part = tn(
            N1[...].reshape(M * TP, D), GJ[:, :, k * TW : (k + 1) * TW].reshape(M * TP, TW)
        )
        DG[k] = part.astype(BF16).reshape(nz, 2, RF, TW)
    RB1, RY1, RX1, RX2, RY2, RZ, FIN = (
        b[k] for k in ("RB1", "RY1", "RX1", "RX2", "RY2", "RZ", "FIN")
    )
    GB, SB1, SB2, SB3, SB4 = (b[k] for k in ("GB", "SB1", "SB2", "SB3", "SB4"))
    s_r1, r_r1 = sends.take(1), sems.take(1)
    for j in range(G):
        send(DG.at[2 * j + 1 - core], RB1.at[j], s_r1, r_r1, sibling)
    sent_later(s_r1, RB1)
    for m in range(M):
        backward_end(m)
    b["AO"][...] = b["AR"][...].astype(BF16)
    kept.append(fetch(b["AO"], act))
    kept.append(fetch(b["IG"], igrad))
    GB[...] = GR[...].astype(BF16)
    r_b1 = one_send(GB, SB1, sibling)
    arrived(RB1, r_r1)
    for j in range(G):
        DG[2 * j + core] = DG[2 * j + core] + RB1[j]
    s_ry1, r_ry1 = sends.take(G), sems.take(G)
    for d in range(1, G):
        q = (y + d) % G
        piece = DG.at[2 * q + core, 0:h]
        send(piece, RY1.at[y], s_ry1 + d, r_ry1 + d, at(z, x, 2 * q + core))
        sent_later(s_ry1 + d, piece)
    s_rx1, r_rx1 = sends.take(1), sems.take(1)
    for j in range(G):
        send(DG.at[2 * j + core, h:nz, 1 - x], RX1.at[j], s_rx1, r_rx1, across)
    sent_later(s_rx1, RX1)
    arrived(SB1, r_b1)
    SB2[y] = GB[...] + SB1[...]
    s_b2, r_b2 = sends.take(G), sems.take(G)
    for d in range(1, G):
        send(SB2.at[y], SB2.at[y], s_b2 + d, r_b2 + d, at(z, x, ((y + d) % G) * 2 + core))
        sent_later(s_b2 + d, SB2.at[y])
    sums_next(1)
    for d in range(1, G):
        q = (y + G - d) % G
        arrived(RY1.at[q], r_ry1 + d)
        DG[e, 0:h] = DG[e, 0:h] + RY1[q]
    r_rx2 = one_send(DG.at[e, 0:h, 1 - x], RX2, across)
    arrived(RX1, r_rx1)
    for j in range(G):
        DG[2 * j + core, h:nz, x] = DG[2 * j + core, h:nz, x] + RX1[j]
    s_ry2, r_ry2 = sends.take(G), sems.take(G)
    for d in range(1, G):
        q = (y + d) % G
        piece = DG.at[2 * q + core, h:nz, x]
        send(piece, RY2.at[y], s_ry2 + d, r_ry2 + d, at(z, x, 2 * q + core))
        sent_later(s_ry2 + d, piece)
    for d in range(1, G):
        arrived(SB2.at[(y + G - d) % G], r_b2 + d)
    total = SB2[0].astype(F32)
    for j in range(1, G):
        total = total + SB2[j].astype(F32)
    SB3[x] = total.astype(BF16)
    r_b3 = one_send(SB3.at[x], SB3.at[x], across)
    sums_next(1)
    arrived(RX2, r_rx2)
    DG[e, 0:h, x] = DG[e, 0:h, x] + RX2[...]
    for d in range(1, G):
        q = (y + G - d) % G
        arrived(RY2.at[q], r_ry2 + d)
        DG[e, h:nz, x] = DG[e, h:nz, x] + RY2[q]
    s_rz, r_rz = sends.take(1), sems.take(1)
    for dz in orders:
        zz = (z + dz) % nz
        send(DG.at[e, zz, x], RZ.at[z], s_rz, r_rz, at(zz, x, e))
    sent_later(s_rz, RZ.at[0 : nz - 1])
    arrived(SB3.at[1 - x], r_b3)
    SB4[z] = SB3[0] + SB3[1]
    s_b4, r_b4 = sends.take(1), sems.take(1)
    for dz in orders:
        send(SB4.at[z], SB4.at[z], s_b4, r_b4, at((z + dz) % nz, x, e))
    sent_later(s_b4, SB4.at[0 : nz - 1])
    sums_rest()
    ends = [0, nz - 1] + list(range(1, nz - 1))
    for k in ends[:2]:
        sums_end_in(k)
    RZ[z] = DG[e, z, x]
    arrived(RZ.at[0 : nz - 1], r_rz)
    total = RZ[0].astype(F32)
    for k in range(1, nz):
        total = total + RZ[k].astype(F32)
    FIN[e] = total.astype(BF16)
    s_fe, r_fe = sends.take(1), sems.take(1)

    def hand_out(d, carry):
        send(FIN.at[e], FIN.at[e], s_fe, r_fe, at(z, x, (e + d) % E))
        return carry

    lax.fori_loop(1, E, hand_out, 0)
    sent_later(s_fe, FIN.at[0 : E - 1])
    arrived(SB4.at[0 : nz - 1], r_b4)
    total = SB4[0].astype(F32)
    for k in range(1, nz):
        total = total + SB4[k].astype(F32)
    mine = (
        lax.broadcasted_iota(jnp.int32, (D, RF), 0)
        == lax.broadcasted_iota(jnp.int32, (D, RF), 1) + f * RF
    ).astype(F32)
    b["GS"][...] = lax.dot_general(
        total,
        mine,
        (((1,), (0,)), ((), ())),
        precision=lax.Precision.HIGHEST,
        preferred_element_type=F32,
    )
    kept.append(fetch(b["GS"].at[0:NE], grouter))
    kept.append(fetch(b["GS"].at[NE : NE + 1], ggain1))
    kept.append(fetch(b["GS"].at[NE + 1 : NE + 2], ggain2))
    sums_end_out()
    for k in ends[2:]:
        sums_end_in(k)
    sums_close()
    arrived(FIN.at[0 : E - 1], r_fe)
    for k in range(nq):
        b["GQ"][:, k * TW : (k + 1) * TW] = FIN[k].astype(F32)
    for k in range(nb):
        b["GO"][:, k * TW : (k + 1) * TW] = FIN[nq + k].astype(F32)
    kept.append(fetch(b["GQ"], gqkv))
    kept.append(fetch(b["GO"], gout))

    for cond, copy in pending:
        when(cond, copy.wait_send)
    for copy in kept:
        copy.wait()
    used = (sends.used, sems.used, locals_.used)
    assert all(a <= b for a, b in zip(used, counts)), (used, counts)


def hand_over(*refs):
    source, target, held = refs[:9], refs[9:18], refs[18:27]
    sem = refs[27]
    order = sorted(range(9), key=lambda k: -math.prod(source[k].shape))
    into = {k: pltpu.make_async_copy(source[k], held[k], sem.at[0, k]) for k in order}
    out = {k: pltpu.make_async_copy(held[k], target[k], sem.at[1, k]) for k in order}
    for k in order:
        into[k].start()
    for k in order:
        into[k].wait()
        out[k].start()
    for k in order:
        out[k].wait()


def body(
    mesh_shape,
    inputs,
    gain_attn,
    qkv_weight,
    out_weight,
    gain_moe,
    router_weight,
    expert_in,
    expert_out,
    routes,
    cotangent,
):
    micro, images, seq, width = inputs.shape
    c = layout(mesh_shape, micro, images * seq, width, expert_in.shape[2])
    rows = images * seq
    scratch = scratch_of(c)
    names = list(scratch)
    nz, G = c["nz"], c["G"]
    counts = (31 + 6 * G, 14 + 16 * nz + 2 * nz * nz + G * nz + 5 * G, 20)
    shapes = (
        ((rows, micro, width), BF16),
        ((micro, rows, 1, width), F32),
        (qkv_weight.shape, F32),
        (out_weight.shape, F32),
        ((1, c["RF"]), F32),
        ((1, c["RF"]), F32),
        ((c["NE"], c["RF"]), F32),
        (expert_in.shape, F32),
        (expert_out.shape, F32),
    )
    shapes = [jax.ShapeDtypeStruct(s, t) for s, t in shapes]
    anywhere = pl.BlockSpec(memory_space=pltpu.HBM)
    results = pl.pallas_call(
        functools.partial(kernel, c, names, counts),
        out_shape=shapes,
        in_specs=[anywhere] * 10,
        out_specs=[anywhere] * 9,
        scratch_shapes=[pltpu.VMEM(s, t) for s, t in scratch.values()]
        + [pltpu.SemaphoreType.DMA((count,)) for count in counts],
        compiler_params=pltpu.CompilerParams(
            collective_id=0, has_side_effects=True, vmem_limit_bytes=60 * 1024 * 1024
        ),
    )(
        jnp.transpose(inputs, (1, 2, 0, 3)).reshape(rows, micro, width),
        jnp.transpose(cotangent, (1, 2, 0, 3)).reshape(rows, micro, width),
        jnp.transpose(routes, (0, 1, 3, 2)).reshape(micro, 2, rows),
        qkv_weight,
        out_weight,
        gain_attn[None, :],
        gain_moe[None, :],
        router_weight.T,
        expert_in,
        expert_out,
    )
    act, igrad, gqkv, gout, ggain1, ggain2, grouter, gein, geout = pl.pallas_call(
        hand_over,
        out_shape=shapes,
        in_specs=[anywhere] * 9,
        out_specs=[anywhere] * 9,
        scratch_shapes=[pltpu.VMEM(s.shape, s.dtype) for s in shapes]
        + [pltpu.SemaphoreType.DMA((2, 9))],
        compiler_params=pltpu.CompilerParams(vmem_limit_bytes=60 * 1024 * 1024),
    )(*results)
    return (
        jnp.transpose(act.reshape(images, seq, micro, width), (2, 0, 1, 3)),
        igrad.reshape(inputs.shape),
        ggain1[0],
        gqkv,
        gout,
        ggain2[0],
        grouter.T,
        gein,
        geout,
    )


def solution(mesh):
    return jax.shard_map(
        functools.partial(body, dict(mesh.shape)),
        mesh=mesh,
        in_specs=(
            P(None, ("fsdp", "expert"), None, None),
            P("fsdp"),
            P("fsdp", None),
            P("fsdp", None),
            P("fsdp"),
            P("fsdp", None),
            P("expert", "fsdp", None),
            P("expert", "fsdp", None),
            P(None, ("fsdp", "expert"), None, None),
            P(None, ("fsdp", "expert"), None, None),
        ),
        out_specs=(
            P(None, ("fsdp", "expert"), None, None),
            P(None, ("fsdp", "expert"), None, None),
            P("fsdp"),
            P("fsdp", None),
            P("fsdp", None),
            P("fsdp"),
            P("fsdp", None),
            P("expert", "fsdp", None),
            P("expert", "fsdp", None),
        ),
        check_vma=False,
    )
```

```python
import functools
import math

import jax
import jax.numpy as jnp
from jax import lax
from jax.experimental import pallas as pl
from jax.experimental.pallas import tpu as pltpu
from jax.sharding import PartitionSpec as P

HEADS = 8
EPS = 1e-06
MESH = pl.DeviceIdType.MESH
F32 = jnp.float32
BF16 = jnp.bfloat16


def nn(a, b):
    return lax.dot_general(a, b, (((1,), (0,)), ((), ())), preferred_element_type=F32)


def nt(a, b):
    return lax.dot_general(a, b, (((1,), (1,)), ((), ())), preferred_element_type=F32)


def tn(a, b):
    return lax.dot_general(a, b, (((0,), (0,)), ((), ())), preferred_element_type=F32)


def normalize(values):
    center = jnp.mean(values, axis=-1, keepdims=True)
    shifted = values - center
    spread = jnp.mean(shifted * shifted, axis=-1, keepdims=True)
    rstd = lax.rsqrt(spread + EPS)
    return shifted * rstd, rstd


def normalize_back(grad, hat, rstd):
    return rstd * (
        grad
        - jnp.mean(grad, axis=-1, keepdims=True)
        - hat * jnp.mean(grad * hat, axis=-1, keepdims=True)
    )


class Semaphores:
    def __init__(self):
        self.used = 0

    def take(self, count):
        start = self.used
        self.used += count
        return start


SIZES = ("nz", "E", "G", "NE", "NR", "T", "TP", "CP", "S", "D", "FC", "RF", "CF", "TW", "M")


def layout(mesh_shape, micro, seq, width, ff_width):
    fsdp, peers = mesh_shape["fsdp"], mesh_shape["expert"]
    c = {}
    c["nz"] = fsdp // 2
    c["E"] = peers
    c["G"] = peers // 2
    c["NE"] = 2 * peers
    c["T"] = seq
    c["TP"] = -(-seq // 16) * 16
    c["CP"] = -(-max(2, 10 * seq // (4 * 2 * peers) + 1) // 16) * 16
    c["S"] = c["NE"] * c["CP"]
    c["NR"] = -(-(c["NE"] + 2) // 16) * 16
    c["D"] = width
    c["FF"] = ff_width
    c["RF"] = width // fsdp
    c["CF"] = ff_width // fsdp
    c["FC"] = 2 * c["CF"]
    c["TW"] = 4 * width // peers
    c["M"] = micro
    return c


def scratch_of(c):
    nz, E, G, NE, NR, T, TP, CP, S, D, FC, RF, CF, TW, M = (c[k] for k in SIZES)
    h = nz // 2
    v = {
        "XP": ((M, TP, D), BF16),
        "CT": ((M, TP, D), BF16),
        "XR": ((T, M, D), BF16),
        "CR": ((T, M, D), BF16),
        "AR": ((T, M, D), F32),
        "AO": ((T, M, D), BF16),
        "IG": ((M, T, 1, D), F32),
        "RR": ((M, 2, T), jnp.int32),
        "RT": ((M, TP, 128), F32),
        "SR": ((nz, 2, NR, RF), BF16),
        "G1": ((1, RF), BF16),
        "G2": ((1, RF), BF16),
        "RW": ((NE, RF), BF16),
        "GQ": ((RF, 3 * D), F32),
        "GO": ((RF, D), F32),
        "GI": ((2, RF, nz * FC), F32),
        "GT": ((2, CF, D), F32),
        "GS": ((NR, RF), F32),
        "DW": ((E, nz, 2, RF, TW), BF16),
        "SM": ((nz, 2, RF, 128), BF16),
        "WIN": ((nz, nz, 2, RF, FC), BF16),
        "WOUT": ((nz, 2, CF, D), BF16),
        "N1": ((M, TP, D), BF16),
        "J": ((M, TP, 3 * D), BF16),
        "ATT": ((M, TP, D), BF16),
        "MID": ((M, TP, D), F32),
        "N2": ((M, TP, D), BF16),
        "GATES": ((M, TP, 128), F32),
        "PM": ((M, 2, TP, S), BF16),
        "XS": ((M, NE, CP, D), BF16),
        "XB": ((M, NE, CP, D), BF16),
        "GSS": ((M, NE, CP, D), BF16),
        "GRB": ((M, NE, CP, D), BF16),
        "CSS": ((M, NE, 8, 128), F32),
        "CSB": ((M, NE, 8, 128), F32),
        "CROW": ((8, S), F32),
        "GC": ((M, S, D), BF16),
        "YS": ((M, NE, CP, D), BF16),
        "YB": ((M, NE, CP, D), BF16),
        "DXS": ((M, NE, CP, D), BF16),
        "DXB": ((M, NE, CP, D), BF16),
        "GCS": ((M, NE, 8, 128), F32),
        "GCB": ((M, NE, 8, 128), F32),
        "YACC": ((M, S, D), F32),
        "DXACC": ((M, S, D), F32),
        "AS": ((M, S, FC), BF16),
        "GHS": ((M, S, FC), BF16),
        "DWI": ((nz, nz, 2, RF, FC), BF16),
        "DWO": ((nz, 2, CF, D), BF16),
        "UPI": ((nz, nz, 2, RF, FC), BF16),
        "UPO": ((nz, 2, CF, D), BF16),
        "DNI": ((nz, nz, 2, RF, FC), BF16),
        "DNO": ((nz, 2, CF, D), BF16),
        "FXI": ((nz, RF, FC), BF16),
        "FXO": ((CF, D), BF16),
        "FYI": ((nz, RF, FC), BF16),
        "FYO": ((CF, D), BF16),
        "GM": ((M, TP, D), F32),
        "GA": ((M, TP, D), BF16),
        "GJ": ((M, TP, 3 * D), BF16),
        "GR": ((NR, D), F32),
        "DG": ((E, nz, 2, RF, TW), BF16),
        "RB1": ((G, nz, 2, RF, TW), BF16),
        "RY1": ((G, h, 2, RF, TW), BF16),
        "RX1": ((G, nz - h, RF, TW), BF16),
        "RX2": ((h, RF, TW), BF16),
        "RY2": ((G, nz - h, RF, TW), BF16),
        "RZ": ((nz, RF, TW), BF16),
        "FIN": ((E, RF, TW), BF16),
        "GB": ((NR, D), BF16),
        "SB1": ((NR, D), BF16),
        "SB2": ((G, NR, D), BF16),
        "SB3": ((2, NR, D), BF16),
        "SB4": ((nz, NR, D), BF16),
    }
    return v


def kernel(c, names, counts, *refs):
    nz, E, G, NE, NR, T, TP, CP, S, D, FC, RF, CF, TW, M = (c[k] for k in SIZES)
    (xin, cot, routes, qkv_s, out_s, gain1, gain2, router, ein, eout) = refs[:10]
    (act, igrad, gqkv, gout, ggain1, ggain2, grouter, gein, geout) = refs[10:19]
    b = dict(zip(names, refs[19:]))
    SS, RS, LS = refs[-3:]
    h = nz // 2
    nb = D // TW
    nq = 3 * nb
    head = D // HEADS
    pair = 2 * head
    scale = 1.0 / math.sqrt(head)
    sems, sends, locals_ = Semaphores(), Semaphores(), Semaphores()
    pending = []

    f = lax.axis_index("fsdp")
    e = lax.axis_index("expert")
    z, x = f // 2, f % 2
    y, core = e // 2, e % 2
    pme = 2 * e + x

    def at(zz, xx, ee):
        return (zz * 2 + xx, ee)

    sibling = at(z, x, y * 2 + (1 - core))
    across = at(z, 1 - x, e)

    def copy_of(src, dst, ssem, rsem, device):
        return pltpu.make_async_remote_copy(
            src_ref=src,
            dst_ref=dst,
            send_sem=SS.at[ssem],
            recv_sem=RS.at[rsem],
            device_id=device,
            device_id_type=MESH,
        )

    def when(cond, run):
        if cond is None:
            run()
        else:
            pl.when(cond)(run)

    def send(src, dst, ssem, rsem, device, cond=None):
        when(cond, copy_of(src, dst, ssem, rsem, device).start)

    def arrived(dst, rsem, cond=None):
        when(cond, copy_of(dst, dst, 0, rsem, sibling).wait_recv)

    def sent_later(ssem, src, cond=None):
        pending.append((cond, copy_of(src, src, ssem, 0, sibling)))

    def one_send(src, dst, device):
        ssem, rsem = sends.take(1), sems.take(1)
        send(src, dst, ssem, rsem, device)
        sent_later(ssem, src)
        return rsem

    barrier = pltpu.get_barrier_semaphore()
    for dz in range(1, nz):
        pl.semaphore_signal(
            barrier, inc=1, device_id=at((z + dz) % nz, x, e), device_id_type=MESH
        )

    def greet(d, carry):
        p = (pme + d) % NE
        pl.semaphore_signal(barrier, inc=1, device_id=at(z, p % 2, p // 2), device_id_type=MESH)
        return carry

    lax.fori_loop(1, NE, greet, 0)

    DW, SM, WIN, WOUT = b["DW"], b["SM"], b["WIN"], b["WOUT"]
    UP, DN = (b["UPI"], b["UPO"]), (b["DNI"], b["DNO"])

    def fetch(src, dst):
        copy = pltpu.make_async_copy(src, dst, LS.at[locals_.take(1)])
        copy.start()
        return copy

    def columns_of_shard(k):
        shard = qkv_s if k < nq else out_s
        return shard.at[:, (k % nq) * TW : (k % nq + 1) * TW]

    own_dense = locals_.take(1)
    for k in range(nq + nb):

        @pl.when(e == k)
        def _():
            pltpu.make_async_copy(
                columns_of_shard(k), DW.at[k, z, x], LS.at[own_dense]
            ).start()

    SR = b["SR"]
    SR[z, x] = jnp.zeros((NR, RF), BF16)
    small_in = [
        fetch(gain1, b["G1"]),
        fetch(gain2, b["G2"]),
        fetch(router, b["RW"]),
    ]
    token_in = [fetch(routes, b["RR"]), fetch(xin, b["XR"]), fetch(cot, b["CR"])]
    own_in = locals_.take(1)
    for k in range(nz):
        pltpu.make_async_copy(
            ein.at[x, :, k * FC : (k + 1) * FC], WIN.at[k, z, x], LS.at[own_in]
        ).start()
    own_out = fetch(eout.at[x], WOUT.at[z, x])

    for copy in small_in:
        copy.wait()
    SR[z, x, 0:NE] = b["RW"][...]
    SR[z, x, NE : NE + 1] = b["G1"][...]
    SR[z, x, NE + 1 : NE + 2] = b["G2"][...]
    entry = lax.broadcasted_iota(jnp.int32, (NR, 128), 0)
    place = lax.broadcasted_iota(jnp.int32, (NR, 128), 1)
    pick = (
        ((entry < NE) & (entry == place))
        | ((entry >= NE) & (entry < NE + 2) & (place == entry - NE + 126))
    ).astype(BF16)
    pltpu.make_async_copy(DW.at[e, z, x], DW.at[e, z, x], LS.at[own_dense]).wait()
    pl.semaphore_wait(barrier, nz - 1 + NE - 1)

    far_first = [d for k in range(1, nz) for d in (k, nz - k) if 2 * k <= nz]
    orders = list(dict.fromkeys(far_first))
    r_dz, r_sz, s_dz, s_sz = sems.take(nz), sems.take(1), sends.take(1), sends.take(1)
    for dz in orders:
        to = at((z + dz) % nz, x, e)
        send(DW.at[e, z, x], DW.at[e, z, x], s_dz, r_dz + dz, to)
    for dz in orders:
        to = at((z + dz) % nz, x, e)
        send(SR.at[z, x], SR.at[z, x], s_sz, r_sz, to)
    sent_later(s_dz, DW.at[e, 0 : nz - 1, x])
    sent_later(s_sz, SR.at[0 : nz - 1, x])

    s_px, r_px = sends.take(1), sems.take(nz)
    s_py, r_py = sends.take(G), sems.take(G * nz)
    s_c, r_c = sends.take(1), sems.take(1)

    def spread_shard(dz):
        zz = (z + nz - dz) % nz
        piece = DW.at[e, zz, x]
        send(piece, piece, s_px, r_px + dz, across)
        for d in range(1, G):
            send(piece, piece, s_py + d, r_py + d * nz + dz, at(z, x, ((y + d) % G) * 2 + core))
        send(piece, piece, s_c, r_c, sibling)

    spread_shard(0)
    sent_later(s_px, DW.at[e, :, x])
    for d in range(1, G):
        sent_later(s_py + d, DW.at[e, :, x])
    sent_later(s_c, DW.at[0:G])

    s_xi, r_xi = sends.take(1), sems.take(1)
    for k in range(nz):
        send(ein.at[1 - x, :, k * FC : (k + 1) * FC], WIN.at[k, z, x], s_xi, r_xi, across)
    sent_later(s_xi, WIN.at[:, z, x])

    XP, CT, RT, PM = b["XP"], b["CT"], b["RT"], b["PM"]

    @pl.when(z == 0)
    def _():
        UP[0][:, 0] = jnp.zeros((nz, 2, RF, FC), BF16)
        UP[1][0] = jnp.zeros((2, CF, D), BF16)

    @pl.when(z == nz - 1)
    def _():
        DN[0][:, nz - 1] = jnp.zeros((nz, 2, RF, FC), BF16)
        DN[1][nz - 1] = jnp.zeros((2, CF, D), BF16)

    for copy in token_in:
        copy.wait()
    lane = lax.broadcasted_iota(jnp.int32, (TP, 128), 1)
    lane_f = lane.astype(F32)
    swap = (
        lax.broadcasted_iota(jnp.int32, (2, 128), 0) == lax.broadcasted_iota(jnp.int32, (2, 128), 1)
    ).astype(BF16)
    for m in range(M):
        XP[m] = jnp.zeros((TP, D), BF16)
        CT[m] = jnp.zeros((TP, D), BF16)
        RT[m] = jnp.full((TP, 128), -1.0, F32)
        XP[m, 0:T] = b["XR"][:, m, :]
        CT[m, 0:T] = b["CR"][:, m, :]
        RT[m, 0:T] = tn(b["RR"][m].astype(BF16), swap)

    def onehot(m, j):
        return RT[m][:, j : j + 1] == lane_f

    before = (
        lax.broadcasted_iota(jnp.int32, (TP, TP), 1) < lax.broadcasted_iota(jnp.int32, (TP, TP), 0)
    ).astype(BF16)
    spots = lax.broadcasted_iota(jnp.int32, (TP, S), 1).astype(F32)
    for m in range(M):
        first = onehot(m, 0).astype(F32)
        second = onehot(m, 1).astype(F32)
        rank0 = nn(before, first.astype(BF16))
        rank1 = nn(before, second.astype(BF16)) + jnp.sum(first, axis=0, keepdims=True)
        for j, (hot, rank) in enumerate(((first, rank0), (second, rank1))):
            slot = jnp.sum(hot * rank, axis=-1, keepdims=True)
            route = RT[m][:, j : j + 1]
            spot = jnp.where(route >= 0, route * CP + slot, -1.0)
            PM[m, j] = (spots == spot).astype(BF16)

    def turn_of(i):
        return 0 if i == 0 else i % (nz - 1) + 1

    groups = (range(0, 2), range(2, nz))
    s_zi = [[sends.take(1) for _ in groups] for _ in range(2)]
    s_zo = [sends.take(1) for _ in range(2)]
    r_zi = [[sems.take(nz) for _ in groups] for _ in range(2)]
    r_zo = [sems.take(2 * nz) for _ in range(2)]
    for zz in range(nz):
        for side in range(2):
            count = zz + 1 if side == 0 else nz - zz
            if count < nz:
                for g, turns in enumerate(groups):
                    sent_later(s_zi[side][g], WIN.at[0 : len(turns), 0:count], z == zz)
                sent_later(s_zo[side], WOUT.at[0:count], z == zz)

    def reach(side, d, some=None):
        begun = z - d if side == 0 else z + d
        there = (begun >= 0) if side == 0 else (begun < nz)
        last = (z == nz - 1) if side == 0 else (z == 0)
        if some is not None:
            there = there & some(begun)
        return begun, there, there & jnp.logical_not(last)

    def onward(side):
        return at((z + 1) % nz if side == 0 else (z + nz - 1) % nz, x, e)

    def pass_in(g, d, halves=(0, 1)):
        for side in range(2):
            begun, there, goes = reach(side, d)
            r = r_zi[side][g]
            if d > 0:
                arrived(WIN.at[0 : len(groups[g]), begun], r + d, there)
            if d < nz - 1:

                @pl.when(goes)
                def _():
                    for i in groups[g]:
                        k = turn_of(i) if side == 1 else nz - 1 - turn_of(i)
                        for half in halves:
                            piece = WIN.at[k, begun, x if half == 0 else 1 - x]
                            send(piece, piece, s_zi[side][g], r + d + 1, onward(side))

    def pass_out(d, half, late=None, near=None):
        xx = x if half == 0 else 1 - x
        for side in range(2):
            odd = nz - 2 if side == 0 else 1
            some = None
            if late is not None:
                some = (lambda begun: begun == odd) if late else (lambda begun: begun != odd)
            if near is not None:
                lower = (z < h) if side == 0 else (z >= h)
                chosen = lower if near else jnp.logical_not(lower)
                some = lambda begun, odd=odd, chosen=chosen: (begun != odd) & chosen
            begun, there, goes = reach(side, d, some)
            r = r_zo[side] + 2 * d + half
            piece = WOUT.at[begun, xx]
            if d > 0:
                arrived(piece, r, there)
            if d < nz - 1:
                send(piece, piece, s_zo[side], r + 2, onward(side), goes)

    early, others = 0, 1
    for dz in orders[:2]:
        arrived(DW.at[e, (z + nz - dz) % nz, x], r_dz + dz)
        spread_shard(dz)
    pltpu.make_async_copy(WIN.at[:, z, x], WIN.at[:, z, x], LS.at[own_in]).wait()
    pass_in(early, 0, (0,))
    for dz in orders[2:]:
        arrived(DW.at[e, (z + nz - dz) % nz, x], r_dz + dz)
        spread_shard(dz)
    arrived(SR.at[0 : nz - 1, x], r_sz)
    r_sx = one_send(SR.at[:, x], SR.at[:, x], across)
    arrived(WIN.at[:, z, 1 - x], r_xi)
    pass_in(early, 0, (1,))
    own_out.wait()
    pass_out(0, 0)

    s_f1, r_f1 = sends.take(G), sems.take(G)
    s_f2, r_f2 = sends.take(G), sems.take(G)
    for d in range(1, G):
        sent_later(s_f1 + d, DW.at[e, 0:h, x])
        sent_later(s_f2 + d, DW.at[e, h:nz, x])

    def forward_shard(dz):
        zz = (z + nz - dz) % nz
        piece = DW.at[e, zz, 1 - x]
        arrived(piece, r_px + dz)
        for d in range(1, G):
            to = at(z, x, ((y + d) % G) * 2 + core)
            send(piece, piece, s_f1 + d, r_f1 + d, to, zz < h)
        send(piece, piece, s_c, r_c, sibling)
        for d in range(1, G):
            piece = DW.at[((y + G - d) % G) * 2 + core, zz, x]
            arrived(piece, r_py + d * nz + dz)
            send(piece, piece, s_f2 + d, r_f2 + d, across, zz >= h)
            send(piece, piece, s_c, r_c, sibling)

    for dz in [0] + orders:
        forward_shard(dz)
    for d in range(1, G):
        ee = ((y + G - d) % G) * 2 + core
        arrived(DW.at[ee, 0:h, 1 - x], r_f1 + d)
        arrived(DW.at[ee, h:nz, 1 - x], r_f2 + d)
        send(DW.at[ee, :, 1 - x], DW.at[ee, :, 1 - x], s_c, r_c, sibling)
    r_xo = one_send(eout.at[1 - x], WOUT.at[z, x], across)
    arrived(SR.at[:, 1 - x], r_sx)
    for zz in range(nz):
        for xx in range(2):
            SM[zz, xx] = tn(SR[zz, xx], pick).astype(BF16)
    arrived(DW.at[0:G], r_c)

    pass_in(early, 1)
    pass_in(others, 0)

    def dense(k):
        return DW[k].reshape(D, TW)

    small = SM[...].reshape(D, 128)
    gains = nt(pick, small)
    gain_one, gain_two = gains[NE : NE + 1], gains[NE + 1 : NE + 2]
    key_ok = lax.broadcasted_iota(jnp.int32, (1, TP), 1) < T
    low_half = lax.broadcasted_iota(jnp.int32, (1, pair), 1) < head
    N1, J, ATT, MID, N2 = b["N1"], b["J"], b["ATT"], b["MID"], b["N2"]
    GATES, XS, XB, GC, CROW = (b[k] for k in ("GATES", "XS", "XB", "GC", "CROW"))
    GSS, GRB, CSS, CSB = (b[k] for k in ("GSS", "GRB", "CSS", "CSB"))
    GCS, GCB, YS, YB, DXS, DXB = (b[k] for k in ("GCS", "GCB", "YS", "YB", "DXS", "DXB"))

    def half_of(value, i):
        keep = low_half if i == 0 else jnp.logical_not(low_half)
        return jnp.where(keep, value, jnp.zeros_like(value))

    def softmax_scores(query, keys):
        scores = jnp.where(key_ok, nt(query, keys) * scale, -1e30)
        raised = jnp.exp(scores - jnp.max(scores, axis=-1, keepdims=True))
        return raised * (1.0 / jnp.sum(raised, axis=-1, keepdims=True))

    def columns(base, hp):
        return pl.ds(pl.multiple_of(base + hp * pair, 128), pair)

    def chosen_of(m, j):
        gates = GATES[m]
        return jnp.sum(jnp.where(onehot(m, j), gates, 0.0), axis=-1, keepdims=True)

    def forward(m):
        tokens = XP[m].astype(F32)
        hat, _ = normalize(tokens)
        N1[m] = (hat * gain_one).astype(BF16)
        for k in range(nq):
            J[m, :, k * TW : (k + 1) * TW] = nn(N1[m], dense(k)).astype(BF16)

        def attend(hp, carry):
            query, keys, values = (J[m, :, columns(i * D, hp)] for i in range(3))
            total = jnp.zeros((TP, pair), F32)
            for i in range(2):
                probs = softmax_scores(half_of(query, i), keys).astype(BF16)
                total = total + nn(probs, half_of(values, i))
            ATT[m, :, columns(0, hp)] = total.astype(BF16)
            return carry

        lax.fori_loop(0, D // pair, attend, 0)
        for k in range(nb):
            cols = slice(k * TW, (k + 1) * TW)
            MID[m, :, cols] = XP[m, :, cols].astype(F32) + nn(ATT[m], dense(nq + k))
        hat, _ = normalize(MID[m])
        N2[m] = (hat * gain_two).astype(BF16)
        logits = jnp.where(lane < NE, nn(N2[m], small), -1e30)
        raised = jnp.exp(logits - jnp.max(logits, axis=-1, keepdims=True))
        GATES[m] = raised / jnp.sum(raised, axis=-1, keepdims=True)
        XS[m] = tn(PM[m, 0] + PM[m, 1], N2[m]).astype(BF16).reshape(NE, CP, D)
        weight = PM[m, 0].astype(F32) * chosen_of(m, 0) + PM[m, 1].astype(F32) * chosen_of(m, 1)
        CROW[0:1] = jnp.sum(weight, axis=0, keepdims=True)
        for k in range(NE):
            CSS[m, k, 0:1, 0:CP] = CROW[0:1, k * CP : (k + 1) * CP]

    diagonal = lax.broadcasted_iota(jnp.int32, (CP, 128), 0) == lax.broadcasted_iota(
        jnp.int32, (CP, 128), 1
    )

    def scale_grads(m):
        for p in range(NE):
            by_lane = CSB[m, p, 0:1]
            weight = jnp.sum(jnp.where(diagonal, by_lane, 0.0), axis=1, keepdims=True)
            GC[m, p * CP : (p + 1) * CP] = (weight * GRB[m, p].astype(F32)).astype(BF16)

    def exchange(src, dst, m, sem):
        def one(d, carry):
            p = (pme + d) % NE
            send(src.at[m, p], dst.at[m, pme], *sem, at(z, p % 2, p // 2))
            return carry

        lax.fori_loop(1, NE, one, 0)
        sent_later(sem[0], src.at[m, 0 : NE - 1])
        dst[m, pme] = src[m, pme]

    def exchanged(dst, m, sem):
        arrived(dst.at[m, 0 : NE - 1], sem[1])

    def pairs():
        return [(sends.take(1), sems.take(1)) for _ in range(M)]

    s_x, s_cs, s_gr, s_dx, s_gc, s_y = (pairs() for _ in range(6))
    for m in range(M):
        GSS[m] = tn(PM[m, 0] + PM[m, 1], CT[m]).astype(BF16).reshape(NE, CP, D)
        exchange(GSS, GRB, m, s_gr[m])
    for m in range(M):
        forward(m)
        exchange(XS, XB, m, s_x[m])
        exchange(CSS, CSB, m, s_cs[m])
        if m == 0:
            arrived(WOUT.at[z, 1 - x], r_xo)
            pass_out(0, 1, False)
    for d in range(2, nz):
        pass_in(early, d)
    pass_out(1, 0)
    pass_in(others, 1)
    pass_out(1, 1, False, True)
    if nz > 4:
        pass_out(1, 1, False, False)

    YACC, DXACC, AS, GHS = b["YACC"], b["DXACC"], b["AS"], b["GHS"]
    DWI, DWO = b["DWI"], b["DWO"]
    YACC[...] = jnp.zeros_like(YACC)
    DXACC[...] = jnp.zeros_like(DXACC)
    c0, c1 = math.sqrt(2.0 / math.pi), 0.044715

    OWN = (DWI, DWO)
    s_up = [(sends.take(1), sends.take(1)) for _ in range(2)]
    r_up = [(sems.take(nz * nz), sems.take(2 * nz)) for _ in range(2)]

    def expert_part(k, m):
        tokens = XB[m].reshape(S, D)
        grads = GC[m]
        for xx in range(2):
            cols = slice(xx * CF, (xx + 1) * CF)
            w_in = WIN[k, :, :, :, cols].reshape(D, CF)
            w_out = WOUT[k, xx]
            hidden = nn(tokens, w_in)
            grad_acted = nt(grads, w_out)
            square = hidden * hidden
            bent = jnp.tanh(c0 * hidden * (1.0 + c1 * square))
            acted = (0.5 * hidden * (1.0 + bent)).astype(BF16)
            slope = 0.5 * (1.0 + bent) + 0.5 * c0 * hidden * (1.0 - bent * bent) * (
                1.0 + 3.0 * c1 * square
            )
            grad_hidden = (grad_acted * slope).astype(BF16)
            AS[m, :, cols] = acted
            GHS[m, :, cols] = grad_hidden
            YACC[m] = YACC[m] + nn(acted, w_out)
            DXACC[m] = DXACC[m] + nt(grad_hidden, w_in)

    def expert_weights(k):
        grads = GC[...].reshape(M * S, D)
        tokens = XB[...].reshape(M * S, D)
        for xx in range(2):
            cols = slice(xx * CF, (xx + 1) * CF)
            DWO[k, xx] = tn(AS[:, :, cols].reshape(M * S, CF), grads).astype(BF16)
            DWI[k, :, :, :, cols] = (
                tn(tokens, GHS[:, :, cols].reshape(M * S, CF))
                .astype(BF16)
                .reshape(nz, 2, RF, CF)
            )

    def sum_step(side, i, begins):
        far = z if side == 0 else nz - 1 - z
        GOT = UP if side == 0 else DN
        turn = ((i % (nz - 1)) + 1) * jnp.minimum(i, 1)
        k = turn if side == 0 else nz - 1 - turn

        def tokens_side(j, carry):
            goal = nz - 1 - j
            t = goal if side == 0 else nz - 1 - goal
            rsem = r_up[side][0] + k * nz + t

            @pl.when(goal > far)
            def _():
                if not begins:
                    arrived(GOT[0].at[k, t], rsem)
                    DWI[k, t] = DWI[k, t] + GOT[0][k, t]
                send(DWI.at[k, t], GOT[0].at[k, t], s_up[side][0], rsem, onward(side))

            return carry

        def results_side():
            for xx in (1 - x, x):
                rsem = r_up[side][1] + 2 * k + xx
                if not begins:
                    arrived(GOT[1].at[k, xx], rsem)
                    DWO[k, xx] = DWO[k, xx] + GOT[1][k, xx]
                send(DWO.at[k, xx], GOT[1].at[k, xx], s_up[side][1], rsem, onward(side))

        pl.when(turn == nz - 1)(results_side)
        lax.fori_loop(0, nz - 1, tokens_side, 0)
        pl.when((turn > far) & (turn < nz - 1))(results_side)

    def sums_begin(i):
        for side in range(2):
            far = z if side == 0 else nz - 1 - z
            pl.when(far == 0)(functools.partial(sum_step, side, jnp.int32(i), True))

    def sums_pass(far_at, i):
        for side in range(2):
            far = z if side == 0 else nz - 1 - z
            pl.when(far == far_at)(functools.partial(sum_step, side, jnp.int32(i), False))

    passes = [(far, i) for far in range(1, nz - 1) for i in range(nz)]

    def sums_now(*wanted):
        for far, i in wanted:
            if (far, i) in passes:
                passes.remove((far, i))
                sums_pass(far, i)

    def sums_rest():
        for far in range(1, nz - 1):
            left = [i for k, i in passes if k == far]
            if len(left) <= 1:
                for i in left:
                    sums_pass(far, i)
            else:

                def one(i, carry, far=far):
                    sums_pass(far, i)
                    return carry

                lax.fori_loop(left[0], nz, one, 0)

    for zz in range(nz):
        for side in range(2):
            count = nz - 1 - zz if side == 0 else zz
            if count > 0:
                sent_later(s_up[side][0], DWI.at[:, 0:count], z == zz)
                sent_later(s_up[side][1], DWO.at[0:count], z == zz)

    def give_back(m):
        DXS[m] = DXACC[m].astype(BF16).reshape(NE, CP, D)
        exchange(DXS, DXB, m, s_dx[m])
        results = YACC[m].astype(BF16)
        YS[m] = results.reshape(NE, CP, D)
        for p in range(NE):
            rows = slice(p * CP, (p + 1) * CP)
            weight = jnp.sum(
                results[rows].astype(F32) * GRB[m, p].astype(F32), axis=1, keepdims=True
            )
            GCS[m, p, 0:1] = jnp.sum(jnp.where(diagonal, weight, 0.0), axis=0, keepdims=True)
        exchange(GCS, GCB, m, s_gc[m])

    when_two, when_far, when_late = (1, 2, nz - 1) if nz <= 4 else (0, 0, 0)
    for i in range(nz):
        if i == when_two:
            pass_in(others, 2)
            pass_out(2, 0)
            pass_out(2, 1, False)
        if i == when_far:
            pass_out(0, 1, True)
            for d in range(3, nz):
                pass_in(others, d)
                pass_out(d, 0)
                pass_out(d, 1, False)
        if i == when_late:
            for d in range(1, nz):
                pass_out(d, 1, True)
        block = turn_of(i) + (z // h) * (nz - 1 - 2 * turn_of(i))
        for m in range(M):
            if i == 0:
                exchanged(GRB, m, s_gr[m])
                exchanged(XB, m, s_x[m])
                exchanged(CSB, m, s_cs[m])
                scale_grads(m)
            expert_part(block, m)
            if i == 0 and m == 0 and nz <= 4:
                pass_out(1, 1, False, False)
            if i == nz - 1:
                give_back(m)
        expert_weights(block)
        sums_begin(i)

    r_fin, s_fin = (sems.take(nz), sems.take(1)), (sends.take(1), sends.take(1))
    FX, FY = (b["FXI"], b["FXO"]), (b["FYI"], b["FYO"])
    GI, GT = b["GI"], b["GT"]
    sent_later(s_fin[0], FX[0])
    sent_later(s_fin[1], FX[1])
    kept = []

    def total_of(kind, place):
        return (
            OWN[kind][place].astype(F32)
            + UP[kind][place].astype(F32)
            + DN[kind][place].astype(F32)
        )

    def sums_end_in(k):
        for side, ref, ok in ((0, UP, z > 0), (1, DN, z < nz - 1)):
            arrived(ref[0].at[k, z], r_up[side][0] + k * nz + z, ok)
        FX[0][k] = total_of(0, (k, z, 1 - x)).astype(BF16)
        send(FX[0].at[k], FY[0].at[k], s_fin[0], r_fin[0] + k, across)
        GI[x, :, k * FC : (k + 1) * FC] = total_of(0, (k, z, x))

    def sums_end_out():
        for xx, mine in ((1 - x, False), (x, True)):
            for side, ref, ok in ((0, UP, z > 0), (1, DN, z < nz - 1)):
                arrived(ref[1].at[z, xx], r_up[side][1] + 2 * z + xx, ok)
            if mine:
                GT[x] = total_of(1, (z, xx))
            else:
                FX[1][...] = total_of(1, (z, xx)).astype(BF16)
                send(FX[1], FY[1], s_fin[1], r_fin[1], across)

    def sums_close():
        kept.append(fetch(GI.at[x], gein.at[x]))
        kept.append(fetch(GT.at[x], geout.at[x]))
        for k in range(nz):
            arrived(FY[0].at[k], r_fin[0] + k)
            GI[1 - x, :, k * FC : (k + 1) * FC] = FY[0][k].astype(F32)
        kept.append(fetch(GI.at[1 - x], gein.at[1 - x]))
        arrived(FY[1], r_fin[1])
        GT[1 - x] = FY[1][...].astype(F32)
        kept.append(fetch(GT.at[1 - x], geout.at[1 - x]))

    GM, GA, GJ, GR = b["GM"], b["GA"], b["GJ"], b["GR"]
    DG = b["DG"]
    GR[...] = jnp.zeros_like(GR)

    def outputs(m):
        results = YB[m].reshape(S, D)
        out = MID[m] + chosen_of(m, 0) * nn(PM[m, 0], results)
        b["AR"][:, m, :] = (out + chosen_of(m, 1) * nn(PM[m, 1], results))[0:T]

    def backward_top(m):
        upstream = CT[m].astype(F32)
        for k in range(NE):
            CROW[0:1, k * CP : (k + 1) * CP] = GCB[m, k, 0:1, 0:CP]

        def grad_chosen(j):
            return jnp.sum(PM[m, j].astype(F32) * CROW[0:1], axis=-1, keepdims=True)

        gates = GATES[m]
        grad_gates = jnp.where(onehot(m, 0), grad_chosen(0), 0.0) + jnp.where(
            onehot(m, 1), grad_chosen(1), 0.0
        )
        grad_logits = (
            gates * (grad_gates - jnp.sum(grad_gates * gates, axis=-1, keepdims=True))
        ).astype(BF16)
        GR[0:NE] = GR[0:NE] + tn(grad_logits, N2[m])[0:NE]
        grad = nn(PM[m, 0] + PM[m, 1], DXB[m].reshape(S, D)) + nt(grad_logits, small)
        hat, rstd = normalize(MID[m])
        GR[NE + 1 : NE + 2] = GR[NE + 1 : NE + 2] + jnp.sum(grad * hat, axis=0, keepdims=True)
        grad_middle = upstream + normalize_back(grad * gain_two, hat, rstd)
        GM[m] = grad_middle
        branch = grad_middle.astype(BF16)
        N2[m] = branch
        back = None
        for k in range(nb):
            term = nt(branch[:, k * TW : (k + 1) * TW], dense(nq + k))
            back = term if back is None else back + term
        GA[m] = back.astype(BF16)

    def backward_heads(m):
        def attend(hp, carry):
            query, keys, values = (J[m, :, columns(i * D, hp)] for i in range(3))
            grads = GA[m, :, columns(0, hp)]
            grad_query = jnp.zeros((TP, pair), F32)
            grad_keys = jnp.zeros((TP, pair), F32)
            grad_values = jnp.zeros((TP, pair), F32)
            for i in range(2):
                part = half_of(query, i)
                upstream = half_of(grads, i)
                probs = softmax_scores(part, keys)
                grad_probs = nt(upstream, values)
                grad_values = grad_values + tn(probs.astype(BF16), upstream)
                grad_scores = (
                    probs
                    * (grad_probs - jnp.sum(grad_probs * probs, axis=-1, keepdims=True))
                ).astype(BF16)
                grad_query = grad_query + nn(grad_scores, half_of(keys, i))
                grad_keys = grad_keys + tn(grad_scores, part)
            GJ[m, :, columns(0, hp)] = (grad_query * scale).astype(BF16)
            GJ[m, :, columns(D, hp)] = (grad_keys * scale).astype(BF16)
            GJ[m, :, columns(2 * D, hp)] = grad_values.astype(BF16)
            return carry

        lax.fori_loop(0, D // pair, attend, 0)

    def backward_end(m):
        grad = None
        for k in range(nq):
            term = nt(GJ[m, :, k * TW : (k + 1) * TW], dense(k))
            grad = term if grad is None else grad + term
        hat, rstd = normalize(XP[m].astype(F32))
        GR[NE : NE + 1] = GR[NE : NE + 1] + jnp.sum(grad * hat, axis=0, keepdims=True)
        full = GM[m] + normalize_back(grad * gain_one, hat, rstd)
        b["IG"][m, :, 0, :] = full[0:T]

    sums_now((1, 0), (1, 1))
    for m in range(M):
        exchanged(DXB, m, s_dx[m])
        exchanged(GCB, m, s_gc[m])
        if m == M - 1:
            for k in range(M):
                exchange(YS, YB, k, s_y[k])
        backward_top(m)
        backward_heads(m)
        sums_now(*(((2, 0),) if m == 0 else ((1, 2), (2, 1)) if m == 1 else ()))
    for k in range(nb):
        part = tn(
            ATT[...].reshape(M * TP, D), N2[:, :, k * TW : (k + 1) * TW].reshape(M * TP, TW)
        )
        DG[nq + k] = part.astype(BF16).reshape(nz, 2, RF, TW)
    for k in range(nq):
        part = tn(
            N1[...].reshape(M * TP, D), GJ[:, :, k * TW : (k + 1) * TW].reshape(M * TP, TW)
        )
        DG[k] = part.astype(BF16).reshape(nz, 2, RF, TW)
    RB1, RY1, RX1, RX2, RY2, RZ, FIN = (
        b[k] for k in ("RB1", "RY1", "RX1", "RX2", "RY2", "RZ", "FIN")
    )
    GB, SB1, SB2, SB3, SB4 = (b[k] for k in ("GB", "SB1", "SB2", "SB3", "SB4"))
    s_r1, r_r1 = sends.take(1), sems.take(1)
    for j in range(G):
        send(DG.at[2 * j + 1 - core], RB1.at[j], s_r1, r_r1, sibling)
    sent_later(s_r1, RB1)
    for m in range(M):
        backward_end(m)
    kept.append(fetch(b["IG"], igrad))
    GB[...] = GR[...].astype(BF16)
    r_b1 = one_send(GB, SB1, sibling)
    arrived(RB1, r_r1)
    for j in range(G):
        DG[2 * j + core] = DG[2 * j + core] + RB1[j]
    s_ry1, r_ry1 = sends.take(G), sems.take(G)
    for d in range(1, G):
        q = (y + d) % G
        piece = DG.at[2 * q + core, 0:h]
        send(piece, RY1.at[y], s_ry1 + d, r_ry1 + d, at(z, x, 2 * q + core))
        sent_later(s_ry1 + d, piece)
    s_rx1, r_rx1 = sends.take(1), sems.take(1)
    for j in range(G):
        send(DG.at[2 * j + core, h:nz, 1 - x], RX1.at[j], s_rx1, r_rx1, across)
    sent_later(s_rx1, RX1)
    arrived(SB1, r_b1)
    SB2[y] = GB[...] + SB1[...]
    s_b2, r_b2 = sends.take(G), sems.take(G)
    for d in range(1, G):
        send(SB2.at[y], SB2.at[y], s_b2 + d, r_b2 + d, at(z, x, ((y + d) % G) * 2 + core))
        sent_later(s_b2 + d, SB2.at[y])
    sums_now((2, 2), (1, 3))
    for d in range(1, G):
        q = (y + G - d) % G
        arrived(RY1.at[q], r_ry1 + d)
        DG[e, 0:h] = DG[e, 0:h] + RY1[q]
    r_rx2 = one_send(DG.at[e, 0:h, 1 - x], RX2, across)
    arrived(RX1, r_rx1)
    for j in range(G):
        DG[2 * j + core, h:nz, x] = DG[2 * j + core, h:nz, x] + RX1[j]
    s_ry2, r_ry2 = sends.take(G), sems.take(G)
    for d in range(1, G):
        q = (y + d) % G
        piece = DG.at[2 * q + core, h:nz, x]
        send(piece, RY2.at[y], s_ry2 + d, r_ry2 + d, at(z, x, 2 * q + core))
        sent_later(s_ry2 + d, piece)
    for d in range(1, G):
        arrived(SB2.at[(y + G - d) % G], r_b2 + d)
    total = SB2[0].astype(F32)
    for j in range(1, G):
        total = total + SB2[j].astype(F32)
    SB3[x] = total.astype(BF16)
    r_b3 = one_send(SB3.at[x], SB3.at[x], across)
    arrived(RX2, r_rx2)
    DG[e, 0:h, x] = DG[e, 0:h, x] + RX2[...]
    for d in range(1, G):
        q = (y + G - d) % G
        arrived(RY2.at[q], r_ry2 + d)
        DG[e, h:nz, x] = DG[e, h:nz, x] + RY2[q]
    s_rz, r_rz = sends.take(1), sems.take(1)
    for dz in orders:
        zz = (z + dz) % nz
        send(DG.at[e, zz, x], RZ.at[z], s_rz, r_rz, at(zz, x, e))
    sent_later(s_rz, RZ.at[0 : nz - 1])
    arrived(SB3.at[1 - x], r_b3)
    SB4[z] = SB3[0] + SB3[1]
    s_b4, r_b4 = sends.take(1), sems.take(1)
    for dz in orders:
        send(SB4.at[z], SB4.at[z], s_b4, r_b4, at((z + dz) % nz, x, e))
    sent_later(s_b4, SB4.at[0 : nz - 1])
    sums_rest()
    for k in (0, nz - 1):
        sums_end_in(k)
    sums_end_out()
    for k in range(1, nz - 1):
        sums_end_in(k)
    for m in range(M):
        exchanged(YB, m, s_y[m])
        outputs(m)
    b["AO"][...] = b["AR"][...].astype(BF16)
    kept.append(fetch(b["AO"], act))
    RZ[z] = DG[e, z, x]
    arrived(RZ.at[0 : nz - 1], r_rz)
    total = RZ[0].astype(F32)
    for k in range(1, nz):
        total = total + RZ[k].astype(F32)
    FIN[e] = total.astype(BF16)
    s_fe, r_fe = sends.take(1), sems.take(1)

    def hand_out(d, carry):
        send(FIN.at[e], FIN.at[e], s_fe, r_fe, at(z, x, (e + d) % E))
        return carry

    lax.fori_loop(1, E, hand_out, 0)
    sent_later(s_fe, FIN.at[0 : E - 1])
    arrived(SB4.at[0 : nz - 1], r_b4)
    total = SB4[0].astype(F32)
    for k in range(1, nz):
        total = total + SB4[k].astype(F32)
    mine = (
        lax.broadcasted_iota(jnp.int32, (D, RF), 0)
        == lax.broadcasted_iota(jnp.int32, (D, RF), 1) + f * RF
    ).astype(F32)
    b["GS"][...] = lax.dot_general(
        total,
        mine,
        (((1,), (0,)), ((), ())),
        precision=lax.Precision.HIGHEST,
        preferred_element_type=F32,
    )
    kept.append(fetch(b["GS"].at[0:NE], grouter))
    kept.append(fetch(b["GS"].at[NE : NE + 1], ggain1))
    kept.append(fetch(b["GS"].at[NE + 1 : NE + 2], ggain2))
    sums_close()
    arrived(FIN.at[0 : E - 1], r_fe)
    for k in range(nq):
        b["GQ"][:, k * TW : (k + 1) * TW] = FIN[k].astype(F32)
    for k in range(nb):
        b["GO"][:, k * TW : (k + 1) * TW] = FIN[nq + k].astype(F32)
    kept.append(fetch(b["GQ"], gqkv))
    kept.append(fetch(b["GO"], gout))

    for cond, copy in pending:
        when(cond, copy.wait_send)
    for copy in kept:
        copy.wait()
    used = (sends.used, sems.used, locals_.used)
    assert all(a <= b for a, b in zip(used, counts)), (used, counts)


def hand_over(*refs):
    source, target, held = refs[:9], refs[9:18], refs[18:27]
    sem = refs[27]
    order = sorted(range(9), key=lambda k: -math.prod(source[k].shape))
    into = {k: pltpu.make_async_copy(source[k], held[k], sem.at[0, k]) for k in order}
    out = {k: pltpu.make_async_copy(held[k], target[k], sem.at[1, k]) for k in order}
    for k in order:
        into[k].start()
    for k in order:
        into[k].wait()
        out[k].start()
    for k in order:
        out[k].wait()


def body(
    mesh_shape,
    inputs,
    gain_attn,
    qkv_weight,
    out_weight,
    gain_moe,
    router_weight,
    expert_in,
    expert_out,
    routes,
    cotangent,
):
    micro, images, seq, width = inputs.shape
    c = layout(mesh_shape, micro, images * seq, width, expert_in.shape[2])
    rows = images * seq
    scratch = scratch_of(c)
    names = list(scratch)
    nz, G = c["nz"], c["G"]
    counts = (39 + 6 * G, 22 + 16 * nz + 2 * nz * nz + G * nz + 5 * G, 20)
    shapes = (
        ((rows, micro, width), BF16),
        ((micro, rows, 1, width), F32),
        (qkv_weight.shape, F32),
        (out_weight.shape, F32),
        ((1, c["RF"]), F32),
        ((1, c["RF"]), F32),
        ((c["NE"], c["RF"]), F32),
        (expert_in.shape, F32),
        (expert_out.shape, F32),
    )
    shapes = [jax.ShapeDtypeStruct(s, t) for s, t in shapes]
    anywhere = pl.BlockSpec(memory_space=pltpu.HBM)
    results = pl.pallas_call(
        functools.partial(kernel, c, names, counts),
        out_shape=shapes,
        in_specs=[anywhere] * 10,
        out_specs=[anywhere] * 9,
        scratch_shapes=[pltpu.VMEM(s, t) for s, t in scratch.values()]
        + [pltpu.SemaphoreType.DMA((count,)) for count in counts],
        compiler_params=pltpu.CompilerParams(
            collective_id=0, has_side_effects=True, vmem_limit_bytes=60 * 1024 * 1024
        ),
    )(
        jnp.transpose(inputs, (1, 2, 0, 3)).reshape(rows, micro, width),
        jnp.transpose(cotangent, (1, 2, 0, 3)).reshape(rows, micro, width),
        jnp.transpose(routes, (0, 1, 3, 2)).reshape(micro, 2, rows),
        qkv_weight,
        out_weight,
        gain_attn[None, :],
        gain_moe[None, :],
        router_weight.T,
        expert_in,
        expert_out,
    )
    act, igrad, gqkv, gout, ggain1, ggain2, grouter, gein, geout = pl.pallas_call(
        hand_over,
        out_shape=shapes,
        in_specs=[anywhere] * 9,
        out_specs=[anywhere] * 9,
        scratch_shapes=[pltpu.VMEM(s.shape, s.dtype) for s in shapes]
        + [pltpu.SemaphoreType.DMA((2, 9))],
        compiler_params=pltpu.CompilerParams(vmem_limit_bytes=60 * 1024 * 1024),
    )(*results)
    return (
        jnp.transpose(act.reshape(images, seq, micro, width), (2, 0, 1, 3)),
        igrad.reshape(inputs.shape),
        ggain1[0],
        gqkv,
        gout,
        ggain2[0],
        grouter.T,
        gein,
        geout,
    )


def solution(mesh):
    return jax.shard_map(
        functools.partial(body, dict(mesh.shape)),
        mesh=mesh,
        in_specs=(
            P(None, ("fsdp", "expert"), None, None),
            P("fsdp"),
            P("fsdp", None),
            P("fsdp", None),
            P("fsdp"),
            P("fsdp", None),
            P("expert", "fsdp", None),
            P("expert", "fsdp", None),
            P(None, ("fsdp", "expert"), None, None),
            P(None, ("fsdp", "expert"), None, None),
        ),
        out_specs=(
            P(None, ("fsdp", "expert"), None, None),
            P(None, ("fsdp", "expert"), None, None),
            P("fsdp"),
            P("fsdp", None),
            P("fsdp", None),
            P("fsdp"),
            P("fsdp", None),
            P("expert", "fsdp", None),
            P("expert", "fsdp", None),
        ),
        check_vma=False,
    )
```

```python
import functools
import math

import jax
import jax.numpy as jnp
from jax import lax
from jax.experimental import pallas as pl
from jax.experimental.pallas import tpu as pltpu
from jax.sharding import PartitionSpec as P

HEADS = 8
EPS = 1e-06
MESH = pl.DeviceIdType.MESH
F32 = jnp.float32
BF16 = jnp.bfloat16


def nn(a, b):
    return lax.dot_general(a, b, (((1,), (0,)), ((), ())), preferred_element_type=F32)


def nt(a, b):
    return lax.dot_general(a, b, (((1,), (1,)), ((), ())), preferred_element_type=F32)


def tn(a, b):
    return lax.dot_general(a, b, (((0,), (0,)), ((), ())), preferred_element_type=F32)


def normalize(values):
    center = jnp.mean(values, axis=-1, keepdims=True)
    shifted = values - center
    spread = jnp.mean(shifted * shifted, axis=-1, keepdims=True)
    rstd = lax.rsqrt(spread + EPS)
    return shifted * rstd, rstd


def normalize_back(grad, hat, rstd):
    return rstd * (
        grad
        - jnp.mean(grad, axis=-1, keepdims=True)
        - hat * jnp.mean(grad * hat, axis=-1, keepdims=True)
    )


class Semaphores:
    def __init__(self):
        self.used = 0

    def take(self, count):
        start = self.used
        self.used += count
        return start


SIZES = ("nz", "E", "G", "NE", "NR", "T", "TP", "CP", "S", "D", "FC", "RF", "CF", "M")


def layout(mesh_shape, micro, seq, width, ff_width):
    fsdp, peers = mesh_shape["fsdp"], mesh_shape["expert"]
    c = {}
    c["nz"] = fsdp // 2
    c["E"] = peers
    c["G"] = peers // 2
    c["NE"] = 2 * peers
    c["T"] = seq
    c["TP"] = -(-seq // 16) * 16
    c["CP"] = -(-max(2, 10 * seq // (4 * 2 * peers) + 1) // 16) * 16
    c["S"] = c["NE"] * c["CP"]
    c["NR"] = -(-(c["NE"] + 2) // 16) * 16
    c["D"] = width
    c["FF"] = ff_width
    c["RF"] = width // fsdp
    c["CF"] = ff_width // fsdp
    c["FC"] = 2 * c["CF"]
    c["WQ"] = 128 * -(-(3 * width // 128) // peers)
    c["WO"] = 128 * -(-(width // 128) // peers)
    c["M"] = micro
    return c


def scratch_of(c):
    nz, E, G, NE, NR, T, TP, CP, S, D, FC, RF, CF, M = (c[k] for k in SIZES)
    h = nz // 2
    v = {
        "XP": ((M, TP, D), BF16),
        "CT": ((M, TP, D), BF16),
        "XR": ((T, M, D), BF16),
        "CR": ((T, M, D), BF16),
        "AR": ((T, M, D), F32),
        "AO": ((T, M, D), BF16),
        "IG": ((M, T, 1, D), F32),
        "RR": ((M, 2, T), jnp.int32),
        "RT": ((M, TP, 128), F32),
        "SR": ((nz, 2, NR, RF), BF16),
        "G1": ((1, RF), BF16),
        "G2": ((1, RF), BF16),
        "RW": ((NE, RF), BF16),
        "GI": ((2, RF, nz * FC), BF16),
        "GT": ((2, CF, D), BF16),
        "GS": ((NR, RF), F32),
        "SM": ((nz, 2, RF, 128), BF16),
        "WIN": ((nz, nz, 2, RF, FC), BF16),
        "WOUT": ((nz, 2, CF, D), BF16),
        "N1": ((M, TP, D), BF16),
        "J": ((M, TP, 3 * D), BF16),
        "ATT": ((M, TP, D), BF16),
        "MID": ((M, TP, D), F32),
        "N2": ((M, TP, D), BF16),
        "GATES": ((M, TP, 128), F32),
        "PM": ((M, 2, TP, S), BF16),
        "XS": ((M, NE, CP, D), BF16),
        "XB": ((M, NE, CP, D), BF16),
        "GSS": ((M, NE, CP, D), BF16),
        "GRB": ((M, NE, CP, D), BF16),
        "CSS": ((M, NE, 8, 128), F32),
        "CSB": ((M, NE, 8, 128), F32),
        "CROW": ((8, S), F32),
        "GC": ((M, S, D), BF16),
        "YS": ((M, NE, CP, D), BF16),
        "YB": ((M, NE, CP, D), BF16),
        "DXS": ((M, NE, CP, D), BF16),
        "DXB": ((M, NE, CP, D), BF16),
        "GCS": ((M, NE, 8, 128), F32),
        "GCB": ((M, NE, 8, 128), F32),
        "YACC": ((M, S, D), F32),
        "DXACC": ((M, S, D), F32),
        "AS": ((M, S, FC), BF16),
        "GHS": ((M, S, FC), BF16),
        "DWI": ((nz, nz, 2, RF, FC), BF16),
        "DWO": ((nz, 2, CF, D), BF16),
        "UPI": ((nz, nz, 2, RF, FC), BF16),
        "UPO": ((nz, 2, CF, D), BF16),
        "DNI": ((nz, nz, 2, RF, FC), BF16),
        "DNO": ((nz, 2, CF, D), BF16),
        "FXI": ((nz, RF, FC), BF16),
        "FXO": ((CF, D), BF16),
        "GM": ((M, TP, D), F32),
        "GA": ((M, TP, D), BF16),
        "GJ": ((M, TP, 3 * D), BF16),
        "GR": ((NR, D), F32),
        "GB": ((NR, D), BF16),
        "SB1": ((NR, D), BF16),
        "SB2": ((G, NR, D), BF16),
        "SB3": ((2, NR, D), BF16),
        "SB4": ((nz, NR, D), BF16),
    }
    for name, wide in (("Q", c["WQ"]), ("O", c["WO"])):
        for part, lead in (
            ("W", (E, nz, 2)),
            ("G", (E, nz, 2)),
            ("B1", (G, nz, 2)),
            ("Y1", (G, h, 2)),
            ("X1", (G, nz - h)),
            ("X2", (h,)),
            ("Y2", (G, nz - h)),
            ("Z", (nz,)),
            ("F", (E,)),
        ):
            v[name + part] = (lead + (RF, wide), BF16)
    return v


def kernel(c, names, counts, *refs):
    nz, E, G, NE, NR, T, TP, CP, S, D, FC, RF, CF, M = (c[k] for k in SIZES)
    (xin, cot, routes, qkv_s, out_s, gain1, gain2, router, ein, eout) = refs[:10]
    (act, igrad, gqkv, gout, ggain1, ggain2, grouter, gein, geout) = refs[10:19]
    b = dict(zip(names, refs[19:]))
    SS, RS, LS = refs[-3:]
    h = nz // 2
    head = D // HEADS
    pair = 2 * head
    scale = 1.0 / math.sqrt(head)
    sems, sends, locals_ = Semaphores(), Semaphores(), Semaphores()
    pending = []

    f = lax.axis_index("fsdp")
    e = lax.axis_index("expert")
    z, x = f // 2, f % 2
    y, core = e // 2, e % 2
    pme = 2 * e + x

    def at(zz, xx, ee):
        return (zz * 2 + xx, ee)

    sibling = at(z, x, y * 2 + (1 - core))
    across = at(z, 1 - x, e)

    def copy_of(src, dst, ssem, rsem, device):
        return pltpu.make_async_remote_copy(
            src_ref=src,
            dst_ref=dst,
            send_sem=SS.at[ssem],
            recv_sem=RS.at[rsem],
            device_id=device,
            device_id_type=MESH,
        )

    def when(cond, run):
        if cond is None:
            run()
        else:
            pl.when(cond)(run)

    def send(src, dst, ssem, rsem, device, cond=None):
        when(cond, copy_of(src, dst, ssem, rsem, device).start)

    def arrived(dst, rsem, cond=None):
        when(cond, copy_of(dst, dst, 0, rsem, sibling).wait_recv)

    def sent_later(ssem, src, cond=None):
        pending.append((cond, copy_of(src, src, ssem, 0, sibling)))

    def one_send(src, dst, device):
        ssem, rsem = sends.take(1), sems.take(1)
        send(src, dst, ssem, rsem, device)
        sent_later(ssem, src)
        return rsem

    barrier = pltpu.get_barrier_semaphore()
    for dz in range(1, nz):
        pl.semaphore_signal(
            barrier, inc=1, device_id=at((z + dz) % nz, x, e), device_id_type=MESH
        )

    def greet(d, carry):
        p = (pme + d) % NE
        pl.semaphore_signal(barrier, inc=1, device_id=at(z, p % 2, p // 2), device_id_type=MESH)
        return carry

    lax.fori_loop(1, NE, greet, 0)

    SM, WIN, WOUT = b["SM"], b["WIN"], b["WOUT"]
    UP, DN = (b["UPI"], b["UPO"]), (b["DNI"], b["DNO"])

    def fetch(src, dst):
        copy = pltpu.make_async_copy(src, dst, LS.at[locals_.take(1)])
        copy.start()
        return copy

    far_first = [d for k in range(1, nz) for d in (k, nz - k) if 2 * k <= nz]
    orders = list(dict.fromkeys(far_first))

    class Dense:
        def __init__(self, name, shard, wide):
            self.name, self.shard, self.wide = name, shard, wide
            self.w, self.g = b[name + "W"], b[name + "G"]
            self.used = -(-shard.shape[1] // wide)
            self.own = locals_.take(1)
            for k in range(self.used):

                @pl.when(e == k)
                def _():
                    pltpu.make_async_copy(
                        self.columns(shard, k), self.w.at[k, z, x], LS.at[self.own]
                    ).start()

        def columns(self, ref, k):
            return ref.at[:, k * self.wide : (k + 1) * self.wide]

        def own_ready(self):
            copy = pltpu.make_async_copy(
                self.w.at[e, z, x], self.w.at[e, z, x], LS.at[self.own]
            )
            when(None if self.used == E else e < self.used, copy.wait)

        def along_z(self):
            w = self.w
            self.r_z, s_z = sems.take(nz - 1) - 1, sends.take(1)
            for dz in orders:
                to = at((z + dz) % nz, x, e)
                send(w.at[e, z, x], w.at[e, z, x], s_z, self.r_z + dz, to)
            sent_later(s_z, w.at[e, 0 : nz - 1, x])
            self.s_x, self.r_x = sends.take(1), sems.take(nz)
            self.s_y, self.r_y = sends.take(G - 1) - 1, sems.take((G - 1) * nz) - nz
            self.s_c, self.r_c = sends.take(1), sems.take(1)
            sent_later(self.s_x, w.at[e, :, x])
            for d in range(1, G):
                sent_later(self.s_y + d, w.at[e, :, x])
            sent_later(self.s_c, w.at[0:G])

        def spread(self, dz):
            zz = (z + nz - dz) % nz
            piece = self.w.at[e, zz, x]
            if dz > 0:
                arrived(piece, self.r_z + dz)
            send(piece, piece, self.s_x, self.r_x + dz, across)
            for d in range(1, G):
                to = at(z, x, ((y + d) % G) * 2 + core)
                send(piece, piece, self.s_y + d, self.r_y + d * nz + dz, to)
            send(piece, piece, self.s_c, self.r_c, sibling)

        def forward(self):
            w = self.w
            self.s_xy, self.r_xy = sends.take(G - 1) - 1, sems.take(G - 1) - 1
            self.s_yx, self.r_yx = sends.take(G - 1) - 1, sems.take(G - 1) - 1
            for d in range(1, G):
                sent_later(self.s_xy + d, w.at[e, 0:h, x])
                sent_later(self.s_yx + d, w.at[e, h:nz, x])
            for dz in [0] + orders:
                zz = (z + nz - dz) % nz
                piece = w.at[e, zz, 1 - x]
                arrived(piece, self.r_x + dz)
                for d in range(1, G):
                    to = at(z, x, ((y + d) % G) * 2 + core)
                    send(piece, piece, self.s_xy + d, self.r_xy + d, to, zz < h)
                send(piece, piece, self.s_c, self.r_c, sibling)
                for d in range(1, G):
                    piece = w.at[((y + G - d) % G) * 2 + core, zz, x]
                    arrived(piece, self.r_y + d * nz + dz)
                    send(piece, piece, self.s_yx + d, self.r_yx + d, across, zz >= h)
                    send(piece, piece, self.s_c, self.r_c, sibling)

        def corner(self):
            w = self.w
            for d in range(1, G):
                ee = ((y + G - d) % G) * 2 + core
                arrived(w.at[ee, 0:h, 1 - x], self.r_xy + d)
                arrived(w.at[ee, h:nz, 1 - x], self.r_yx + d)
                send(w.at[ee, :, 1 - x], w.at[ee, :, 1 - x], self.s_c, self.r_c, sibling)

        def ready(self):
            arrived(self.w.at[0:G], self.r_c)

        def blocks(self):
            for k in range(self.used):
                cols = slice(k * self.wide, min((k + 1) * self.wide, self.shard.shape[1]))
                yield cols, self.w[k].reshape(D, self.wide)

        def put(self, left, right):
            for k in range(self.used):
                cols = slice(k * self.wide, (k + 1) * self.wide)
                part = tn(left, right[:, :, cols].reshape(M * TP, self.wide))
                self.g[k] = part.astype(BF16).reshape(nz, 2, RF, self.wide)

        def sum_core(self):
            s, self.r_1 = sends.take(1), sems.take(1)
            for j in range(G):
                send(self.g.at[2 * j + 1 - core], b[self.name + "B1"].at[j], s, self.r_1, sibling)
            sent_later(s, b[self.name + "B1"])

        def sum_plane(self):
            g, first = self.g, b[self.name + "B1"]
            arrived(first, self.r_1)
            for j in range(G):
                g[2 * j + core] = g[2 * j + core] + first[j]
            s, self.r_y1 = sends.take(G - 1) - 1, sems.take(G - 1) - 1
            for d in range(1, G):
                q = (y + d) % G
                piece = g.at[2 * q + core, 0:h]
                send(piece, b[self.name + "Y1"].at[y], s + d, self.r_y1 + d, at(z, x, 2 * q + core))
                sent_later(s + d, piece)
            s, self.r_x1 = sends.take(1), sems.take(1)
            for j in range(G):
                piece = g.at[2 * j + core, h:nz, 1 - x]
                send(piece, b[self.name + "X1"].at[j], s, self.r_x1, across)
            sent_later(s, b[self.name + "X1"])

        def sum_cross(self):
            g, from_y, from_x = self.g, b[self.name + "Y1"], b[self.name + "X1"]
            for d in range(1, G):
                q = (y + G - d) % G
                arrived(from_y.at[q], self.r_y1 + d)
                g[e, 0:h] = g[e, 0:h] + from_y[q]
            self.r_x2 = one_send(g.at[e, 0:h, 1 - x], b[self.name + "X2"], across)
            arrived(from_x, self.r_x1)
            for j in range(G):
                g[2 * j + core, h:nz, x] = g[2 * j + core, h:nz, x] + from_x[j]
            s, self.r_y2 = sends.take(G - 1) - 1, sems.take(G - 1) - 1
            for d in range(1, G):
                q = (y + d) % G
                piece = g.at[2 * q + core, h:nz, x]
                send(piece, b[self.name + "Y2"].at[y], s + d, self.r_y2 + d, at(z, x, 2 * q + core))
                sent_later(s + d, piece)

        def sum_z(self):
            g, from_x, from_y = self.g, b[self.name + "X2"], b[self.name + "Y2"]
            arrived(from_x, self.r_x2)
            g[e, 0:h, x] = g[e, 0:h, x] + from_x[...]
            for d in range(1, G):
                q = (y + G - d) % G
                arrived(from_y.at[q], self.r_y2 + d)
                g[e, h:nz, x] = g[e, h:nz, x] + from_y[q]
            s, self.r_z2 = sends.take(1), sems.take(1)
            parts = b[self.name + "Z"]
            for dz in orders:
                zz = (z + dz) % nz
                send(g.at[e, zz, x], parts.at[z], s, self.r_z2, at(zz, x, e))
            sent_later(s, parts.at[0 : nz - 1])
            parts[z] = g[e, z, x]

        def hand_out(self):
            parts, done = b[self.name + "Z"], b[self.name + "F"]
            arrived(parts.at[0 : nz - 1], self.r_z2)
            total = parts[0].astype(F32)
            for k in range(1, nz):
                total = total + parts[k].astype(F32)
            done[e] = total.astype(BF16)
            s, self.r_f = sends.take(1), sems.take(1)

            def one(d, carry):
                send(done.at[e], done.at[e], s, self.r_f, at(z, x, (e + d) % E))
                return carry

            lax.fori_loop(1, E, one, 0)
            sent_later(s, done.at[0 : E - 1])

        def leave(self, out):
            done = b[self.name + "F"]
            arrived(done.at[0 : E - 1], self.r_f)
            for k in range(self.used):
                kept.append(fetch(done.at[k], self.columns(out, k)))

    qkv, proj = Dense("Q", qkv_s, c["WQ"]), Dense("O", out_s, c["WO"])
    kept = []

    SR = b["SR"]
    SR[z, x] = jnp.zeros((NR, RF), BF16)
    small_in = [
        fetch(gain1, b["G1"]),
        fetch(gain2, b["G2"]),
        fetch(router, b["RW"]),
    ]
    token_in = [fetch(routes, b["RR"]), fetch(xin, b["XR"]), fetch(cot, b["CR"])]
    own_in = locals_.take(1)
    for k in range(nz):
        pltpu.make_async_copy(
            ein.at[x, :, k * FC : (k + 1) * FC], WIN.at[k, z, x], LS.at[own_in]
        ).start()
    own_out = fetch(eout.at[x], WOUT.at[z, x])

    for copy in small_in:
        copy.wait()
    SR[z, x, 0:NE] = b["RW"][...]
    SR[z, x, NE : NE + 1] = b["G1"][...]
    SR[z, x, NE + 1 : NE + 2] = b["G2"][...]
    entry = lax.broadcasted_iota(jnp.int32, (NR, 128), 0)
    place = lax.broadcasted_iota(jnp.int32, (NR, 128), 1)
    pick = (
        ((entry < NE) & (entry == place))
        | ((entry >= NE) & (entry < NE + 2) & (place == entry - NE + 126))
    ).astype(BF16)
    qkv.own_ready()
    proj.own_ready()
    pl.semaphore_wait(barrier, nz - 1 + NE - 1)

    qkv.along_z()
    r_sz, s_sz = sems.take(1), sends.take(1)
    for dz in orders:
        send(SR.at[z, x], SR.at[z, x], s_sz, r_sz, at((z + dz) % nz, x, e))
    sent_later(s_sz, SR.at[0 : nz - 1, x])
    qkv.spread(0)

    s_xi, r_xi = sends.take(1), sems.take(1)
    for k in range(nz):
        send(ein.at[1 - x, :, k * FC : (k + 1) * FC], WIN.at[k, z, x], s_xi, r_xi, across)
    sent_later(s_xi, WIN.at[:, z, x])


    XP, CT, RT, PM = b["XP"], b["CT"], b["RT"], b["PM"]

    @pl.when(z == 0)
    def _():
        UP[0][:, 0] = jnp.zeros((nz, 2, RF, FC), BF16)
        UP[1][0] = jnp.zeros((2, CF, D), BF16)

    @pl.when(z == nz - 1)
    def _():
        DN[0][:, nz - 1] = jnp.zeros((nz, 2, RF, FC), BF16)
        DN[1][nz - 1] = jnp.zeros((2, CF, D), BF16)

    for copy in token_in:
        copy.wait()
    lane = lax.broadcasted_iota(jnp.int32, (TP, 128), 1)
    lane_f = lane.astype(F32)
    swap = (
        lax.broadcasted_iota(jnp.int32, (2, 128), 0) == lax.broadcasted_iota(jnp.int32, (2, 128), 1)
    ).astype(BF16)
    for m in range(M):
        XP[m] = jnp.zeros((TP, D), BF16)
        CT[m] = jnp.zeros((TP, D), BF16)
        RT[m] = jnp.full((TP, 128), -1.0, F32)
        XP[m, 0:T] = b["XR"][:, m, :]
        CT[m, 0:T] = b["CR"][:, m, :]
        RT[m, 0:T] = tn(b["RR"][m].astype(BF16), swap)

    def onehot(m, j):
        return RT[m][:, j : j + 1] == lane_f

    before = (
        lax.broadcasted_iota(jnp.int32, (TP, TP), 1) < lax.broadcasted_iota(jnp.int32, (TP, TP), 0)
    ).astype(BF16)
    spots = lax.broadcasted_iota(jnp.int32, (TP, S), 1).astype(F32)
    for m in range(M):
        first = onehot(m, 0).astype(F32)
        second = onehot(m, 1).astype(F32)
        rank0 = nn(before, first.astype(BF16))
        rank1 = nn(before, second.astype(BF16)) + jnp.sum(first, axis=0, keepdims=True)
        for j, (hot, rank) in enumerate(((first, rank0), (second, rank1))):
            slot = jnp.sum(hot * rank, axis=-1, keepdims=True)
            route = RT[m][:, j : j + 1]
            spot = jnp.where(route >= 0, route * CP + slot, -1.0)
            PM[m, j] = (spots == spot).astype(BF16)

    def turn_of(i):
        return 0 if i == 0 else i % (nz - 1) + 1

    groups = (range(0, 2), range(2, nz))
    s_zi = [[sends.take(1) for _ in groups] for _ in range(2)]
    s_zo = [sends.take(1) for _ in range(2)]
    r_zi = [[sems.take(nz) for _ in groups] for _ in range(2)]
    r_zo = [sems.take(2 * nz) for _ in range(2)]
    for zz in range(nz):
        for side in range(2):
            count = zz + 1 if side == 0 else nz - zz
            if count < nz:
                for g, turns in enumerate(groups):
                    sent_later(s_zi[side][g], WIN.at[0 : len(turns), 0:count], z == zz)
                sent_later(s_zo[side], WOUT.at[0:count], z == zz)

    def reach(side, d, some=None):
        begun = z - d if side == 0 else z + d
        there = (begun >= 0) if side == 0 else (begun < nz)
        last = (z == nz - 1) if side == 0 else (z == 0)
        if some is not None:
            there = there & some(begun)
        return begun, there, there & jnp.logical_not(last)

    def onward(side):
        return at((z + 1) % nz if side == 0 else (z + nz - 1) % nz, x, e)

    def pass_in(g, d, halves=(0, 1)):
        for side in range(2):
            begun, there, goes = reach(side, d)
            r = r_zi[side][g]
            if d > 0:
                arrived(WIN.at[0 : len(groups[g]), begun], r + d, there)
            if d < nz - 1:

                @pl.when(goes)
                def _():
                    for i in groups[g]:
                        k = turn_of(i) if side == 1 else nz - 1 - turn_of(i)
                        for half in halves:
                            piece = WIN.at[k, begun, x if half == 0 else 1 - x]
                            send(piece, piece, s_zi[side][g], r + d + 1, onward(side))

    def pass_out(d, half, late=None, near=None):
        xx = x if half == 0 else 1 - x
        for side in range(2):
            odd = nz - 2 if side == 0 else 1
            some = None
            if late is not None:
                some = (lambda begun: begun == odd) if late else (lambda begun: begun != odd)
            if near is not None:
                lower = (z < h) if side == 0 else (z >= h)
                chosen = lower if near else jnp.logical_not(lower)
                some = lambda begun, odd=odd, chosen=chosen: (begun != odd) & chosen
            begun, there, goes = reach(side, d, some)
            r = r_zo[side] + 2 * d + half
            piece = WOUT.at[begun, xx]
            if d > 0:
                arrived(piece, r, there)
            if d < nz - 1:
                send(piece, piece, s_zo[side], r + 2, onward(side), goes)

    early, others = 0, 1
    GATES, XS, XB, GC, CROW = (b[k] for k in ("GATES", "XS", "XB", "GC", "CROW"))
    GSS, GRB, CSS, CSB = (b[k] for k in ("GSS", "GRB", "CSS", "CSB"))
    GCS, GCB, YS, YB, DXS, DXB = (b[k] for k in ("GCS", "GCB", "YS", "YB", "DXS", "DXB"))

    def exchange(src, dst, m, sem):
        def one(d, carry):
            p = (pme + d) % NE
            send(src.at[m, p], dst.at[m, pme], *sem, at(z, p % 2, p // 2))
            return carry

        lax.fori_loop(1, NE, one, 0)
        sent_later(sem[0], src.at[m, 0 : NE - 1])
        dst[m, pme] = src[m, pme]

    def exchanged(dst, m, sem):
        arrived(dst.at[m, 0 : NE - 1], sem[1])

    def pairs():
        return [(sends.take(1), sems.take(1)) for _ in range(M)]

    s_x, s_cs, s_gr, s_dx, s_gc, s_y = (pairs() for _ in range(6))
    for m in range(M):
        GSS[m] = tn(PM[m, 0] + PM[m, 1], CT[m]).astype(BF16).reshape(NE, CP, D)

    for dz in orders[:2]:
        qkv.spread(dz)
    proj.along_z()
    proj.spread(0)
    pltpu.make_async_copy(WIN.at[:, z, x], WIN.at[:, z, x], LS.at[own_in]).wait()
    pass_in(early, 0, (0,))
    for dz in orders[2:]:
        qkv.spread(dz)
    arrived(SR.at[0 : nz - 1, x], r_sz)
    r_sx = one_send(SR.at[:, x], SR.at[:, x], across)
    own_out.wait()
    pass_out(0, 0)
    arrived(WIN.at[:, z, 1 - x], r_xi)
    pass_in(early, 0, (1,))
    qkv.forward()
    for dz in orders:
        proj.spread(dz)
    proj.forward()
    r_xo = one_send(eout.at[1 - x], WOUT.at[z, x], across)
    for m in range(M):
        exchange(GSS, GRB, m, s_gr[m])
    pass_in(others, 0, (0,))
    arrived(SR.at[:, 1 - x], r_sx)
    for zz in range(nz):
        for xx in range(2):
            SM[zz, xx] = tn(SR[zz, xx], pick).astype(BF16)
    qkv.corner()
    qkv.ready()

    small = SM[...].reshape(D, 128)
    gains = nt(pick, small)
    gain_one, gain_two = gains[NE : NE + 1], gains[NE + 1 : NE + 2]
    key_ok = lax.broadcasted_iota(jnp.int32, (1, TP), 1) < T
    low_half = lax.broadcasted_iota(jnp.int32, (1, pair), 1) < head
    N1, J, ATT, MID, N2 = b["N1"], b["J"], b["ATT"], b["MID"], b["N2"]
    def half_of(value, i):
        keep = low_half if i == 0 else jnp.logical_not(low_half)
        return jnp.where(keep, value, jnp.zeros_like(value))

    def softmax_scores(query, keys):
        scores = jnp.where(key_ok, nt(query, keys) * scale, -1e30)
        raised = jnp.exp(scores - jnp.max(scores, axis=-1, keepdims=True))
        return raised * (1.0 / jnp.sum(raised, axis=-1, keepdims=True))

    def columns(base, hp):
        return pl.ds(pl.multiple_of(base + hp * pair, 128), pair)

    def chosen_of(m, j):
        gates = GATES[m]
        return jnp.sum(jnp.where(onehot(m, j), gates, 0.0), axis=-1, keepdims=True)

    def forward(m):
        tokens = XP[m].astype(F32)
        hat, _ = normalize(tokens)
        N1[m] = (hat * gain_one).astype(BF16)
        for cols, block in qkv.blocks():
            J[m, :, cols] = nn(N1[m], block).astype(BF16)

        def attend(hp, carry):
            query, keys, values = (J[m, :, columns(i * D, hp)] for i in range(3))
            total = jnp.zeros((TP, pair), F32)
            for i in range(2):
                probs = softmax_scores(half_of(query, i), keys).astype(BF16)
                total = total + nn(probs, half_of(values, i))
            ATT[m, :, columns(0, hp)] = total.astype(BF16)
            return carry

        lax.fori_loop(0, D // pair, attend, 0)
        if m == 0:
            pass_in(early, 1)
            pass_in(others, 0, (1,))
            proj.corner()
            proj.ready()
        for cols, block in proj.blocks():
            MID[m, :, cols] = XP[m, :, cols].astype(F32) + nn(ATT[m], block)
        hat, _ = normalize(MID[m])
        N2[m] = (hat * gain_two).astype(BF16)
        logits = jnp.where(lane < NE, nn(N2[m], small), -1e30)
        raised = jnp.exp(logits - jnp.max(logits, axis=-1, keepdims=True))
        GATES[m] = raised / jnp.sum(raised, axis=-1, keepdims=True)
        XS[m] = tn(PM[m, 0] + PM[m, 1], N2[m]).astype(BF16).reshape(NE, CP, D)
        weight = PM[m, 0].astype(F32) * chosen_of(m, 0) + PM[m, 1].astype(F32) * chosen_of(m, 1)
        CROW[0:1] = jnp.sum(weight, axis=0, keepdims=True)
        for k in range(NE):
            CSS[m, k, 0:1, 0:CP] = CROW[0:1, k * CP : (k + 1) * CP]

    diagonal = lax.broadcasted_iota(jnp.int32, (CP, 128), 0) == lax.broadcasted_iota(
        jnp.int32, (CP, 128), 1
    )

    def scale_grads(m):
        for p in range(NE):
            by_lane = CSB[m, p, 0:1]
            weight = jnp.sum(jnp.where(diagonal, by_lane, 0.0), axis=1, keepdims=True)
            GC[m, p * CP : (p + 1) * CP] = (weight * GRB[m, p].astype(F32)).astype(BF16)

    for m in range(M):
        forward(m)
        exchange(XS, XB, m, s_x[m])
        exchange(CSS, CSB, m, s_cs[m])
        if m == 0:
            arrived(WOUT.at[z, 1 - x], r_xo)
            pass_out(0, 1, False)
    pass_in(early, 2)
    pass_out(1, 0)
    pass_in(others, 1)
    for d in range(3, nz):
        pass_in(early, d)
    pass_out(1, 1, False, True)
    if nz > 4:
        pass_out(1, 1, False, False)

    YACC, DXACC, AS, GHS = b["YACC"], b["DXACC"], b["AS"], b["GHS"]
    DWI, DWO = b["DWI"], b["DWO"]
    YACC[...] = jnp.zeros_like(YACC)
    DXACC[...] = jnp.zeros_like(DXACC)
    c0, c1 = math.sqrt(2.0 / math.pi), 0.044715

    OWN = (DWI, DWO)
    s_up = [(sends.take(1), sends.take(1)) for _ in range(2)]
    r_up = [(sems.take(nz * nz), sems.take(2 * nz)) for _ in range(2)]

    def expert_part(k, m):
        tokens = XB[m].reshape(S, D)
        grads = GC[m]
        for xx in range(2):
            cols = slice(xx * CF, (xx + 1) * CF)
            w_in = WIN[k, :, :, :, cols].reshape(D, CF)
            w_out = WOUT[k, xx]
            hidden = nn(tokens, w_in)
            grad_acted = nt(grads, w_out)
            square = hidden * hidden
            bent = jnp.tanh(c0 * hidden * (1.0 + c1 * square))
            acted = (0.5 * hidden * (1.0 + bent)).astype(BF16)
            slope = 0.5 * (1.0 + bent) + 0.5 * c0 * hidden * (1.0 - bent * bent) * (
                1.0 + 3.0 * c1 * square
            )
            grad_hidden = (grad_acted * slope).astype(BF16)
            AS[m, :, cols] = acted
            GHS[m, :, cols] = grad_hidden
            YACC[m] = YACC[m] + nn(acted, w_out)
            DXACC[m] = DXACC[m] + nt(grad_hidden, w_in)

    def expert_weights(k):
        grads = GC[...].reshape(M * S, D)
        tokens = XB[...].reshape(M * S, D)
        for xx in range(2):
            cols = slice(xx * CF, (xx + 1) * CF)
            DWO[k, xx] = tn(AS[:, :, cols].reshape(M * S, CF), grads).astype(BF16)
            DWI[k, :, :, :, cols] = (
                tn(tokens, GHS[:, :, cols].reshape(M * S, CF))
                .astype(BF16)
                .reshape(nz, 2, RF, CF)
            )

    def sum_step(side, i, begins, parts):
        far = z if side == 0 else nz - 1 - z
        GOT = UP if side == 0 else DN
        turn = ((i % (nz - 1)) + 1) * jnp.minimum(i, 1)
        k = turn if side == 0 else nz - 1 - turn

        def tokens_side(j, carry):
            goal = nz - 1 - j
            t = goal if side == 0 else nz - 1 - goal
            rsem = r_up[side][0] + k * nz + t

            @pl.when(goal > far)
            def _():
                if not begins:
                    arrived(GOT[0].at[k, t], rsem)
                    DWI[k, t] = DWI[k, t] + GOT[0][k, t]
                send(DWI.at[k, t], GOT[0].at[k, t], s_up[side][0], rsem, onward(side))

            return carry

        def results_side():
            for xx in [xx for part, xx in ((1, 1 - x), (2, x)) if part in parts]:
                rsem = r_up[side][1] + 2 * k + xx
                if not begins:
                    arrived(GOT[1].at[k, xx], rsem)
                    DWO[k, xx] = DWO[k, xx] + GOT[1][k, xx]
                send(DWO.at[k, xx], GOT[1].at[k, xx], s_up[side][1], rsem, onward(side))

        if parts != (0,):
            pl.when(turn == nz - 1)(results_side)
        if 0 in parts:
            lax.fori_loop(0, nz - 1, tokens_side, 0)
        if parts != (0,):
            pl.when((turn > far) & (turn < nz - 1))(results_side)

    def sums_begin(i, parts=(0, 1, 2)):
        for side in range(2):
            far = z if side == 0 else nz - 1 - z
            step = functools.partial(sum_step, side, jnp.int32(i), True, parts)
            pl.when(far == 0)(step)

    def sums_pass(far_at, i, parts=(0, 1, 2)):
        for side in range(2):
            far = z if side == 0 else nz - 1 - z
            step = functools.partial(sum_step, side, jnp.int32(i), False, parts)
            pl.when(far == far_at)(step)

    passes = [(far, i, part) for far in range(1, nz - 1) for i in range(nz) for part in range(3)]

    def sums_now(*wanted):
        for step in wanted:
            if step in passes:
                passes.remove(step)
                sums_pass(step[0], step[1], (step[2],))

    def sums_rest():
        for far in range(1, nz - 1):
            left = [step for step in passes if step[0] == far]
            if nz <= 4:
                for _, i, part in left:
                    sums_pass(far, i, (part,))
            else:

                def one(i, carry, far=far):
                    sums_pass(far, i)
                    return carry

                lax.fori_loop(left[0][1], nz, one, 0)

    for zz in range(nz):
        for side in range(2):
            count = nz - 1 - zz if side == 0 else zz
            if count > 0:
                sent_later(s_up[side][0], DWI.at[:, 0:count], z == zz)
                sent_later(s_up[side][1], DWO.at[0:count], z == zz)

    def give_back(m):
        DXS[m] = DXACC[m].astype(BF16).reshape(NE, CP, D)
        exchange(DXS, DXB, m, s_dx[m])
        results = YACC[m].astype(BF16)
        YS[m] = results.reshape(NE, CP, D)
        for p in range(NE):
            rows = slice(p * CP, (p + 1) * CP)
            weight = jnp.sum(
                results[rows].astype(F32) * GRB[m, p].astype(F32), axis=1, keepdims=True
            )
            GCS[m, p, 0:1] = jnp.sum(jnp.where(diagonal, weight, 0.0), axis=0, keepdims=True)
        exchange(GCS, GCB, m, s_gc[m])

    when_two, when_far, when_late = (1, 2, nz - 1) if nz <= 4 else (0, 0, 0)
    for i in range(nz):
        if i == when_two:
            pass_in(others, 2)
            pass_out(2, 0)
            pass_out(2, 1, False)
        if i == when_far:
            pass_out(0, 1, True)
            for d in range(3, nz):
                pass_in(others, d)
                pass_out(d, 0)
                pass_out(d, 1, False)
        if i == when_late:
            for d in range(1, nz):
                pass_out(d, 1, True)
            sums_now((1, 0, 0), (1, 0, 1), (1, 0, 2))
        block = turn_of(i) + (z // h) * (nz - 1 - 2 * turn_of(i))
        for m in range(M):
            if i == 0:
                exchanged(GRB, m, s_gr[m])
                exchanged(XB, m, s_x[m])
                exchanged(CSB, m, s_cs[m])
                scale_grads(m)
            expert_part(block, m)
            if i == 0 and m == 0 and nz <= 4:
                pass_out(1, 1, False, False)
            if i == nz - 1:
                give_back(m)
        if i == nz - 1:
            for m in range(M):
                exchange(YS, YB, m, s_y[m])
        expert_weights(block)
        sums_begin(i, (0, 1, 2) if i < nz - 1 else (0, 1))

    r_fin, s_fin = (sems.take(nz), sems.take(1)), (sends.take(1), sends.take(1))
    FX = (b["FXI"], b["FXO"])
    GI, GT = b["GI"], b["GT"]
    sent_later(s_fin[0], FX[0])
    sent_later(s_fin[1], FX[1])

    def total_of(kind, place):
        return (
            OWN[kind][place].astype(F32)
            + UP[kind][place].astype(F32)
            + DN[kind][place].astype(F32)
        )

    def sums_end_in(k):
        cols = pl.ds(pl.multiple_of(k * FC, 128), FC)
        for side, ref, ok in ((0, UP, z > 0), (1, DN, z < nz - 1)):
            arrived(ref[0].at[k, z], r_up[side][0] + k * nz + z, ok)
        FX[0][k] = total_of(0, (k, z, 1 - x)).astype(BF16)
        send(FX[0].at[k], GI.at[x, :, cols], s_fin[0], r_fin[0] + k, across)
        GI[x, :, cols] = total_of(0, (k, z, x)).astype(BF16)

    def sums_end_out(mine):
        xx = x if mine else 1 - x
        for side, ref, ok in ((0, UP, z > 0), (1, DN, z < nz - 1)):
            arrived(ref[1].at[z, xx], r_up[side][1] + 2 * z + xx, ok)
        if mine:
            GT[x] = total_of(1, (z, xx)).astype(BF16)
        else:
            FX[1][...] = total_of(1, (z, xx)).astype(BF16)
            send(FX[1], GT.at[x], s_fin[1], r_fin[1], across)

    at_end = (z == 0) | (z == nz - 1)
    upper = z // h
    first_ends = [nz - 1 - upper * (nz - 1), 1 + upper * (nz - 3)]
    last_ends = [upper * (nz - 1), 2 - upper * (5 - nz)] if nz == 4 else []

    def sums_close():
        kept.append(fetch(GI.at[x], gein.at[x]))
        kept.append(fetch(GT.at[x], geout.at[x]))
        arrived(GT.at[1 - x], r_fin[1])
        kept.append(fetch(GT.at[1 - x], geout.at[1 - x]))
        for k in range(nz):
            arrived(GI.at[1 - x, :, k * FC : (k + 1) * FC], r_fin[0] + k)
        kept.append(fetch(GI.at[1 - x], gein.at[1 - x]))

    GM, GA, GJ, GR = b["GM"], b["GA"], b["GJ"], b["GR"]
    GR[...] = jnp.zeros_like(GR)

    def outputs(m):
        results = YB[m].reshape(S, D)
        out = MID[m] + chosen_of(m, 0) * nn(PM[m, 0], results)
        b["AR"][:, m, :] = (out + chosen_of(m, 1) * nn(PM[m, 1], results))[0:T]

    def backward_top(m):
        upstream = CT[m].astype(F32)
        for k in range(NE):
            CROW[0:1, k * CP : (k + 1) * CP] = GCB[m, k, 0:1, 0:CP]

        def grad_chosen(j):
            return jnp.sum(PM[m, j].astype(F32) * CROW[0:1], axis=-1, keepdims=True)

        gates = GATES[m]
        grad_gates = jnp.where(onehot(m, 0), grad_chosen(0), 0.0) + jnp.where(
            onehot(m, 1), grad_chosen(1), 0.0
        )
        grad_logits = (
            gates * (grad_gates - jnp.sum(grad_gates * gates, axis=-1, keepdims=True))
        ).astype(BF16)
        GR[0:NE] = GR[0:NE] + tn(grad_logits, N2[m])[0:NE]
        grad = nn(PM[m, 0] + PM[m, 1], DXB[m].reshape(S, D)) + nt(grad_logits, small)
        hat, rstd = normalize(MID[m])
        GR[NE + 1 : NE + 2] = GR[NE + 1 : NE + 2] + jnp.sum(grad * hat, axis=0, keepdims=True)
        grad_middle = upstream + normalize_back(grad * gain_two, hat, rstd)
        GM[m] = grad_middle
        branch = grad_middle.astype(BF16)
        N2[m] = branch
        back = None
        for cols, block in proj.blocks():
            term = nt(branch[:, cols], block)
            back = term if back is None else back + term
        GA[m] = back.astype(BF16)

    def backward_heads(m):
        def attend(hp, carry):
            query, keys, values = (J[m, :, columns(i * D, hp)] for i in range(3))
            grads = GA[m, :, columns(0, hp)]
            grad_query = jnp.zeros((TP, pair), F32)
            grad_keys = jnp.zeros((TP, pair), F32)
            grad_values = jnp.zeros((TP, pair), F32)
            for i in range(2):
                part = half_of(query, i)
                upstream = half_of(grads, i)
                probs = softmax_scores(part, keys)
                grad_probs = nt(upstream, values)
                grad_values = grad_values + tn(probs.astype(BF16), upstream)
                grad_scores = (
                    probs
                    * (grad_probs - jnp.sum(grad_probs * probs, axis=-1, keepdims=True))
                ).astype(BF16)
                grad_query = grad_query + nn(grad_scores, half_of(keys, i))
                grad_keys = grad_keys + tn(grad_scores, part)
            GJ[m, :, columns(0, hp)] = (grad_query * scale).astype(BF16)
            GJ[m, :, columns(D, hp)] = (grad_keys * scale).astype(BF16)
            GJ[m, :, columns(2 * D, hp)] = grad_values.astype(BF16)
            return carry

        lax.fori_loop(0, D // pair, attend, 0)

    def backward_end(m):
        grad = None
        for cols, block in qkv.blocks():
            term = nt(GJ[m, :, cols], block)
            grad = term if grad is None else grad + term
        hat, rstd = normalize(XP[m].astype(F32))
        GR[NE : NE + 1] = GR[NE : NE + 1] + jnp.sum(grad * hat, axis=0, keepdims=True)
        full = GM[m] + normalize_back(grad * gain_one, hat, rstd)
        b["IG"][m, :, 0, :] = full[0:T]

    sums_now((1, 1, 0), (2, 0, 0))
    for m in range(M):
        exchanged(DXB, m, s_dx[m])
        exchanged(GCB, m, s_gc[m])
        backward_top(m)
        if m == 0:
            sums_now((1, 1, 1))
        if m == M - 1:
            proj.put(ATT[...].reshape(M * TP, D), N2)
            proj.sum_core()
            sums_now((1, 2, 1))
        backward_heads(m)
        if m == 0:
            sums_now((2, 0, 1), (2, 0, 2), (1, 1, 2), (2, 1, 0))
    sums_now((1, 2, 2))
    proj.sum_plane()
    qkv.put(N1[...].reshape(M * TP, D), GJ)
    GB, SB1, SB2, SB3, SB4 = (b[k] for k in ("GB", "SB1", "SB2", "SB3", "SB4"))
    qkv.sum_core()
    for m in range(M):
        backward_end(m)
    kept.append(fetch(b["IG"], igrad))
    GB[...] = GR[...].astype(BF16)
    r_b1 = one_send(GB, SB1, sibling)
    qkv.sum_plane()
    proj.sum_cross()
    arrived(SB1, r_b1)
    SB2[y] = GB[...] + SB1[...]
    s_b2, r_b2 = sends.take(G - 1) - 1, sems.take(G - 1) - 1
    for d in range(1, G):
        send(SB2.at[y], SB2.at[y], s_b2 + d, r_b2 + d, at(z, x, ((y + d) % G) * 2 + core))
        sent_later(s_b2 + d, SB2.at[y])
    sums_now((2, 1, 1), (2, 1, 2), (2, 2, 1), (1, 2, 0), (2, 2, 2))
    qkv.sum_cross()
    proj.sum_z()
    if nz == 4:

        @pl.when(at_end)
        def _():
            for k in first_ends:
                sums_end_in(k)

    for d in range(1, G):
        arrived(SB2.at[(y + G - d) % G], r_b2 + d)
    total = SB2[0].astype(F32)
    for j in range(1, G):
        total = total + SB2[j].astype(F32)
    SB3[x] = total.astype(BF16)
    r_b3 = one_send(SB3.at[x], SB3.at[x], across)
    sums_now((1, 3, 0), (1, 3, 1), (1, 3, 2), (2, 2, 0))
    qkv.sum_z()
    arrived(SB3.at[1 - x], r_b3)
    SB4[z] = SB3[0] + SB3[1]
    s_b4, r_b4 = sends.take(1), sems.take(1)
    for dz in orders:
        send(SB4.at[z], SB4.at[z], s_b4, r_b4, at((z + dz) % nz, x, e))
    sent_later(s_b4, SB4.at[0 : nz - 1])
    sums_begin(nz - 1, (2,))
    sums_rest()
    sums_end_out(False)
    if nz == 4:

        @pl.when(jnp.logical_not(at_end))
        def _():
            for k in (0, nz - 1):
                sums_end_in(k)

    proj.hand_out()
    qkv.hand_out()
    if nz == 4:

        @pl.when(at_end)
        def _():
            for k in last_ends:
                sums_end_in(k)

        @pl.when(jnp.logical_not(at_end))
        def _():
            for k in range(1, nz - 1):
                sums_end_in(k)

    else:
        for k in range(nz):
            sums_end_in(k)
    sums_end_out(True)
    for m in range(M):
        exchanged(YB, m, s_y[m])
        outputs(m)
    b["AO"][...] = b["AR"][...].astype(BF16)
    kept.append(fetch(b["AO"], act))
    arrived(SB4.at[0 : nz - 1], r_b4)
    total = SB4[0].astype(F32)
    for k in range(1, nz):
        total = total + SB4[k].astype(F32)
    mine = (
        lax.broadcasted_iota(jnp.int32, (D, RF), 0)
        == lax.broadcasted_iota(jnp.int32, (D, RF), 1) + f * RF
    ).astype(F32)
    b["GS"][...] = lax.dot_general(
        total,
        mine,
        (((1,), (0,)), ((), ())),
        precision=lax.Precision.HIGHEST,
        preferred_element_type=F32,
    )
    kept.append(fetch(b["GS"].at[0:NE], grouter))
    kept.append(fetch(b["GS"].at[NE : NE + 1], ggain1))
    kept.append(fetch(b["GS"].at[NE + 1 : NE + 2], ggain2))
    sums_close()
    proj.leave(gout)
    qkv.leave(gqkv)
    for cond, copy in pending:
        when(cond, copy.wait_send)
    for copy in kept:
        copy.wait()
    used = (sends.used, sems.used, locals_.used)
    assert all(a <= b for a, b in zip(used, counts)), (used, counts)


def hand_over(*refs):
    source, target, held, sem = refs[:9], refs[9:18], refs[18:-1], refs[-1]
    cast = [k for k in range(9) if source[k].dtype != target[k].dtype]
    order = sorted(range(9), key=lambda k: -math.prod(target[k].shape))
    for k in order:
        pltpu.make_async_copy(source[k], held[k], sem.at[0, k]).start()
    for k in order:
        pltpu.make_async_copy(source[k], held[k], sem.at[0, k]).wait()
        ready = held[k]
        if k in cast:
            ready = held[9 + cast.index(k)]
            ready[...] = held[k][...].astype(ready.dtype)
        pltpu.make_async_copy(ready, target[k], sem.at[1, k]).start()
    for k in order:
        pltpu.make_async_copy(target[k], target[k], sem.at[1, k]).wait()


def body(
    mesh_shape,
    inputs,
    gain_attn,
    qkv_weight,
    out_weight,
    gain_moe,
    router_weight,
    expert_in,
    expert_out,
    routes,
    cotangent,
):
    micro, images, seq, width = inputs.shape
    c = layout(mesh_shape, micro, images * seq, width, expert_in.shape[2])
    rows = images * seq
    scratch = scratch_of(c)
    names = list(scratch)
    nz, G = c["nz"], c["G"]
    counts = (48 + 11 * (G - 1), 25 + 20 * nz + 2 * nz * nz + (2 * nz + 9) * (G - 1), 19 + 2 * c["E"])
    shapes = (
        ((rows, micro, width), BF16),
        ((micro, rows, 1, width), F32),
        (qkv_weight.shape, F32),
        (out_weight.shape, F32),
        ((1, c["RF"]), F32),
        ((1, c["RF"]), F32),
        ((c["NE"], c["RF"]), F32),
        (expert_in.shape, F32),
        (expert_out.shape, F32),
    )
    shapes = [jax.ShapeDtypeStruct(s, t) for s, t in shapes]
    sums = (2, 3, 7, 8)
    halves = [
        jax.ShapeDtypeStruct(s.shape, BF16 if k in sums else s.dtype) for k, s in enumerate(shapes)
    ]
    anywhere = pl.BlockSpec(memory_space=pltpu.HBM)
    results = pl.pallas_call(
        functools.partial(kernel, c, names, counts),
        out_shape=halves,
        in_specs=[anywhere] * 10,
        out_specs=[anywhere] * 9,
        scratch_shapes=[pltpu.VMEM(s, t) for s, t in scratch.values()]
        + [pltpu.SemaphoreType.DMA((count,)) for count in counts],
        compiler_params=pltpu.CompilerParams(
            collective_id=0, has_side_effects=True, vmem_limit_bytes=60 * 1024 * 1024
        ),
    )(
        jnp.transpose(inputs, (1, 2, 0, 3)).reshape(rows, micro, width),
        jnp.transpose(cotangent, (1, 2, 0, 3)).reshape(rows, micro, width),
        jnp.transpose(routes, (0, 1, 3, 2)).reshape(micro, 2, rows),
        qkv_weight,
        out_weight,
        gain_attn[None, :],
        gain_moe[None, :],
        router_weight.T,
        expert_in,
        expert_out,
    )
    act, igrad, gqkv, gout, ggain1, ggain2, grouter, gein, geout = pl.pallas_call(
        hand_over,
        out_shape=shapes,
        in_specs=[anywhere] * 9,
        out_specs=[anywhere] * 9,
        scratch_shapes=[pltpu.VMEM(s.shape, s.dtype) for s in halves]
        + [pltpu.VMEM(shapes[k].shape, F32) for k in sums]
        + [pltpu.SemaphoreType.DMA((2, 9))],
        compiler_params=pltpu.CompilerParams(vmem_limit_bytes=60 * 1024 * 1024),
    )(*results)
    return (
        jnp.transpose(act.reshape(images, seq, micro, width), (2, 0, 1, 3)),
        igrad.reshape(inputs.shape),
        ggain1[0],
        gqkv,
        gout,
        ggain2[0],
        grouter.T,
        gein,
        geout,
    )


def solution(mesh):
    return jax.shard_map(
        functools.partial(body, dict(mesh.shape)),
        mesh=mesh,
        in_specs=(
            P(None, ("fsdp", "expert"), None, None),
            P("fsdp"),
            P("fsdp", None),
            P("fsdp", None),
            P("fsdp"),
            P("fsdp", None),
            P("expert", "fsdp", None),
            P("expert", "fsdp", None),
            P(None, ("fsdp", "expert"), None, None),
            P(None, ("fsdp", "expert"), None, None),
        ),
        out_specs=(
            P(None, ("fsdp", "expert"), None, None),
            P(None, ("fsdp", "expert"), None, None),
            P("fsdp"),
            P("fsdp", None),
            P("fsdp", None),
            P("fsdp"),
            P("fsdp", None),
            P("expert", "fsdp", None),
            P("expert", "fsdp", None),
        ),
        check_vma=False,
    )
```

```python
import functools
import math

import jax
import jax.numpy as jnp
from jax import lax
from jax.experimental import pallas as pl
from jax.experimental.pallas import tpu as pltpu
from jax.sharding import PartitionSpec as P

HEADS = 8
EPS = 1e-06
MESH = pl.DeviceIdType.MESH
F32 = jnp.float32
BF16 = jnp.bfloat16


def nn(a, b):
    return lax.dot_general(a, b, (((1,), (0,)), ((), ())), preferred_element_type=F32)


def nt(a, b):
    return lax.dot_general(a, b, (((1,), (1,)), ((), ())), preferred_element_type=F32)


def tn(a, b):
    return lax.dot_general(a, b, (((0,), (0,)), ((), ())), preferred_element_type=F32)


def normalize(values):
    center = jnp.mean(values, axis=-1, keepdims=True)
    shifted = values - center
    spread = jnp.mean(shifted * shifted, axis=-1, keepdims=True)
    rstd = lax.rsqrt(spread + EPS)
    return shifted * rstd, rstd


def normalize_back(grad, hat, rstd):
    return rstd * (
        grad
        - jnp.mean(grad, axis=-1, keepdims=True)
        - hat * jnp.mean(grad * hat, axis=-1, keepdims=True)
    )


class Semaphores:
    def __init__(self):
        self.used = 0

    def take(self, count):
        start = self.used
        self.used += count
        return start


SIZES = ("nz", "E", "G", "NE", "NR", "T", "TP", "CP", "S", "D", "FC", "RF", "CF", "M")


def layout(mesh_shape, micro, seq, width, ff_width):
    fsdp, peers = mesh_shape["fsdp"], mesh_shape["expert"]
    c = {}
    c["nz"] = fsdp // 2
    c["E"] = peers
    c["G"] = peers // 2
    c["NE"] = 2 * peers
    c["T"] = seq
    c["TP"] = -(-seq // 16) * 16
    c["CP"] = -(-max(2, 10 * seq // (4 * 2 * peers) + 1) // 16) * 16
    c["S"] = c["NE"] * c["CP"]
    c["NR"] = -(-(c["NE"] + 2) // 16) * 16
    c["D"] = width
    c["FF"] = ff_width
    c["RF"] = width // fsdp
    c["CF"] = ff_width // fsdp
    c["FC"] = 2 * c["CF"]
    c["WQ"] = 128 * -(-(3 * width // 128) // peers)
    c["WO"] = 128 * -(-(width // 128) // peers)
    c["M"] = micro
    return c


def scratch_of(c):
    nz, E, G, NE, NR, T, TP, CP, S, D, FC, RF, CF, M = (c[k] for k in SIZES)
    h = nz // 2
    v = {
        "XP": ((M, TP, D), BF16),
        "CT": ((M, TP, D), BF16),
        "XR": ((T, M, D), BF16),
        "CR": ((T, M, D), BF16),
        "AR": ((T, M, D), F32),
        "AO": ((T, M, D), BF16),
        "IG": ((M, T, 1, D), F32),
        "RR": ((M, 2, T), jnp.int32),
        "RT": ((M, TP, 128), F32),
        "SR": ((nz, 2, NR, RF), BF16),
        "G1": ((1, RF), BF16),
        "G2": ((1, RF), BF16),
        "RW": ((NE, RF), BF16),
        "GI": ((2, RF, nz * FC), BF16),
        "GT": ((2, CF, D), BF16),
        "GS": ((NR, RF), F32),
        "SM": ((nz, 2, RF, 128), BF16),
        "WIN": ((nz, nz, 2, RF, FC), BF16),
        "WOUT": ((nz, 2, CF, D), BF16),
        "N1": ((M, TP, D), BF16),
        "J": ((M, TP, 3 * D), BF16),
        "ATT": ((M, TP, D), BF16),
        "MID": ((M, TP, D), F32),
        "N2": ((M, TP, D), BF16),
        "GATES": ((M, TP, 128), F32),
        "PM": ((M, 2, TP, S), BF16),
        "XS": ((M, NE, CP, D), BF16),
        "XB": ((M, NE, CP, D), BF16),
        "GSS": ((M, NE, CP, D), BF16),
        "GRB": ((M, NE, CP, D), BF16),
        "CSS": ((M, NE, 8, 128), F32),
        "CSB": ((M, NE, 8, 128), F32),
        "CROW": ((8, S), F32),
        "GC": ((M, S, D), BF16),
        "YS": ((M, NE, CP, D), BF16),
        "YB": ((M, NE, CP, D), BF16),
        "DXS": ((M, NE, CP, D), BF16),
        "DXB": ((M, NE, CP, D), BF16),
        "GCS": ((M, NE, 8, 128), F32),
        "GCB": ((M, NE, 8, 128), F32),
        "YACC": ((M, S, D), F32),
        "DXACC": ((M, S, D), F32),
        "AS": ((M, S, FC), BF16),
        "GHS": ((M, S, FC), BF16),
        "DWI": ((nz, nz, 2, RF, FC), BF16),
        "DWO": ((nz, 2, CF, D), BF16),
        "UPI": ((nz, nz, 2, RF, FC), BF16),
        "UPO": ((nz, 2, CF, D), BF16),
        "DNI": ((nz, nz, 2, RF, FC), BF16),
        "DNO": ((nz, 2, CF, D), BF16),
        "FXI": ((nz, RF, FC), BF16),
        "FXO": ((CF, D), BF16),
        "GM": ((M, TP, D), F32),
        "GA": ((M, TP, D), BF16),
        "GJ": ((M, TP, 3 * D), BF16),
        "GR": ((NR, D), F32),
        "GB": ((NR, D), BF16),
        "SB1": ((NR, D), BF16),
        "SB2": ((G, NR, D), BF16),
        "SB3": ((2, NR, D), BF16),
        "SB4": ((nz, NR, D), BF16),
    }
    for name, wide in (("Q", c["WQ"]), ("O", c["WO"])):
        for part, lead in (
            ("W", (E, nz, 2)),
            ("G", (E, nz, 2)),
            ("B1", (G, nz, 2)),
            ("Y1", (G, h, 2)),
            ("X1", (G, nz - h)),
            ("X2", (h,)),
            ("Y2", (G, nz - h)),
            ("Z", (nz,)),
            ("F", (E,)),
        ):
            v[name + part] = (lead + (RF, wide), BF16)
    return v


def kernel(c, names, counts, *refs):
    nz, E, G, NE, NR, T, TP, CP, S, D, FC, RF, CF, M = (c[k] for k in SIZES)
    (xin, cot, routes, qkv_s, out_s, gain1, gain2, router, ein, eout) = refs[:10]
    (act, igrad, gqkv, gout, ggain1, ggain2, grouter, gein, geout) = refs[10:19]
    b = dict(zip(names, refs[19:]))
    SS, RS, LS = refs[-3:]
    h = nz // 2
    head = D // HEADS
    pair = 2 * head
    scale = 1.0 / math.sqrt(head)
    sems, sends, locals_ = Semaphores(), Semaphores(), Semaphores()
    pending = []

    f = lax.axis_index("fsdp")
    e = lax.axis_index("expert")
    z, x = f // 2, f % 2
    y, core = e // 2, e % 2
    pme = 2 * e + x

    def at(zz, xx, ee):
        return (zz * 2 + xx, ee)

    sibling = at(z, x, y * 2 + (1 - core))
    across = at(z, 1 - x, e)

    def copy_of(src, dst, ssem, rsem, device):
        return pltpu.make_async_remote_copy(
            src_ref=src,
            dst_ref=dst,
            send_sem=SS.at[ssem],
            recv_sem=RS.at[rsem],
            device_id=device,
            device_id_type=MESH,
        )

    def when(cond, run):
        if cond is None:
            run()
        else:
            pl.when(cond)(run)

    def send(src, dst, ssem, rsem, device, cond=None):
        when(cond, copy_of(src, dst, ssem, rsem, device).start)

    def arrived(dst, rsem, cond=None):
        when(cond, copy_of(dst, dst, 0, rsem, sibling).wait_recv)

    def sent_later(ssem, src, cond=None):
        pending.append((cond, copy_of(src, src, ssem, 0, sibling)))

    def one_send(src, dst, device):
        ssem, rsem = sends.take(1), sems.take(1)
        send(src, dst, ssem, rsem, device)
        sent_later(ssem, src)
        return rsem

    barrier = pltpu.get_barrier_semaphore()
    for dz in range(1, nz):
        pl.semaphore_signal(
            barrier, inc=1, device_id=at((z + dz) % nz, x, e), device_id_type=MESH
        )

    def greet(d, carry):
        p = (pme + d) % NE
        pl.semaphore_signal(barrier, inc=1, device_id=at(z, p % 2, p // 2), device_id_type=MESH)
        return carry

    lax.fori_loop(1, NE, greet, 0)

    SM, WIN, WOUT = b["SM"], b["WIN"], b["WOUT"]
    UP, DN = (b["UPI"], b["UPO"]), (b["DNI"], b["DNO"])

    def fetch(src, dst):
        copy = pltpu.make_async_copy(src, dst, LS.at[locals_.take(1)])
        copy.start()
        return copy

    far_first = [d for k in range(1, nz) for d in (k, nz - k) if 2 * k <= nz]
    orders = list(dict.fromkeys(far_first))

    class Dense:
        def __init__(self, name, shard, wide):
            self.name, self.shard, self.wide = name, shard, wide
            self.w, self.g = b[name + "W"], b[name + "G"]
            self.used = -(-shard.shape[1] // wide)
            self.own = locals_.take(1)
            for k in range(self.used):

                @pl.when(e == k)
                def _():
                    pltpu.make_async_copy(
                        self.columns(shard, k), self.w.at[k, z, x], LS.at[self.own]
                    ).start()

        def columns(self, ref, k):
            return ref.at[:, k * self.wide : (k + 1) * self.wide]

        def own_ready(self):
            copy = pltpu.make_async_copy(
                self.w.at[e, z, x], self.w.at[e, z, x], LS.at[self.own]
            )
            when(None if self.used == E else e < self.used, copy.wait)

        def along_z(self):
            w = self.w
            self.r_z, s_z = sems.take(nz - 1) - 1, sends.take(1)
            for dz in orders:
                to = at((z + dz) % nz, x, e)
                send(w.at[e, z, x], w.at[e, z, x], s_z, self.r_z + dz, to)
            sent_later(s_z, w.at[e, 0 : nz - 1, x])
            self.s_x, self.r_x = sends.take(1), sems.take(nz)
            self.s_y, self.r_y = sends.take(G - 1) - 1, sems.take(G - 1) - 1
            self.s_c, self.r_c = sends.take(1), sems.take(1)
            sent_later(self.s_x, w.at[e, :, x])
            for d in range(1, G):
                sent_later(self.s_y + d, w.at[e, :, x])
            sent_later(self.s_c, w.at[0:G])

        def spread(self, dz):
            zz = (z + nz - dz) % nz
            piece = self.w.at[e, zz, x]
            if dz > 0:
                arrived(piece, self.r_z + dz)
            send(piece, piece, self.s_x, self.r_x + dz, across)
            for d in range(1, G):
                to = at(z, x, ((y + d) % G) * 2 + core)
                send(piece, piece, self.s_y + d, self.r_y + d, to)
            send(piece, piece, self.s_c, self.r_c, sibling)

        def forward(self):
            w = self.w
            self.s_xy, self.r_xy = sends.take(G - 1) - 1, sems.take(G - 1) - 1
            for d in range(1, G):
                sent_later(self.s_xy + d, w.at[e, :, x])
            for dz in [0] + orders:
                piece = w.at[e, (z + nz - dz) % nz, 1 - x]
                arrived(piece, self.r_x + dz)
                for d in range(1, G):
                    to = at(z, x, ((y + d) % G) * 2 + core)
                    send(piece, piece, self.s_xy + d, self.r_xy + d, to)
                send(piece, piece, self.s_c, self.r_c, sibling)

        def corner(self):
            w = self.w
            for d in range(1, G):
                ee = ((y + G - d) % G) * 2 + core
                arrived(w.at[ee, :, x], self.r_y + d)
                send(w.at[ee, :, x], w.at[ee, :, x], self.s_c, self.r_c, sibling)
                arrived(w.at[ee, :, 1 - x], self.r_xy + d)
                send(w.at[ee, :, 1 - x], w.at[ee, :, 1 - x], self.s_c, self.r_c, sibling)

        def ready(self):
            arrived(self.w.at[0:G], self.r_c)

        def blocks(self):
            for k in range(self.used):
                cols = slice(k * self.wide, min((k + 1) * self.wide, self.shard.shape[1]))
                yield cols, self.w[k].reshape(D, self.wide)

        def put(self, left, right):
            for k in range(self.used):
                cols = slice(k * self.wide, (k + 1) * self.wide)
                part = tn(left, right[:, :, cols].reshape(M * TP, self.wide))
                self.g[k] = part.astype(BF16).reshape(nz, 2, RF, self.wide)

        def sum_core(self):
            s, self.r_1 = sends.take(1), sems.take(1)
            for j in range(G):
                send(self.g.at[2 * j + 1 - core], b[self.name + "B1"].at[j], s, self.r_1, sibling)
            sent_later(s, b[self.name + "B1"])

        def sum_plane(self):
            g, first = self.g, b[self.name + "B1"]
            arrived(first, self.r_1)
            for j in range(G):
                g[2 * j + core] = g[2 * j + core] + first[j]
            s, self.r_y1 = sends.take(G - 1) - 1, sems.take(G - 1) - 1
            for d in range(1, G):
                q = (y + d) % G
                piece = g.at[2 * q + core, 0:h]
                send(piece, b[self.name + "Y1"].at[y], s + d, self.r_y1 + d, at(z, x, 2 * q + core))
                sent_later(s + d, piece)
            s, self.r_x1 = sends.take(1), sems.take(1)
            for j in range(G):
                piece = g.at[2 * j + core, h:nz, 1 - x]
                send(piece, b[self.name + "X1"].at[j], s, self.r_x1, across)
            sent_later(s, b[self.name + "X1"])

        def sum_cross(self):
            g, from_y, from_x = self.g, b[self.name + "Y1"], b[self.name + "X1"]
            for d in range(1, G):
                q = (y + G - d) % G
                arrived(from_y.at[q], self.r_y1 + d)
                g[e, 0:h] = g[e, 0:h] + from_y[q]
            self.r_x2 = one_send(g.at[e, 0:h, 1 - x], b[self.name + "X2"], across)
            arrived(from_x, self.r_x1)
            for j in range(G):
                g[2 * j + core, h:nz, x] = g[2 * j + core, h:nz, x] + from_x[j]
            s, self.r_y2 = sends.take(G - 1) - 1, sems.take(G - 1) - 1
            for d in range(1, G):
                q = (y + d) % G
                piece = g.at[2 * q + core, h:nz, x]
                send(piece, b[self.name + "Y2"].at[y], s + d, self.r_y2 + d, at(z, x, 2 * q + core))
                sent_later(s + d, piece)

        def sum_z(self):
            g, from_x, from_y = self.g, b[self.name + "X2"], b[self.name + "Y2"]
            arrived(from_x, self.r_x2)
            g[e, 0:h, x] = g[e, 0:h, x] + from_x[...]
            for d in range(1, G):
                q = (y + G - d) % G
                arrived(from_y.at[q], self.r_y2 + d)
                g[e, h:nz, x] = g[e, h:nz, x] + from_y[q]
            s, self.r_z2 = sends.take(1), sems.take(1)
            parts = b[self.name + "Z"]
            for dz in orders:
                zz = (z + dz) % nz
                send(g.at[e, zz, x], parts.at[z], s, self.r_z2, at(zz, x, e))
            sent_later(s, parts.at[0 : nz - 1])
            parts[z] = g[e, z, x]

        def hand_out(self):
            parts, done = b[self.name + "Z"], b[self.name + "F"]
            arrived(parts.at[0 : nz - 1], self.r_z2)
            total = parts[0].astype(F32)
            for k in range(1, nz):
                total = total + parts[k].astype(F32)
            done[e] = total.astype(BF16)
            s, self.r_f = sends.take(1), sems.take(1)

            def one(d, carry):
                send(done.at[e], done.at[e], s, self.r_f, at(z, x, (e + d) % E))
                return carry

            lax.fori_loop(1, E, one, 0)
            sent_later(s, done.at[0 : E - 1])

        def leave(self, out):
            done = b[self.name + "F"]
            arrived(done.at[0 : E - 1], self.r_f)
            for k in range(self.used):
                kept.append(fetch(done.at[k], self.columns(out, k)))

    qkv, proj = Dense("Q", qkv_s, c["WQ"]), Dense("O", out_s, c["WO"])
    kept = []

    SR = b["SR"]
    SR[z, x] = jnp.zeros((NR, RF), BF16)
    small_in = [
        fetch(gain1, b["G1"]),
        fetch(gain2, b["G2"]),
        fetch(router, b["RW"]),
    ]
    token_in = [fetch(routes, b["RR"]), fetch(xin, b["XR"]), fetch(cot, b["CR"])]
    own_in = locals_.take(1)
    for k in range(nz):
        pltpu.make_async_copy(
            ein.at[x, :, k * FC : (k + 1) * FC], WIN.at[k, z, x], LS.at[own_in]
        ).start()
    own_out = fetch(eout.at[x], WOUT.at[z, x])

    for copy in small_in:
        copy.wait()
    SR[z, x, 0:NE] = b["RW"][...]
    SR[z, x, NE : NE + 1] = b["G1"][...]
    SR[z, x, NE + 1 : NE + 2] = b["G2"][...]
    entry = lax.broadcasted_iota(jnp.int32, (NR, 128), 0)
    place = lax.broadcasted_iota(jnp.int32, (NR, 128), 1)
    pick = (
        ((entry < NE) & (entry == place))
        | ((entry >= NE) & (entry < NE + 2) & (place == entry - NE + 126))
    ).astype(BF16)
    qkv.own_ready()
    proj.own_ready()
    pl.semaphore_wait(barrier, nz - 1 + NE - 1)

    qkv.along_z()
    r_sz, s_sz = sems.take(1), sends.take(1)
    for dz in orders:
        send(SR.at[z, x], SR.at[z, x], s_sz, r_sz, at((z + dz) % nz, x, e))
    sent_later(s_sz, SR.at[0 : nz - 1, x])
    qkv.spread(0)

    s_xi, r_xi = sends.take(1), sems.take(1)
    for k in range(nz):
        send(ein.at[1 - x, :, k * FC : (k + 1) * FC], WIN.at[k, z, x], s_xi, r_xi, across)
    sent_later(s_xi, WIN.at[:, z, x])


    XP, CT, RT, PM = b["XP"], b["CT"], b["RT"], b["PM"]

    @pl.when(z == 0)
    def _():
        UP[0][:, 0] = jnp.zeros((nz, 2, RF, FC), BF16)
        UP[1][0] = jnp.zeros((2, CF, D), BF16)

    @pl.when(z == nz - 1)
    def _():
        DN[0][:, nz - 1] = jnp.zeros((nz, 2, RF, FC), BF16)
        DN[1][nz - 1] = jnp.zeros((2, CF, D), BF16)

    for copy in token_in:
        copy.wait()
    lane = lax.broadcasted_iota(jnp.int32, (TP, 128), 1)
    lane_f = lane.astype(F32)
    swap = (
        lax.broadcasted_iota(jnp.int32, (2, 128), 0) == lax.broadcasted_iota(jnp.int32, (2, 128), 1)
    ).astype(BF16)
    for m in range(M):
        XP[m] = jnp.zeros((TP, D), BF16)
        CT[m] = jnp.zeros((TP, D), BF16)
        RT[m] = jnp.full((TP, 128), -1.0, F32)
        XP[m, 0:T] = b["XR"][:, m, :]
        CT[m, 0:T] = b["CR"][:, m, :]
        RT[m, 0:T] = tn(b["RR"][m].astype(BF16), swap)

    def onehot(m, j):
        return RT[m][:, j : j + 1] == lane_f

    before = (
        lax.broadcasted_iota(jnp.int32, (TP, TP), 1) < lax.broadcasted_iota(jnp.int32, (TP, TP), 0)
    ).astype(BF16)
    spots = lax.broadcasted_iota(jnp.int32, (TP, S), 1).astype(F32)
    for m in range(M):
        first = onehot(m, 0).astype(F32)
        second = onehot(m, 1).astype(F32)
        rank0 = nn(before, first.astype(BF16))
        rank1 = nn(before, second.astype(BF16)) + jnp.sum(first, axis=0, keepdims=True)
        for j, (hot, rank) in enumerate(((first, rank0), (second, rank1))):
            slot = jnp.sum(hot * rank, axis=-1, keepdims=True)
            route = RT[m][:, j : j + 1]
            spot = jnp.where(route >= 0, route * CP + slot, -1.0)
            PM[m, j] = (spots == spot).astype(BF16)

    def turn_of(i):
        return 0 if i == 0 else i % (nz - 1) + 1

    groups = (range(0, 2), range(2, nz))
    s_zi = [[sends.take(1) for _ in groups] for _ in range(2)]
    s_zo = [sends.take(1) for _ in range(2)]
    r_zi = [[sems.take(nz) for _ in groups] for _ in range(2)]
    r_zo = [sems.take(2 * nz) for _ in range(2)]
    for zz in range(nz):
        for side in range(2):
            count = zz + 1 if side == 0 else nz - zz
            if count < nz:
                for g, turns in enumerate(groups):
                    sent_later(s_zi[side][g], WIN.at[0 : len(turns), 0:count], z == zz)
                sent_later(s_zo[side], WOUT.at[0:count], z == zz)

    def reach(side, d, some=None):
        begun = z - d if side == 0 else z + d
        there = (begun >= 0) if side == 0 else (begun < nz)
        last = (z == nz - 1) if side == 0 else (z == 0)
        if some is not None:
            there = there & some(begun)
        return begun, there, there & jnp.logical_not(last)

    def onward(side):
        return at((z + 1) % nz if side == 0 else (z + nz - 1) % nz, x, e)

    def pass_in(g, d, halves=(0, 1)):
        for side in range(2):
            begun, there, goes = reach(side, d)
            r = r_zi[side][g]
            if d > 0:
                arrived(WIN.at[0 : len(groups[g]), begun], r + d, there)
            if d < nz - 1:

                @pl.when(goes)
                def _():
                    for i in groups[g]:
                        k = turn_of(i) if side == 1 else nz - 1 - turn_of(i)
                        for half in halves:
                            piece = WIN.at[k, begun, x if half == 0 else 1 - x]
                            send(piece, piece, s_zi[side][g], r + d + 1, onward(side))

    def pass_out(d, half, late=None):
        xx = x if half == 0 else 1 - x
        for side in range(2):
            odd = nz - 2 if side == 0 else 1
            some = None
            if late is not None:
                some = (lambda begun: begun == odd) if late else (lambda begun: begun != odd)
            begun, there, goes = reach(side, d, some)
            r = r_zo[side] + 2 * d + half
            piece = WOUT.at[begun, xx]
            if d > 0:
                arrived(piece, r, there)
            if d < nz - 1:
                send(piece, piece, s_zo[side], r + 2, onward(side), goes)

    early, others = 0, 1
    GATES, XS, XB, GC, CROW = (b[k] for k in ("GATES", "XS", "XB", "GC", "CROW"))
    GSS, GRB, CSS, CSB = (b[k] for k in ("GSS", "GRB", "CSS", "CSB"))
    GCS, GCB, YS, YB, DXS, DXB = (b[k] for k in ("GCS", "GCB", "YS", "YB", "DXS", "DXB"))

    def exchange(src, dst, m, sem):
        rows = slice(0, 1 if src.shape[2] == 8 else src.shape[2])

        def one(d, carry):
            p = (pme + d) % NE
            send(src.at[m, p, rows], dst.at[m, pme, rows], *sem, at(z, p % 2, p // 2))
            return carry

        lax.fori_loop(1, NE, one, 0)
        sent_later(sem[0], src.at[m, 0 : NE - 1, rows])
        dst[m, pme] = src[m, pme]

    def exchanged(dst, m, sem):
        rows = slice(0, 1 if dst.shape[2] == 8 else dst.shape[2])
        arrived(dst.at[m, 0 : NE - 1, rows], sem[1])

    def pairs():
        return [(sends.take(1), sems.take(1)) for _ in range(M)]

    s_x, s_cs, s_gr, s_dx, s_gc, s_y = (pairs() for _ in range(6))
    for m in range(M):
        GSS[m] = tn(PM[m, 0] + PM[m, 1], CT[m]).astype(BF16).reshape(NE, CP, D)

    for dz in orders[:2]:
        qkv.spread(dz)
    proj.along_z()
    proj.spread(0)
    pltpu.make_async_copy(WIN.at[:, z, x], WIN.at[:, z, x], LS.at[own_in]).wait()
    pass_in(early, 0, (0,))
    for dz in orders[2:]:
        qkv.spread(dz)
    arrived(SR.at[0 : nz - 1, x], r_sz)
    r_sx = one_send(SR.at[:, x], SR.at[:, x], across)
    own_out.wait()
    pass_out(0, 0)
    arrived(WIN.at[:, z, 1 - x], r_xi)
    pass_in(early, 0, (1,))
    qkv.forward()
    for dz in orders:
        proj.spread(dz)
    proj.forward()
    r_xo = one_send(eout.at[1 - x], WOUT.at[z, x], across)
    for m in range(M):
        exchange(GSS, GRB, m, s_gr[m])
    pass_in(others, 0, (0,))
    arrived(SR.at[:, 1 - x], r_sx)
    for zz in range(nz):
        for xx in range(2):
            SM[zz, xx] = tn(SR[zz, xx], pick).astype(BF16)
    qkv.corner()
    qkv.ready()

    small = SM[...].reshape(D, 128)
    gains = nt(pick, small)
    gain_one, gain_two = gains[NE : NE + 1], gains[NE + 1 : NE + 2]
    key_ok = lax.broadcasted_iota(jnp.int32, (1, TP), 1) < T
    low_half = lax.broadcasted_iota(jnp.int32, (1, pair), 1) < head
    N1, J, ATT, MID, N2 = b["N1"], b["J"], b["ATT"], b["MID"], b["N2"]
    def half_of(value, i):
        keep = low_half if i == 0 else jnp.logical_not(low_half)
        return jnp.where(keep, value, jnp.zeros_like(value))

    def softmax_scores(query, keys):
        scores = jnp.where(key_ok, nt(query, keys) * scale, -1e30)
        raised = jnp.exp(scores - jnp.max(scores, axis=-1, keepdims=True))
        return raised * (1.0 / jnp.sum(raised, axis=-1, keepdims=True))

    def columns(base, hp):
        return pl.ds(pl.multiple_of(base + hp * pair, 128), pair)

    def chosen_of(m, j):
        gates = GATES[m]
        return jnp.sum(jnp.where(onehot(m, j), gates, 0.0), axis=-1, keepdims=True)

    def forward(m):
        tokens = XP[m].astype(F32)
        hat, _ = normalize(tokens)
        N1[m] = (hat * gain_one).astype(BF16)
        for cols, block in qkv.blocks():
            J[m, :, cols] = nn(N1[m], block).astype(BF16)

        def attend(hp, carry):
            query, keys, values = (J[m, :, columns(i * D, hp)] for i in range(3))
            total = jnp.zeros((TP, pair), F32)
            for i in range(2):
                probs = softmax_scores(half_of(query, i), keys).astype(BF16)
                total = total + nn(probs, half_of(values, i))
            ATT[m, :, columns(0, hp)] = total.astype(BF16)
            return carry

        lax.fori_loop(0, D // pair, attend, 0)
        if m == 0:
            pass_in(early, 1)
            pass_in(others, 0, (1,))
            proj.corner()
            proj.ready()
        for cols, block in proj.blocks():
            MID[m, :, cols] = XP[m, :, cols].astype(F32) + nn(ATT[m], block)
        hat, _ = normalize(MID[m])
        N2[m] = (hat * gain_two).astype(BF16)
        logits = jnp.where(lane < NE, nn(N2[m], small), -1e30)
        raised = jnp.exp(logits - jnp.max(logits, axis=-1, keepdims=True))
        GATES[m] = raised / jnp.sum(raised, axis=-1, keepdims=True)
        XS[m] = tn(PM[m, 0] + PM[m, 1], N2[m]).astype(BF16).reshape(NE, CP, D)
        weight = PM[m, 0].astype(F32) * chosen_of(m, 0) + PM[m, 1].astype(F32) * chosen_of(m, 1)
        CROW[0:1] = jnp.sum(weight, axis=0, keepdims=True)
        for k in range(NE):
            CSS[m, k, 0:1, 0:CP] = CROW[0:1, k * CP : (k + 1) * CP]

    diagonal = lax.broadcasted_iota(jnp.int32, (CP, 128), 0) == lax.broadcasted_iota(
        jnp.int32, (CP, 128), 1
    )

    def scale_grads(m):
        for p in range(NE):
            by_lane = CSB[m, p, 0:1]
            weight = jnp.sum(jnp.where(diagonal, by_lane, 0.0), axis=1, keepdims=True)
            GC[m, p * CP : (p + 1) * CP] = (weight * GRB[m, p].astype(F32)).astype(BF16)

    for m in range(M):
        forward(m)
        exchange(XS, XB, m, s_x[m])
        exchange(CSS, CSB, m, s_cs[m])
        if m == 0:
            arrived(WOUT.at[z, 1 - x], r_xo)
            pass_out(0, 1, False)
    pass_in(early, 2)
    pass_out(1, 0)
    for d in range(3, nz):
        pass_in(early, d)
    pass_out(1, 1, False)
    pass_in(others, 1)

    YACC, DXACC, AS, GHS = b["YACC"], b["DXACC"], b["AS"], b["GHS"]
    DWI, DWO = b["DWI"], b["DWO"]
    YACC[...] = jnp.zeros_like(YACC)
    DXACC[...] = jnp.zeros_like(DXACC)
    c0, c1 = math.sqrt(2.0 / math.pi), 0.044715

    OWN = (DWI, DWO)
    s_up = [(sends.take(1), sends.take(1)) for _ in range(2)]
    r_up = [(sems.take(nz * nz), sems.take(2 * nz)) for _ in range(2)]

    def expert_part(k, m, loop=True):
        def half(xx, carry):
            cols = pl.ds(pl.multiple_of(xx * CF, 128), CF)
            w_in = WIN[k, :, :, :, cols].reshape(D, CF)
            w_out = WOUT[k, xx]
            hidden = nn(XB[m].reshape(S, D), w_in)
            grad_acted = nt(GC[m], w_out)
            square = hidden * hidden
            bent = jnp.tanh(c0 * hidden * (1.0 + c1 * square))
            acted = (0.5 * hidden * (1.0 + bent)).astype(BF16)
            slope = 0.5 * (1.0 + bent) + 0.5 * c0 * hidden * (1.0 - bent * bent) * (
                1.0 + 3.0 * c1 * square
            )
            grad_hidden = (grad_acted * slope).astype(BF16)
            AS[m, :, cols] = acted
            GHS[m, :, cols] = grad_hidden
            YACC[m] = YACC[m] + nn(acted, w_out)
            DXACC[m] = DXACC[m] + nt(grad_hidden, w_in)
            return carry

        if loop:
            lax.fori_loop(0, 2, half, 0)
        else:
            half(0, 0)
            half(1, 0)

    def expert_weights(k):
        def half(xx, carry):
            cols = pl.ds(pl.multiple_of(xx * CF, 128), CF)
            grads = GC[...].reshape(M * S, D)
            tokens = XB[...].reshape(M * S, D)
            DWO[k, xx] = tn(AS[:, :, cols].reshape(M * S, CF), grads).astype(BF16)
            DWI[k, :, :, :, cols] = (
                tn(tokens, GHS[:, :, cols].reshape(M * S, CF))
                .astype(BF16)
                .reshape(nz, 2, RF, CF)
            )
            return carry

        lax.fori_loop(0, 2, half, 0)

    def sum_step(side, i, begins, parts):
        far = z if side == 0 else nz - 1 - z
        GOT = UP if side == 0 else DN
        turn = ((i % (nz - 1)) + 1) * jnp.minimum(i, 1)
        k = turn if side == 0 else nz - 1 - turn

        def tokens_side(j, carry):
            goal = nz - 1 - j
            t = goal if side == 0 else nz - 1 - goal
            rsem = r_up[side][0] + k * nz + t

            @pl.when(goal > far)
            def _():
                if not begins:
                    arrived(GOT[0].at[k, t], rsem)
                    DWI[k, t] = DWI[k, t] + GOT[0][k, t]
                send(DWI.at[k, t], GOT[0].at[k, t], s_up[side][0], rsem, onward(side))

            return carry

        def results_side():
            for xx in [xx for part, xx in ((1, 1 - x), (2, x)) if part in parts]:
                rsem = r_up[side][1] + 2 * k + xx
                if not begins:
                    arrived(GOT[1].at[k, xx], rsem)
                    DWO[k, xx] = DWO[k, xx] + GOT[1][k, xx]
                send(DWO.at[k, xx], GOT[1].at[k, xx], s_up[side][1], rsem, onward(side))

        if parts != (0,):
            pl.when(turn == nz - 1)(results_side)
        if 0 in parts:
            lax.fori_loop(0, nz - 1, tokens_side, 0)
        if parts != (0,):
            pl.when((turn > far) & (turn < nz - 1))(results_side)

    def sums_begin(i, parts=(0, 1, 2)):
        for side in range(2):
            far = z if side == 0 else nz - 1 - z
            step = functools.partial(sum_step, side, jnp.int32(i), True, parts)
            pl.when(far == 0)(step)

    def sums_pass(far_at, i, parts=(0, 1, 2)):
        for side in range(2):
            far = z if side == 0 else nz - 1 - z
            step = functools.partial(sum_step, side, jnp.int32(i), False, parts)
            pl.when(far == far_at)(step)

    passes = [(far, i, part) for far in range(1, nz - 1) for i in range(nz) for part in range(3)]

    def sums_now(*wanted):
        for step in wanted:
            if step in passes:
                passes.remove(step)
                sums_pass(step[0], step[1], (step[2],))

    def sums_rest():
        for far in range(1, nz - 1):
            left = [step for step in passes if step[0] == far]
            if nz <= 4:
                for _, i, part in left:
                    sums_pass(far, i, (part,))
            else:

                def one(i, carry, far=far):
                    sums_pass(far, i)
                    return carry

                lax.fori_loop(left[0][1], nz, one, 0)

    for zz in range(nz):
        for side in range(2):
            count = nz - 1 - zz if side == 0 else zz
            if count > 0:
                sent_later(s_up[side][0], DWI.at[:, 0:count], z == zz)
                sent_later(s_up[side][1], DWO.at[0:count], z == zz)

    def give_back(m):
        DXS[m] = DXACC[m].astype(BF16).reshape(NE, CP, D)
        exchange(DXS, DXB, m, s_dx[m])
        results = YACC[m].astype(BF16)
        YS[m] = results.reshape(NE, CP, D)
        for p in range(NE):
            rows = slice(p * CP, (p + 1) * CP)
            weight = jnp.sum(
                results[rows].astype(F32) * GRB[m, p].astype(F32), axis=1, keepdims=True
            )
            GCS[m, p, 0:1] = jnp.sum(jnp.where(diagonal, weight, 0.0), axis=0, keepdims=True)
        exchange(GCS, GCB, m, s_gc[m])

    when_two, when_far, when_late = (1, 2, nz - 1) if nz <= 4 else (0, 0, 0)
    for i in range(nz):
        if i == when_two:
            pass_out(2, 0)
            pass_out(2, 1, False)
        if i == when_far:
            pass_in(others, 2)
            pass_out(0, 1, True)
            for d in range(3, nz):
                pass_in(others, d)
                pass_out(d, 0)
                pass_out(d, 1, False)
        if i == when_late:
            for d in range(1, nz):
                pass_out(d, 1, True)
            sums_now((1, 0, 0), (1, 0, 1), (1, 0, 2))
        block = turn_of(i) + (z // h) * (nz - 1 - 2 * turn_of(i))
        for m in range(M):
            if i == 0:
                exchanged(GRB, m, s_gr[m])
                exchanged(XB, m, s_x[m])
                exchanged(CSB, m, s_cs[m])
                scale_grads(m)
            expert_part(block, m, i == 1)
            if i == nz - 1:
                give_back(m)
        if i == nz - 1:
            for m in range(M):
                exchange(YS, YB, m, s_y[m])
        expert_weights(block)
        sums_begin(i)

    r_fin, s_fin = (sems.take(nz), sems.take(1)), (sends.take(1), sends.take(1))
    FX = (b["FXI"], b["FXO"])
    GI, GT = b["GI"], b["GT"]
    sent_later(s_fin[0], FX[0])
    sent_later(s_fin[1], FX[1])

    def total_of(kind, place):
        return (
            OWN[kind][place].astype(F32)
            + UP[kind][place].astype(F32)
            + DN[kind][place].astype(F32)
        )

    def sums_end_in(k):
        cols = pl.ds(pl.multiple_of(k * FC, 128), FC)
        for side, ref, ok in ((0, UP, z > 0), (1, DN, z < nz - 1)):
            arrived(ref[0].at[k, z], r_up[side][0] + k * nz + z, ok)
        FX[0][k] = total_of(0, (k, z, 1 - x)).astype(BF16)
        send(FX[0].at[k], GI.at[x, :, cols], s_fin[0], r_fin[0] + k, across)
        GI[x, :, cols] = total_of(0, (k, z, x)).astype(BF16)

    def sums_end_out(mine):
        xx = x if mine else 1 - x
        for side, ref, ok in ((0, UP, z > 0), (1, DN, z < nz - 1)):
            arrived(ref[1].at[z, xx], r_up[side][1] + 2 * z + xx, ok)
        if mine:
            GT[x] = total_of(1, (z, xx)).astype(BF16)
        else:
            FX[1][...] = total_of(1, (z, xx)).astype(BF16)
            send(FX[1], GT.at[x], s_fin[1], r_fin[1], across)

    at_end = (z == 0) | (z == nz - 1)
    upper = z // h
    first_ends = [nz - 1 - upper * (nz - 1), 1 + upper * (nz - 3)]
    last_ends = [upper * (nz - 1), 2 - upper * (5 - nz)] if nz == 4 else []

    def sums_close():
        kept.append(fetch(GI.at[x], gein.at[x]))
        kept.append(fetch(GT.at[x], geout.at[x]))
        arrived(GT.at[1 - x], r_fin[1])
        kept.append(fetch(GT.at[1 - x], geout.at[1 - x]))
        for k in range(nz):
            arrived(GI.at[1 - x, :, k * FC : (k + 1) * FC], r_fin[0] + k)
        kept.append(fetch(GI.at[1 - x], gein.at[1 - x]))

    GM, GA, GJ, GR = b["GM"], b["GA"], b["GJ"], b["GR"]
    GR[...] = jnp.zeros_like(GR)

    def outputs(m):
        results = YB[m].reshape(S, D)
        out = MID[m] + chosen_of(m, 0) * nn(PM[m, 0], results)
        b["AR"][:, m, :] = (out + chosen_of(m, 1) * nn(PM[m, 1], results))[0:T]

    def backward_top(m):
        upstream = CT[m].astype(F32)
        for k in range(NE):
            CROW[0:1, k * CP : (k + 1) * CP] = GCB[m, k, 0:1, 0:CP]

        def grad_chosen(j):
            return jnp.sum(PM[m, j].astype(F32) * CROW[0:1], axis=-1, keepdims=True)

        gates = GATES[m]
        grad_gates = jnp.where(onehot(m, 0), grad_chosen(0), 0.0) + jnp.where(
            onehot(m, 1), grad_chosen(1), 0.0
        )
        grad_logits = (
            gates * (grad_gates - jnp.sum(grad_gates * gates, axis=-1, keepdims=True))
        ).astype(BF16)
        GR[0:NE] = GR[0:NE] + tn(grad_logits, N2[m])[0:NE]
        grad = nn(PM[m, 0] + PM[m, 1], DXB[m].reshape(S, D)) + nt(grad_logits, small)
        hat, rstd = normalize(MID[m])
        GR[NE + 1 : NE + 2] = GR[NE + 1 : NE + 2] + jnp.sum(grad * hat, axis=0, keepdims=True)
        grad_middle = upstream + normalize_back(grad * gain_two, hat, rstd)
        GM[m] = grad_middle
        branch = grad_middle.astype(BF16)
        N2[m] = branch
        back = None
        for cols, block in proj.blocks():
            term = nt(branch[:, cols], block)
            back = term if back is None else back + term
        GA[m] = back.astype(BF16)

    def backward_heads(m):
        def attend(hp, carry):
            query, keys, values = (J[m, :, columns(i * D, hp)] for i in range(3))
            grads = GA[m, :, columns(0, hp)]
            grad_query = jnp.zeros((TP, pair), F32)
            grad_keys = jnp.zeros((TP, pair), F32)
            grad_values = jnp.zeros((TP, pair), F32)
            for i in range(2):
                part = half_of(query, i)
                upstream = half_of(grads, i)
                probs = softmax_scores(part, keys)
                grad_probs = nt(upstream, values)
                grad_values = grad_values + tn(probs.astype(BF16), upstream)
                grad_scores = (
                    probs
                    * (grad_probs - jnp.sum(grad_probs * probs, axis=-1, keepdims=True))
                ).astype(BF16)
                grad_query = grad_query + nn(grad_scores, half_of(keys, i))
                grad_keys = grad_keys + tn(grad_scores, part)
            GJ[m, :, columns(0, hp)] = (grad_query * scale).astype(BF16)
            GJ[m, :, columns(D, hp)] = (grad_keys * scale).astype(BF16)
            GJ[m, :, columns(2 * D, hp)] = grad_values.astype(BF16)
            return carry

        lax.fori_loop(0, D // pair, attend, 0)

    def backward_end(m, carry):
        grad = None
        for cols, block in qkv.blocks():
            term = nt(GJ[m, :, cols], block)
            grad = term if grad is None else grad + term
        hat, rstd = normalize(XP[m].astype(F32))
        GR[NE : NE + 1] = GR[NE : NE + 1] + jnp.sum(grad * hat, axis=0, keepdims=True)
        full = GM[m] + normalize_back(grad * gain_one, hat, rstd)
        b["IG"][m, :, 0, :] = full[0:T]
        return carry

    sums_now((1, 1, 0), (2, 0, 0))
    for m in range(M):
        exchanged(DXB, m, s_dx[m])
        exchanged(GCB, m, s_gc[m])
        backward_top(m)
        if m == 0:
            sums_now((1, 1, 1))
        if m == M - 1:
            proj.put(ATT[...].reshape(M * TP, D), N2)
            proj.sum_core()
            sums_now((1, 2, 1))
        backward_heads(m)
        if m == 0:
            sums_now((2, 0, 1), (2, 0, 2), (1, 1, 2), (2, 1, 0))
    sums_now((1, 2, 2))
    proj.sum_plane()
    qkv.put(N1[...].reshape(M * TP, D), GJ)
    GB, SB1, SB2, SB3, SB4 = (b[k] for k in ("GB", "SB1", "SB2", "SB3", "SB4"))
    qkv.sum_core()
    lax.fori_loop(0, M, backward_end, 0)
    kept.append(fetch(b["IG"], igrad))
    GB[...] = GR[...].astype(BF16)
    r_b1 = one_send(GB, SB1, sibling)
    qkv.sum_plane()
    proj.sum_cross()
    arrived(SB1, r_b1)
    SB2[y] = GB[...] + SB1[...]
    s_b2, r_b2 = sends.take(G - 1) - 1, sems.take(G - 1) - 1
    for d in range(1, G):
        send(SB2.at[y], SB2.at[y], s_b2 + d, r_b2 + d, at(z, x, ((y + d) % G) * 2 + core))
        sent_later(s_b2 + d, SB2.at[y])
    sums_now((2, 1, 1), (2, 1, 2), (2, 2, 1), (1, 2, 0), (2, 2, 2))
    qkv.sum_cross()
    proj.sum_z()
    if nz == 4:

        @pl.when(at_end)
        def _():
            for k in first_ends:
                sums_end_in(k)

    for d in range(1, G):
        arrived(SB2.at[(y + G - d) % G], r_b2 + d)
    total = SB2[0].astype(F32)
    for j in range(1, G):
        total = total + SB2[j].astype(F32)
    SB3[x] = total.astype(BF16)
    r_b3 = one_send(SB3.at[x], SB3.at[x], across)
    sums_now((1, 3, 0), (1, 3, 1), (1, 3, 2), (2, 2, 0))
    qkv.sum_z()
    arrived(SB3.at[1 - x], r_b3)
    SB4[z] = SB3[0] + SB3[1]
    s_b4, r_b4 = sends.take(1), sems.take(1)
    for dz in orders:
        send(SB4.at[z], SB4.at[z], s_b4, r_b4, at((z + dz) % nz, x, e))
    sent_later(s_b4, SB4.at[0 : nz - 1])
    sums_rest()
    sums_end_out(False)
    if nz == 4:

        @pl.when(jnp.logical_not(at_end))
        def _():
            for k in (0, nz - 1):
                sums_end_in(k)

    proj.hand_out()
    qkv.hand_out()
    if nz == 4:

        @pl.when(at_end)
        def _():
            for k in last_ends:
                sums_end_in(k)

        @pl.when(jnp.logical_not(at_end))
        def _():
            for k in range(1, nz - 1):
                sums_end_in(k)

    else:
        for k in range(nz):
            sums_end_in(k)
    sums_end_out(True)
    for m in range(M):
        exchanged(YB, m, s_y[m])
        outputs(m)
    b["AO"][...] = b["AR"][...].astype(BF16)
    kept.append(fetch(b["AO"], act))
    arrived(SB4.at[0 : nz - 1], r_b4)
    total = SB4[0].astype(F32)
    for k in range(1, nz):
        total = total + SB4[k].astype(F32)
    mine = (
        lax.broadcasted_iota(jnp.int32, (D, RF), 0)
        == lax.broadcasted_iota(jnp.int32, (D, RF), 1) + f * RF
    ).astype(F32)
    b["GS"][...] = lax.dot_general(
        total,
        mine,
        (((1,), (0,)), ((), ())),
        precision=lax.Precision.HIGHEST,
        preferred_element_type=F32,
    )
    kept.append(fetch(b["GS"].at[0:NE], grouter))
    kept.append(fetch(b["GS"].at[NE : NE + 1], ggain1))
    kept.append(fetch(b["GS"].at[NE + 1 : NE + 2], ggain2))
    sums_close()
    proj.leave(gout)
    qkv.leave(gqkv)
    for cond, copy in pending:
        when(cond, copy.wait_send)
    for copy in kept:
        copy.wait()
    used = (sends.used, sems.used, locals_.used)
    assert all(a <= b for a, b in zip(used, counts)), (used, counts)


def hand_over(*refs):
    source, target, held, sem = refs[:9], refs[9:18], refs[18:-1], refs[-1]
    cast = [k for k in range(9) if source[k].dtype != target[k].dtype]
    order = sorted(range(9), key=lambda k: -math.prod(target[k].shape))
    for k in order:
        pltpu.make_async_copy(source[k], held[k], sem.at[0, k]).start()
    for k in order:
        pltpu.make_async_copy(source[k], held[k], sem.at[0, k]).wait()
        ready = held[k]
        if k in cast:
            ready = held[9 + cast.index(k)]
            ready[...] = held[k][...].astype(ready.dtype)
        pltpu.make_async_copy(ready, target[k], sem.at[1, k]).start()
    for k in order:
        pltpu.make_async_copy(target[k], target[k], sem.at[1, k]).wait()


def body(
    mesh_shape,
    inputs,
    gain_attn,
    qkv_weight,
    out_weight,
    gain_moe,
    router_weight,
    expert_in,
    expert_out,
    routes,
    cotangent,
):
    micro, images, seq, width = inputs.shape
    c = layout(mesh_shape, micro, images * seq, width, expert_in.shape[2])
    rows = images * seq
    scratch = scratch_of(c)
    names = list(scratch)
    nz, G = c["nz"], c["G"]
    counts = (48 + 9 * (G - 1), 25 + 19 * nz + 2 * nz * nz + 9 * (G - 1), 19 + 2 * c["E"])
    shapes = (
        ((rows, micro, width), BF16),
        ((micro, rows, 1, width), F32),
        (qkv_weight.shape, F32),
        (out_weight.shape, F32),
        ((1, c["RF"]), F32),
        ((1, c["RF"]), F32),
        ((c["NE"], c["RF"]), F32),
        (expert_in.shape, F32),
        (expert_out.shape, F32),
    )
    shapes = [jax.ShapeDtypeStruct(s, t) for s, t in shapes]
    sums = (2, 3, 7, 8)
    halves = [
        jax.ShapeDtypeStruct(s.shape, BF16 if k in sums else s.dtype) for k, s in enumerate(shapes)
    ]
    anywhere = pl.BlockSpec(memory_space=pltpu.HBM)
    results = pl.pallas_call(
        functools.partial(kernel, c, names, counts),
        out_shape=halves,
        in_specs=[anywhere] * 10,
        out_specs=[anywhere] * 9,
        scratch_shapes=[pltpu.VMEM(s, t) for s, t in scratch.values()]
        + [pltpu.SemaphoreType.DMA((count,)) for count in counts],
        compiler_params=pltpu.CompilerParams(
            collective_id=0, has_side_effects=True, vmem_limit_bytes=60 * 1024 * 1024
        ),
    )(
        jnp.transpose(inputs, (1, 2, 0, 3)).reshape(rows, micro, width),
        jnp.transpose(cotangent, (1, 2, 0, 3)).reshape(rows, micro, width),
        jnp.transpose(routes, (0, 1, 3, 2)).reshape(micro, 2, rows),
        qkv_weight,
        out_weight,
        gain_attn[None, :],
        gain_moe[None, :],
        router_weight.T,
        expert_in,
        expert_out,
    )
    act, igrad, gqkv, gout, ggain1, ggain2, grouter, gein, geout = pl.pallas_call(
        hand_over,
        out_shape=shapes,
        in_specs=[anywhere] * 9,
        out_specs=[anywhere] * 9,
        scratch_shapes=[pltpu.VMEM(s.shape, s.dtype) for s in halves]
        + [pltpu.VMEM(shapes[k].shape, F32) for k in sums]
        + [pltpu.SemaphoreType.DMA((2, 9))],
        compiler_params=pltpu.CompilerParams(vmem_limit_bytes=60 * 1024 * 1024),
    )(*results)
    return (
        jnp.transpose(act.reshape(images, seq, micro, width), (2, 0, 1, 3)),
        igrad.reshape(inputs.shape),
        ggain1[0],
        gqkv,
        gout,
        ggain2[0],
        grouter.T,
        gein,
        geout,
    )


def solution(mesh):
    return jax.shard_map(
        functools.partial(body, dict(mesh.shape)),
        mesh=mesh,
        in_specs=(
            P(None, ("fsdp", "expert"), None, None),
            P("fsdp"),
            P("fsdp", None),
            P("fsdp", None),
            P("fsdp"),
            P("fsdp", None),
            P("expert", "fsdp", None),
            P("expert", "fsdp", None),
            P(None, ("fsdp", "expert"), None, None),
            P(None, ("fsdp", "expert"), None, None),
        ),
        out_specs=(
            P(None, ("fsdp", "expert"), None, None),
            P(None, ("fsdp", "expert"), None, None),
            P("fsdp"),
            P("fsdp", None),
            P("fsdp", None),
            P("fsdp"),
            P("fsdp", None),
            P("expert", "fsdp", None),
            P("expert", "fsdp", None),
        ),
        check_vma=False,
    )
```

```python
import functools
import math

import jax
import jax.numpy as jnp
from jax import lax
from jax.experimental import pallas as pl
from jax.experimental.pallas import tpu as pltpu
from jax.sharding import PartitionSpec as P

HEADS = 8
EPS = 1e-06
MESH = pl.DeviceIdType.MESH
F32 = jnp.float32
BF16 = jnp.bfloat16


def nn(a, b):
    return lax.dot_general(a, b, (((1,), (0,)), ((), ())), preferred_element_type=F32)


def nt(a, b):
    return lax.dot_general(a, b, (((1,), (1,)), ((), ())), preferred_element_type=F32)


def tn(a, b):
    return lax.dot_general(a, b, (((0,), (0,)), ((), ())), preferred_element_type=F32)


def normalize(values):
    center = jnp.mean(values, axis=-1, keepdims=True)
    shifted = values - center
    spread = jnp.mean(shifted * shifted, axis=-1, keepdims=True)
    rstd = lax.rsqrt(spread + EPS)
    return shifted * rstd, rstd


def normalize_back(grad, hat, rstd):
    return rstd * (
        grad
        - jnp.mean(grad, axis=-1, keepdims=True)
        - hat * jnp.mean(grad * hat, axis=-1, keepdims=True)
    )


class Semaphores:
    def __init__(self):
        self.used = 0

    def take(self, count):
        start = self.used
        self.used += count
        return start


SIZES = ("nz", "E", "G", "NE", "NR", "T", "TP", "CP", "S", "D", "FC", "RF", "CF", "M")


def layout(mesh_shape, micro, seq, width, ff_width):
    fsdp, peers = mesh_shape["fsdp"], mesh_shape["expert"]
    c = {}
    c["nz"] = fsdp // 2
    c["E"] = peers
    c["G"] = peers // 2
    c["NE"] = 2 * peers
    c["T"] = seq
    c["TP"] = -(-seq // 16) * 16
    c["CP"] = -(-max(2, 10 * seq // (4 * 2 * peers) + 1) // 16) * 16
    c["S"] = c["NE"] * c["CP"]
    c["NR"] = -(-(c["NE"] + 2) // 16) * 16
    c["D"] = width
    c["FF"] = ff_width
    c["RF"] = width // fsdp
    c["CF"] = ff_width // fsdp
    c["FC"] = 2 * c["CF"]
    c["WQ"] = 128 * -(-(3 * width // 128) // peers)
    c["WO"] = 128 * -(-(width // 128) // peers)
    c["M"] = micro
    return c


def scratch_of(c):
    nz, E, G, NE, NR, T, TP, CP, S, D, FC, RF, CF, M = (c[k] for k in SIZES)
    h = nz // 2
    v = {
        "XP": ((M, TP, D), BF16),
        "CT": ((M, TP, D), BF16),
        "XR": ((T, M, D), BF16),
        "CR": ((T, M, D), BF16),
        "AR": ((T, M, D), F32),
        "AO": ((T, M, D), BF16),
        "IG": ((M, T, 1, D), F32),
        "RR": ((M, 2, T), jnp.int32),
        "RT": ((M, TP, 128), F32),
        "SR": ((nz, 2, NR, RF), BF16),
        "G1": ((1, RF), BF16),
        "G2": ((1, RF), BF16),
        "RW": ((NE, RF), BF16),
        "GI": ((2, RF, nz * FC), BF16),
        "GT": ((2, CF, D), BF16),
        "GS": ((NR, RF), F32),
        "SM": ((nz, 2, RF, 128), BF16),
        "WIN": ((nz, nz, 2, RF, FC), BF16),
        "WOUT": ((nz, 2, CF, D), BF16),
        "N1": ((M, TP, D), BF16),
        "J": ((M, TP, 3 * D), BF16),
        "ATT": ((M, TP, D), BF16),
        "MID": ((M, TP, D), F32),
        "N2": ((M, TP, D), BF16),
        "GATES": ((M, TP, 128), F32),
        "PB": ((M, HEADS, TP, TP), BF16),
        "N1T": ((M, D, TP), BF16),
        "ATTT": ((M, D, TP), BF16),
        "PM": ((M, 2, TP, S), BF16),
        "XS": ((M, NE, CP, D), BF16),
        "XB": ((M, NE, CP, D), BF16),
        "GSS": ((M, NE, CP, D), BF16),
        "GRB": ((M, NE, CP, D), BF16),
        "CSS": ((M, NE, 8, 128), F32),
        "CSB": ((M, NE, 8, 128), F32),
        "CROW": ((8, S), F32),
        "GC": ((M, S, D), BF16),
        "YB": ((M, NE, CP, D), BF16),
        "DXB": ((M, NE, CP, D), BF16),
        "GCS": ((M, NE, 8, 128), F32),
        "GCB": ((M, NE, 8, 128), F32),
        "YACC": ((M, S, D), F32),
        "DXACC": ((M, S, D), F32),
        "AS": ((M, S, FC), BF16),
        "GHS": ((M, S, FC), BF16),
        "DWI": ((nz, nz, 2, RF, FC), BF16),
        "DWO": ((nz, 2, CF, D), BF16),
        "UPI": ((nz, nz, 2, RF, FC), BF16),
        "UPO": ((nz, 2, CF, D), BF16),
        "DNI": ((nz, nz, 2, RF, FC), BF16),
        "DNO": ((nz, 2, CF, D), BF16),
        "FXI": ((nz, RF, FC), BF16),
        "FXO": ((CF, D), BF16),
        "GM": ((M, TP, D), F32),
        "GA": ((M, TP, D), BF16),
        "GJ": ((M, TP, 3 * D), BF16),
        "GR": ((NR, D), F32),
        "GB": ((NR, D), BF16),
        "SB1": ((NR, D), BF16),
        "SB2": ((G, NR, D), BF16),
        "SB3": ((2, NR, D), BF16),
        "SB4": ((nz, NR, D), BF16),
    }
    for name, wide in (("Q", c["WQ"]), ("O", c["WO"])):
        for part, lead in (
            ("W", (E, nz, 2)),
            ("G", (E, nz, 2)),
            ("B1", (G, nz, 2)),
            ("Y1", (G, h, 2)),
            ("X1", (G, nz - h)),
            ("X2", (h,)),
            ("Y2", (G, nz - h)),
            ("Z", (nz,)),
            ("F", (E,)),
        ):
            v[name + part] = (lead + (RF, wide), BF16)
    return v


def kernel(c, names, counts, *refs):
    nz, E, G, NE, NR, T, TP, CP, S, D, FC, RF, CF, M = (c[k] for k in SIZES)
    (xin, cot, routes, qkv_s, out_s, gain1, gain2, router, ein, eout) = refs[:10]
    (act, igrad, gqkv, gout, ggain1, ggain2, grouter, gein, geout) = refs[10:19]
    b = dict(zip(names, refs[19:]))
    SS, RS, LS = refs[-3:]
    h = nz // 2
    head = D // HEADS
    pair = 2 * head
    scale = 1.0 / math.sqrt(head)
    sems, sends, locals_ = Semaphores(), Semaphores(), Semaphores()
    pending = []

    f = lax.axis_index("fsdp")
    e = lax.axis_index("expert")
    z, x = f // 2, f % 2
    y, core = e // 2, e % 2
    pme = 2 * e + x

    def at(zz, xx, ee):
        return (zz * 2 + xx, ee)

    sibling = at(z, x, y * 2 + (1 - core))
    across = at(z, 1 - x, e)

    def copy_of(src, dst, ssem, rsem, device):
        return pltpu.make_async_remote_copy(
            src_ref=src,
            dst_ref=dst,
            send_sem=SS.at[ssem],
            recv_sem=RS.at[rsem],
            device_id=device,
            device_id_type=MESH,
        )

    def when(cond, run):
        if cond is None:
            run()
        else:
            pl.when(cond)(run)

    def send(src, dst, ssem, rsem, device, cond=None):
        when(cond, copy_of(src, dst, ssem, rsem, device).start)

    def arrived(dst, rsem, cond=None):
        when(cond, copy_of(dst, dst, 0, rsem, sibling).wait_recv)

    def sent_later(ssem, src, cond=None):
        pending.append((cond, copy_of(src, src, ssem, 0, sibling)))

    def one_send(src, dst, device):
        ssem, rsem = sends.take(1), sems.take(1)
        send(src, dst, ssem, rsem, device)
        sent_later(ssem, src)
        return rsem

    barrier = pltpu.get_barrier_semaphore()
    for dz in range(1, nz):
        pl.semaphore_signal(
            barrier, inc=1, device_id=at((z + dz) % nz, x, e), device_id_type=MESH
        )

    def greet(d, carry):
        p = (pme + d) % NE
        pl.semaphore_signal(barrier, inc=1, device_id=at(z, p % 2, p // 2), device_id_type=MESH)
        return carry

    lax.fori_loop(1, NE, greet, 0)

    SM, WIN, WOUT = b["SM"], b["WIN"], b["WOUT"]
    UP, DN = (b["UPI"], b["UPO"]), (b["DNI"], b["DNO"])

    def fetch(src, dst):
        copy = pltpu.make_async_copy(src, dst, LS.at[locals_.take(1)])
        copy.start()
        return copy

    far_first = [d for k in range(1, nz) for d in (k, nz - k) if 2 * k <= nz]
    orders = list(dict.fromkeys(far_first))

    class Dense:
        def __init__(self, name, shard, wide):
            self.name, self.shard, self.wide = name, shard, wide
            self.w, self.g = b[name + "W"], b[name + "G"]
            self.used = -(-shard.shape[1] // wide)
            self.own = locals_.take(1)
            for k in range(self.used):

                @pl.when(e == k)
                def _():
                    pltpu.make_async_copy(
                        self.columns(shard, k), self.w.at[k, z, x], LS.at[self.own]
                    ).start()

        def columns(self, ref, k):
            return ref.at[:, k * self.wide : (k + 1) * self.wide]

        def own_ready(self):
            copy = pltpu.make_async_copy(
                self.w.at[e, z, x], self.w.at[e, z, x], LS.at[self.own]
            )
            when(None if self.used == E else e < self.used, copy.wait)

        def along_z(self):
            w = self.w
            self.r_z, s_z = sems.take(nz - 1) - 1, sends.take(1)
            for dz in orders:
                to = at((z + dz) % nz, x, e)
                send(w.at[e, z, x], w.at[e, z, x], s_z, self.r_z + dz, to)
            sent_later(s_z, w.at[e, 0 : nz - 1, x])
            self.s_x, self.r_x = sends.take(1), sems.take(nz)
            self.s_y, self.r_y = sends.take(G - 1) - 1, sems.take(G - 1) - 1
            self.s_c, self.r_c = sends.take(1), sems.take(1)
            sent_later(self.s_x, w.at[e, :, x])
            for d in range(1, G):
                sent_later(self.s_y + d, w.at[e, :, x])
            sent_later(self.s_c, w.at[0:G])

        def spread(self, dz):
            zz = (z + nz - dz) % nz
            piece = self.w.at[e, zz, x]
            if dz > 0:
                arrived(piece, self.r_z + dz)
            send(piece, piece, self.s_x, self.r_x + dz, across)
            for d in range(1, G):
                to = at(z, x, ((y + d) % G) * 2 + core)
                send(piece, piece, self.s_y + d, self.r_y + d, to)
            send(piece, piece, self.s_c, self.r_c, sibling)

        def forward(self):
            w = self.w
            self.s_xy, self.r_xy = sends.take(G - 1) - 1, sems.take(G - 1) - 1
            for d in range(1, G):
                sent_later(self.s_xy + d, w.at[e, :, x])
            for dz in [0] + orders:
                piece = w.at[e, (z + nz - dz) % nz, 1 - x]
                arrived(piece, self.r_x + dz)
                for d in range(1, G):
                    to = at(z, x, ((y + d) % G) * 2 + core)
                    send(piece, piece, self.s_xy + d, self.r_xy + d, to)
                send(piece, piece, self.s_c, self.r_c, sibling)

        def corner(self):
            w = self.w
            for d in range(1, G):
                ee = ((y + G - d) % G) * 2 + core
                arrived(w.at[ee, :, x], self.r_y + d)
                send(w.at[ee, :, x], w.at[ee, :, x], self.s_c, self.r_c, sibling)
                arrived(w.at[ee, :, 1 - x], self.r_xy + d)
                send(w.at[ee, :, 1 - x], w.at[ee, :, 1 - x], self.s_c, self.r_c, sibling)

        def ready(self):
            arrived(self.w.at[0:G], self.r_c)

        def blocks(self):
            for k in range(self.used):
                cols = slice(k * self.wide, min((k + 1) * self.wide, self.shard.shape[1]))
                yield cols, self.w[k].reshape(D, self.wide)

        def put(self, left, right):
            for k in range(self.used):
                cols = slice(k * self.wide, (k + 1) * self.wide)
                part = nn(left[0], right[0, :, cols])
                for m in range(1, M):
                    part = part + nn(left[m], right[m, :, cols])
                self.g[k] = part.astype(BF16).reshape(nz, 2, RF, self.wide)

        def sum_core(self):
            s, self.r_1 = sends.take(1), sems.take(1)
            for j in range(G):
                send(self.g.at[2 * j + 1 - core], b[self.name + "B1"].at[j], s, self.r_1, sibling)
            sent_later(s, b[self.name + "B1"])

        def sum_plane(self):
            g, first = self.g, b[self.name + "B1"]
            arrived(first, self.r_1)
            for j in range(G):
                g[2 * j + core] = g[2 * j + core] + first[j]
            s, self.r_y1 = sends.take(G - 1) - 1, sems.take(G - 1) - 1
            for d in range(1, G):
                q = (y + d) % G
                piece = g.at[2 * q + core, 0:h]
                send(piece, b[self.name + "Y1"].at[y], s + d, self.r_y1 + d, at(z, x, 2 * q + core))
                sent_later(s + d, piece)
            s, self.r_x1 = sends.take(1), sems.take(1)
            for j in range(G):
                piece = g.at[2 * j + core, h:nz, 1 - x]
                send(piece, b[self.name + "X1"].at[j], s, self.r_x1, across)
            sent_later(s, b[self.name + "X1"])

        def sum_cross(self):
            g, from_y, from_x = self.g, b[self.name + "Y1"], b[self.name + "X1"]
            for d in range(1, G):
                q = (y + G - d) % G
                arrived(from_y.at[q], self.r_y1 + d)
                g[e, 0:h] = g[e, 0:h] + from_y[q]
            self.r_x2 = one_send(g.at[e, 0:h, 1 - x], b[self.name + "X2"], across)
            arrived(from_x, self.r_x1)
            for j in range(G):
                g[2 * j + core, h:nz, x] = g[2 * j + core, h:nz, x] + from_x[j]
            s, self.r_y2 = sends.take(G - 1) - 1, sems.take(G - 1) - 1
            for d in range(1, G):
                q = (y + d) % G
                piece = g.at[2 * q + core, h:nz, x]
                send(piece, b[self.name + "Y2"].at[y], s + d, self.r_y2 + d, at(z, x, 2 * q + core))
                sent_later(s + d, piece)

        def sum_z(self):
            g, from_x, from_y = self.g, b[self.name + "X2"], b[self.name + "Y2"]
            arrived(from_x, self.r_x2)
            g[e, 0:h, x] = g[e, 0:h, x] + from_x[...]
            for d in range(1, G):
                q = (y + G - d) % G
                arrived(from_y.at[q], self.r_y2 + d)
                g[e, h:nz, x] = g[e, h:nz, x] + from_y[q]
            s, self.r_z2 = sends.take(1), sems.take(1)
            parts = b[self.name + "Z"]
            for dz in orders:
                zz = (z + dz) % nz
                send(g.at[e, zz, x], parts.at[z], s, self.r_z2, at(zz, x, e))
            sent_later(s, parts.at[0 : nz - 1])
            parts[z] = g[e, z, x]

        def hand_out(self):
            parts, done = b[self.name + "Z"], b[self.name + "F"]
            arrived(parts.at[0 : nz - 1], self.r_z2)
            total = parts[0].astype(F32)
            for k in range(1, nz):
                total = total + parts[k].astype(F32)
            done[e] = total.astype(BF16)
            s, self.r_f = sends.take(1), sems.take(1)

            def one(d, carry):
                send(done.at[e], done.at[e], s, self.r_f, at(z, x, (e + d) % E))
                return carry

            lax.fori_loop(1, E, one, 0)
            sent_later(s, done.at[0 : E - 1])

        def leave(self, out):
            done = b[self.name + "F"]
            arrived(done.at[0 : E - 1], self.r_f)
            for k in range(self.used):
                kept.append(fetch(done.at[k], self.columns(out, k)))

    qkv, proj = Dense("Q", qkv_s, c["WQ"]), Dense("O", out_s, c["WO"])
    kept = []

    SR = b["SR"]
    SR[z, x] = jnp.zeros((NR, RF), BF16)
    small_in = [
        fetch(gain1, b["G1"]),
        fetch(gain2, b["G2"]),
        fetch(router, b["RW"]),
    ]
    token_in = [fetch(routes, b["RR"]), fetch(xin, b["XR"]), fetch(cot, b["CR"])]
    own_in = locals_.take(1)
    for k in range(nz):
        pltpu.make_async_copy(
            ein.at[x, :, k * FC : (k + 1) * FC], WIN.at[k, z, x], LS.at[own_in]
        ).start()
    own_out = fetch(eout.at[x], WOUT.at[z, x])

    for copy in small_in:
        copy.wait()
    SR[z, x, 0:NE] = b["RW"][...]
    SR[z, x, NE : NE + 1] = b["G1"][...]
    SR[z, x, NE + 1 : NE + 2] = b["G2"][...]
    entry = lax.broadcasted_iota(jnp.int32, (NR, 128), 0)
    place = lax.broadcasted_iota(jnp.int32, (NR, 128), 1)
    pick = (
        ((entry < NE) & (entry == place))
        | ((entry >= NE) & (entry < NE + 2) & (place == entry - NE + 126))
    ).astype(BF16)
    qkv.own_ready()
    proj.own_ready()
    pl.semaphore_wait(barrier, nz - 1 + NE - 1)

    qkv.along_z()
    r_sz, s_sz = sems.take(1), sends.take(1)
    for dz in orders:
        send(SR.at[z, x], SR.at[z, x], s_sz, r_sz, at((z + dz) % nz, x, e))
    sent_later(s_sz, SR.at[0 : nz - 1, x])
    qkv.spread(0)

    s_xi, r_xi = sends.take(1), sems.take(1)
    for k in range(nz):
        send(ein.at[1 - x, :, k * FC : (k + 1) * FC], WIN.at[k, z, x], s_xi, r_xi, across)
    sent_later(s_xi, WIN.at[:, z, x])


    XP, CT, RT, PM = b["XP"], b["CT"], b["RT"], b["PM"]

    @pl.when(z == 0)
    def _():
        UP[0][:, 0] = jnp.zeros((nz, 2, RF, FC), BF16)
        UP[1][0] = jnp.zeros((2, CF, D), BF16)

    @pl.when(z == nz - 1)
    def _():
        DN[0][:, nz - 1] = jnp.zeros((nz, 2, RF, FC), BF16)
        DN[1][nz - 1] = jnp.zeros((2, CF, D), BF16)

    for copy in token_in:
        copy.wait()
    lane = lax.broadcasted_iota(jnp.int32, (TP, 128), 1)
    lane_f = lane.astype(F32)
    swap = (
        lax.broadcasted_iota(jnp.int32, (2, 128), 0) == lax.broadcasted_iota(jnp.int32, (2, 128), 1)
    ).astype(BF16)
    for m in range(M):
        XP[m] = jnp.zeros((TP, D), BF16)
        CT[m] = jnp.zeros((TP, D), BF16)
        RT[m] = jnp.full((TP, 128), -1.0, F32)
        XP[m, 0:T] = b["XR"][:, m, :]
        CT[m, 0:T] = b["CR"][:, m, :]
        RT[m, 0:T] = tn(b["RR"][m].astype(BF16), swap)

    def onehot(m, j):
        return RT[m][:, j : j + 1] == lane_f

    before = (
        lax.broadcasted_iota(jnp.int32, (TP, TP), 1) < lax.broadcasted_iota(jnp.int32, (TP, TP), 0)
    ).astype(BF16)
    spots = lax.broadcasted_iota(jnp.int32, (TP, S), 1).astype(F32)
    for m in range(M):
        first = onehot(m, 0).astype(F32)
        second = onehot(m, 1).astype(F32)
        rank0 = nn(before, first.astype(BF16))
        rank1 = nn(before, second.astype(BF16)) + jnp.sum(first, axis=0, keepdims=True)
        for j, (hot, rank) in enumerate(((first, rank0), (second, rank1))):
            slot = jnp.sum(hot * rank, axis=-1, keepdims=True)
            route = RT[m][:, j : j + 1]
            spot = jnp.where(route >= 0, route * CP + slot, -1.0)
            PM[m, j] = (spots == spot).astype(BF16)

    def turn_of(i):
        return 0 if i == 0 else i % (nz - 1) + 1

    groups = (range(0, 2), range(2, nz))
    s_zi = [[sends.take(1) for _ in groups] for _ in range(2)]
    s_zo = [sends.take(1) for _ in range(2)]
    r_zi = [[sems.take(nz) for _ in groups] for _ in range(2)]
    r_zo = [sems.take(2 * nz) for _ in range(2)]
    for zz in range(nz):
        for side in range(2):
            count = zz + 1 if side == 0 else nz - zz
            if count < nz:
                for g, turns in enumerate(groups):
                    sent_later(s_zi[side][g], WIN.at[0 : len(turns), 0:count], z == zz)
                sent_later(s_zo[side], WOUT.at[0:count], z == zz)

    def reach(side, d, some=None):
        begun = z - d if side == 0 else z + d
        there = (begun >= 0) if side == 0 else (begun < nz)
        last = (z == nz - 1) if side == 0 else (z == 0)
        if some is not None:
            there = there & some(begun)
        return begun, there, there & jnp.logical_not(last)

    def onward(side):
        return at((z + 1) % nz if side == 0 else (z + nz - 1) % nz, x, e)

    def pass_in(g, d, halves=(0, 1)):
        for side in range(2):
            begun, there, goes = reach(side, d)
            r = r_zi[side][g]
            if d > 0:
                arrived(WIN.at[0 : len(groups[g]), begun], r + d, there)
            if d < nz - 1:

                @pl.when(goes)
                def _():
                    for i in groups[g]:
                        k = turn_of(i) if side == 1 else nz - 1 - turn_of(i)
                        for half in halves:
                            piece = WIN.at[k, begun, x if half == 0 else 1 - x]
                            send(piece, piece, s_zi[side][g], r + d + 1, onward(side))

    def pass_out(d, half, late=None):
        xx = x if half == 0 else 1 - x
        for side in range(2):
            odd = nz - 2 if side == 0 else 1
            some = None
            if late is not None:
                some = (lambda begun: begun == odd) if late else (lambda begun: begun != odd)
            begun, there, goes = reach(side, d, some)
            r = r_zo[side] + 2 * d + half
            piece = WOUT.at[begun, xx]
            if d > 0:
                arrived(piece, r, there)
            if d < nz - 1:
                send(piece, piece, s_zo[side], r + 2, onward(side), goes)

    early, others = 0, 1
    GATES, XS, XB, GC, CROW = (b[k] for k in ("GATES", "XS", "XB", "GC", "CROW"))
    GSS, GRB, CSS, CSB = (b[k] for k in ("GSS", "GRB", "CSS", "CSB"))
    GCS, GCB, YB, DXB = (b[k] for k in ("GCS", "GCB", "YB", "DXB"))
    YS, DXS = XS, GSS

    def gone(src, m, sem):
        copy_of(src.at[m, 0 : NE - 1], src.at[m, 0 : NE - 1], sem[0], 0, sibling).wait_send()

    def exchange(src, dst, m, sem, later=True):
        rows = slice(0, 1 if src.shape[2] == 8 else src.shape[2])

        def one(d, carry):
            p = (pme + d) % NE
            send(src.at[m, p, rows], dst.at[m, pme, rows], *sem, at(z, p % 2, p // 2))
            return carry

        lax.fori_loop(1, NE, one, 0)
        if later:
            sent_later(sem[0], src.at[m, 0 : NE - 1, rows])
        dst[m, pme] = src[m, pme]

    def exchanged(dst, m, sem):
        rows = slice(0, 1 if dst.shape[2] == 8 else dst.shape[2])
        arrived(dst.at[m, 0 : NE - 1, rows], sem[1])

    def pairs():
        return [(sends.take(1), sems.take(1)) for _ in range(M)]

    s_x, s_cs, s_gr, s_dx, s_gc, s_y = (pairs() for _ in range(6))
    for m in range(M):
        GSS[m] = tn(PM[m, 0] + PM[m, 1], CT[m]).astype(BF16).reshape(NE, CP, D)

    for dz in orders[:2]:
        qkv.spread(dz)
    proj.along_z()
    proj.spread(0)
    pltpu.make_async_copy(WIN.at[:, z, x], WIN.at[:, z, x], LS.at[own_in]).wait()
    pass_in(early, 0, (0,))
    for dz in orders[2:]:
        qkv.spread(dz)
    arrived(SR.at[0 : nz - 1, x], r_sz)
    r_sx = one_send(SR.at[:, x], SR.at[:, x], across)
    own_out.wait()
    pass_out(0, 0)
    arrived(WIN.at[:, z, 1 - x], r_xi)
    pass_in(early, 0, (1,))
    qkv.forward()
    for dz in orders:
        proj.spread(dz)
    proj.forward()
    r_xo = one_send(eout.at[1 - x], WOUT.at[z, x], across)
    for m in range(M):
        exchange(GSS, GRB, m, s_gr[m], False)
    pass_in(others, 0, (0,))
    arrived(SR.at[:, 1 - x], r_sx)
    for zz in range(nz):
        for xx in range(2):
            SM[zz, xx] = tn(SR[zz, xx], pick).astype(BF16)
    qkv.corner()
    qkv.ready()

    small = SM[...].reshape(D, 128)
    gains = nt(pick, small)
    gain_one, gain_two = gains[NE : NE + 1], gains[NE + 1 : NE + 2]
    key_ok = lax.broadcasted_iota(jnp.int32, (1, TP), 1) < T
    low_half = lax.broadcasted_iota(jnp.int32, (1, pair), 1) < head
    N1, J, ATT, MID, N2 = b["N1"], b["J"], b["ATT"], b["MID"], b["N2"]
    def half_of(value, i):
        keep = low_half if i == 0 else jnp.logical_not(low_half)
        return jnp.where(keep, value, jnp.zeros_like(value))

    def softmax_scores(query, keys):
        scores = jnp.where(key_ok, nt(query, keys) * scale, -1e30)
        raised = jnp.exp(scores - jnp.max(scores, axis=-1, keepdims=True))
        return raised * (1.0 / jnp.sum(raised, axis=-1, keepdims=True))

    def columns(base, hp):
        return pl.ds(pl.multiple_of(base + hp * pair, 128), pair)

    def chosen_of(m, j):
        gates = GATES[m]
        return jnp.sum(jnp.where(onehot(m, j), gates, 0.0), axis=-1, keepdims=True)

    def forward(m):
        tokens = XP[m].astype(F32)
        hat, _ = normalize(tokens)
        N1[m] = (hat * gain_one).astype(BF16)
        for cols, block in qkv.blocks():
            J[m, :, cols] = nn(N1[m], block).astype(BF16)

        def attend(hp, carry):
            query, keys, values = (J[m, :, columns(i * D, hp)] for i in range(3))
            total = jnp.zeros((TP, pair), F32)
            for i in range(2):
                probs = softmax_scores(half_of(query, i), keys)
                probs = probs.astype(BF16)
                b["PB"][m, 2 * hp + i] = probs
                total = total + nn(probs, half_of(values, i))
            ATT[m, :, columns(0, hp)] = total.astype(BF16)
            return carry

        lax.fori_loop(0, D // pair, attend, 0)
        if m == 0:
            pass_in(early, 1)
            pass_in(others, 0, (1,))
            proj.corner()
            proj.ready()
        for cols, block in proj.blocks():
            MID[m, :, cols] = XP[m, :, cols].astype(F32) + nn(ATT[m], block)
        hat, _ = normalize(MID[m])
        N2[m] = (hat * gain_two).astype(BF16)
        logits = jnp.where(lane < NE, nn(N2[m], small), -1e30)
        raised = jnp.exp(logits - jnp.max(logits, axis=-1, keepdims=True))
        GATES[m] = raised / jnp.sum(raised, axis=-1, keepdims=True)
        XS[m] = tn(PM[m, 0] + PM[m, 1], N2[m]).astype(BF16).reshape(NE, CP, D)
        weight = PM[m, 0].astype(F32) * chosen_of(m, 0) + PM[m, 1].astype(F32) * chosen_of(m, 1)
        CROW[0:1] = jnp.sum(weight, axis=0, keepdims=True)
        for k in range(NE):
            CSS[m, k, 0:1, 0:CP] = CROW[0:1, k * CP : (k + 1) * CP]

    diagonal = lax.broadcasted_iota(jnp.int32, (CP, 128), 0) == lax.broadcasted_iota(
        jnp.int32, (CP, 128), 1
    )

    def scale_grads(m):
        for p in range(NE):
            by_lane = CSB[m, p, 0:1]
            weight = jnp.sum(jnp.where(diagonal, by_lane, 0.0), axis=1, keepdims=True)
            GC[m, p * CP : (p + 1) * CP] = (weight * GRB[m, p].astype(F32)).astype(BF16)

    for m in range(M):
        forward(m)
        exchange(XS, XB, m, s_x[m], False)
        exchange(CSS, CSB, m, s_cs[m])
        if m == 0:
            arrived(WOUT.at[z, 1 - x], r_xo)
            pass_out(0, 1, False)
    pass_in(early, 2)
    pass_out(1, 0)
    for d in range(3, nz):
        pass_in(early, d)
    pass_out(1, 1, False)
    pass_in(others, 1)

    same = (
        lax.broadcasted_iota(jnp.int32, (D, D), 0) == lax.broadcasted_iota(jnp.int32, (D, D), 1)
    ).astype(BF16)
    for m in range(M):
        b["N1T"][m] = nt(same, N1[m]).astype(BF16)
        b["ATTT"][m] = nt(same, ATT[m]).astype(BF16)
    YACC, DXACC, AS, GHS = b["YACC"], b["DXACC"], b["AS"], b["GHS"]
    DWI, DWO = b["DWI"], b["DWO"]
    YACC[...] = jnp.zeros_like(YACC)
    DXACC[...] = jnp.zeros_like(DXACC)
    c0, c1 = math.sqrt(2.0 / math.pi), 0.044715

    OWN = (DWI, DWO)
    s_up = [(sends.take(1), sends.take(1)) for _ in range(2)]
    r_up = [(sems.take(nz * nz), sems.take(2 * nz)) for _ in range(2)]

    def expert_part(k, m, loop=True):
        def half(xx, carry):
            cols = pl.ds(pl.multiple_of(xx * CF, 128), CF)
            w_in = WIN[k, :, :, :, cols].reshape(D, CF)
            w_out = WOUT[k, xx]
            hidden = nn(XB[m].reshape(S, D), w_in)
            grad_acted = nt(GC[m], w_out)
            square = hidden * hidden
            bent = jnp.tanh(c0 * hidden * (1.0 + c1 * square))
            acted = (0.5 * hidden * (1.0 + bent)).astype(BF16)
            slope = 0.5 * (1.0 + bent) + 0.5 * c0 * hidden * (1.0 - bent * bent) * (
                1.0 + 3.0 * c1 * square
            )
            grad_hidden = (grad_acted * slope).astype(BF16)
            AS[m, :, cols] = acted
            GHS[m, :, cols] = grad_hidden
            YACC[m] = YACC[m] + nn(acted, w_out)
            DXACC[m] = DXACC[m] + nt(grad_hidden, w_in)
            return carry

        if loop:
            lax.fori_loop(0, 2, half, 0)
        else:
            half(0, 0)
            half(1, 0)

    def expert_weights(k):
        def half(xx, carry):
            cols = pl.ds(pl.multiple_of(xx * CF, 128), CF)
            grads = GC[...].reshape(M * S, D)
            tokens = XB[...].reshape(M * S, D)
            DWO[k, xx] = tn(AS[:, :, cols].reshape(M * S, CF), grads).astype(BF16)
            DWI[k, :, :, :, cols] = (
                tn(tokens, GHS[:, :, cols].reshape(M * S, CF))
                .astype(BF16)
                .reshape(nz, 2, RF, CF)
            )
            return carry

        lax.fori_loop(0, 2, half, 0)

    def sum_step(side, i, begins, parts):
        far = z if side == 0 else nz - 1 - z
        GOT = UP if side == 0 else DN
        turn = ((i % (nz - 1)) + 1) * jnp.minimum(i, 1)
        k = turn if side == 0 else nz - 1 - turn

        def tokens_side(j, carry):
            goal = nz - 1 - j
            t = goal if side == 0 else nz - 1 - goal
            rsem = r_up[side][0] + k * nz + t

            @pl.when(goal > far)
            def _():
                if not begins:
                    arrived(GOT[0].at[k, t], rsem)
                    DWI[k, t] = DWI[k, t] + GOT[0][k, t]
                send(DWI.at[k, t], GOT[0].at[k, t], s_up[side][0], rsem, onward(side))

            return carry

        def results_side():
            for part, xx, rows in (
                (1, 1 - x, slice(0, CF)),
                (2, x, slice(0, CF)),
                (3, x, slice(0, CF // 2)),
                (4, x, slice(CF // 2, CF)),
            ):
                if part not in parts:
                    continue
                rsem = r_up[side][1] + 2 * k + xx
                if not begins:
                    arrived(GOT[1].at[k, xx], rsem)
                    DWO[k, xx] = DWO[k, xx] + GOT[1][k, xx]
                source, target = DWO.at[k, xx, rows], GOT[1].at[k, xx, rows]
                send(source, target, s_up[side][1], rsem, onward(side))

        if parts != (0,):
            pl.when(turn == nz - 1)(results_side)
        if 0 in parts:
            lax.fori_loop(0, nz - 1, tokens_side, 0)
        if parts != (0,):
            pl.when((turn > far) & (turn < nz - 1))(results_side)

    def sums_begin(i, parts=(0, 1, 2)):
        for side in range(2):
            far = z if side == 0 else nz - 1 - z
            step = functools.partial(sum_step, side, jnp.int32(i), True, parts)
            pl.when(far == 0)(step)

    def sums_pass(far_at, i, parts=(0, 1, 2)):
        for side in range(2):
            far = z if side == 0 else nz - 1 - z
            step = functools.partial(sum_step, side, jnp.int32(i), False, parts)
            pl.when(far == far_at)(step)

    passes = [(far, i, part) for far in range(1, nz - 1) for i in range(nz) for part in range(3)]

    def sums_now(*wanted):
        for step in wanted:
            if step in passes:
                passes.remove(step)
                sums_pass(step[0], step[1], (step[2],))

    def sums_rest():
        for far in range(1, nz - 1):
            left = [step for step in passes if step[0] == far]
            if nz <= 4:
                for _, i, part in left:
                    sums_pass(far, i, (part,))
            else:

                def one(i, carry, far=far):
                    sums_pass(far, i)
                    return carry

                lax.fori_loop(left[0][1], nz, one, 0)

    for zz in range(nz):
        for side in range(2):
            count = nz - 1 - zz if side == 0 else zz
            if count > 0:
                sent_later(s_up[side][0], DWI.at[:, 0:count], z == zz)
                sent_later(s_up[side][1], DWO.at[0:count], z == zz)

    def give_back(m):
        gone(GSS, m, s_gr[m])
        gone(XS, m, s_x[m])
        DXS[m] = DXACC[m].astype(BF16).reshape(NE, CP, D)
        exchange(DXS, DXB, m, s_dx[m])
        results = YACC[m].astype(BF16)
        YS[m] = results.reshape(NE, CP, D)
        for p in range(NE):
            rows = slice(p * CP, (p + 1) * CP)
            weight = jnp.sum(
                results[rows].astype(F32) * GRB[m, p].astype(F32), axis=1, keepdims=True
            )
            GCS[m, p, 0:1] = jnp.sum(jnp.where(diagonal, weight, 0.0), axis=0, keepdims=True)
        exchange(GCS, GCB, m, s_gc[m])

    when_two, when_far, when_late = (1, 2, nz - 1) if nz <= 4 else (0, 0, 0)
    for i in range(nz):
        if i == when_two:
            pass_out(2, 0)
            pass_out(2, 1, False)
        if i == when_far:
            pass_in(others, 2)
            if nz > 4:
                pass_out(0, 1, True)
            for d in range(3, nz):
                pass_in(others, d)
                pass_out(d, 0)
                pass_out(d, 1, False)
        if i == when_late:
            for d in range(1, nz):
                pass_out(d, 1, True)
            sums_now((1, 0, 0), (1, 0, 1), (1, 0, 2))
        block = turn_of(i) + (z // h) * (nz - 1 - 2 * turn_of(i))
        for m in range(M):
            if i == 0:
                exchanged(GRB, m, s_gr[m])
                exchanged(XB, m, s_x[m])
                exchanged(CSB, m, s_cs[m])
                scale_grads(m)
            expert_part(block, m, i == 1)
            if i == nz - 1:
                give_back(m)
        if i == nz - 1:
            for m in range(M):
                exchange(YS, YB, m, s_y[m])
        expert_weights(block)
        sums_begin(i, (0, 1, 2) if i < nz - 1 else (0, 1, 3))

    r_fin, s_fin = (sems.take(nz), sems.take(1)), (sends.take(1), sends.take(1))
    FX = (b["FXI"], b["FXO"])
    GI, GT = b["GI"], b["GT"]
    sent_later(s_fin[0], FX[0])
    sent_later(s_fin[1], FX[1])

    def total_of(kind, place):
        return (
            OWN[kind][place].astype(F32)
            + UP[kind][place].astype(F32)
            + DN[kind][place].astype(F32)
        )

    def sums_end_in(k):
        cols = pl.ds(pl.multiple_of(k * FC, 128), FC)
        for side, ref, ok in ((0, UP, z > 0), (1, DN, z < nz - 1)):
            arrived(ref[0].at[k, z], r_up[side][0] + k * nz + z, ok)
        FX[0][k] = total_of(0, (k, z, 1 - x)).astype(BF16)
        send(FX[0].at[k], GI.at[x, :, cols], s_fin[0], r_fin[0] + k, across)
        GI[x, :, cols] = total_of(0, (k, z, x)).astype(BF16)

    def sums_end_out(mine):
        xx = x if mine else 1 - x
        for side, ref, ok in ((0, UP, z > 0), (1, DN, z < nz - 1)):
            arrived(ref[1].at[z, xx], r_up[side][1] + 2 * z + xx, ok)
        if mine:
            GT[x] = total_of(1, (z, xx)).astype(BF16)
        else:
            FX[1][...] = total_of(1, (z, xx)).astype(BF16)
            send(FX[1], GT.at[x], s_fin[1], r_fin[1], across)

    at_end = (z == 0) | (z == nz - 1)
    upper = z // h
    first_ends = [nz - 1 - upper * (nz - 1), 1 + upper * (nz - 3)]
    last_ends = [upper * (nz - 1), 2 - upper * (5 - nz)] if nz == 4 else []

    def sums_close():
        kept.append(fetch(GI.at[x], gein.at[x]))
        kept.append(fetch(GT.at[x], geout.at[x]))
        arrived(GT.at[1 - x], r_fin[1])
        kept.append(fetch(GT.at[1 - x], geout.at[1 - x]))
        for k in range(nz):
            arrived(GI.at[1 - x, :, k * FC : (k + 1) * FC], r_fin[0] + k)
        kept.append(fetch(GI.at[1 - x], gein.at[1 - x]))

    GM, GA, GJ, GR = b["GM"], b["GA"], b["GJ"], b["GR"]
    GR[...] = jnp.zeros_like(GR)

    def outputs(m):
        results = YB[m].reshape(S, D)
        out = MID[m] + chosen_of(m, 0) * nn(PM[m, 0], results)
        b["AR"][:, m, :] = (out + chosen_of(m, 1) * nn(PM[m, 1], results))[0:T]

    def backward_top(m):
        upstream = CT[m].astype(F32)
        for k in range(NE):
            CROW[0:1, k * CP : (k + 1) * CP] = GCB[m, k, 0:1, 0:CP]

        def grad_chosen(j):
            return jnp.sum(PM[m, j].astype(F32) * CROW[0:1], axis=-1, keepdims=True)

        gates = GATES[m]
        grad_gates = jnp.where(onehot(m, 0), grad_chosen(0), 0.0) + jnp.where(
            onehot(m, 1), grad_chosen(1), 0.0
        )
        grad_logits = (
            gates * (grad_gates - jnp.sum(grad_gates * gates, axis=-1, keepdims=True))
        ).astype(BF16)
        GR[0:NE] = GR[0:NE] + tn(grad_logits, N2[m])[0:NE]
        grad = nn(PM[m, 0] + PM[m, 1], DXB[m].reshape(S, D)) + nt(grad_logits, small)
        hat, rstd = normalize(MID[m])
        GR[NE + 1 : NE + 2] = GR[NE + 1 : NE + 2] + jnp.sum(grad * hat, axis=0, keepdims=True)
        grad_middle = upstream + normalize_back(grad * gain_two, hat, rstd)
        GM[m] = grad_middle
        branch = grad_middle.astype(BF16)
        N2[m] = branch
        back = None
        for cols, block in proj.blocks():
            term = nt(branch[:, cols], block)
            back = term if back is None else back + term
        GA[m] = back.astype(BF16)

    def backward_heads(m):
        def attend(hp, carry):
            query, keys, values = (J[m, :, columns(i * D, hp)] for i in range(3))
            grads = GA[m, :, columns(0, hp)]
            grad_query = jnp.zeros((TP, pair), F32)
            grad_keys = jnp.zeros((TP, pair), F32)
            grad_values = jnp.zeros((TP, pair), F32)
            for i in range(2):
                part = half_of(query, i)
                upstream = half_of(grads, i)
                probs_low = b["PB"][m, 2 * hp + i]
                probs = probs_low.astype(F32)
                grad_probs = nt(upstream, values)
                grad_values = grad_values + tn(probs_low, upstream)
                grad_scores = (
                    probs
                    * (grad_probs - jnp.sum(grad_probs * probs, axis=-1, keepdims=True))
                ).astype(BF16)
                grad_query = grad_query + nn(grad_scores, half_of(keys, i))
                grad_keys = grad_keys + tn(grad_scores, part)
            GJ[m, :, columns(0, hp)] = (grad_query * scale).astype(BF16)
            GJ[m, :, columns(D, hp)] = (grad_keys * scale).astype(BF16)
            GJ[m, :, columns(2 * D, hp)] = grad_values.astype(BF16)
            return carry

        lax.fori_loop(0, D // pair, attend, 0)

    def backward_end(m, carry):
        grad = None
        for cols, block in qkv.blocks():
            term = nt(GJ[m, :, cols], block)
            grad = term if grad is None else grad + term
        hat, rstd = normalize(XP[m].astype(F32))
        GR[NE : NE + 1] = GR[NE : NE + 1] + jnp.sum(grad * hat, axis=0, keepdims=True)
        full = GM[m] + normalize_back(grad * gain_one, hat, rstd)
        b["IG"][m, :, 0, :] = full[0:T]
        return carry

    if nz <= 4:
        pass_out(0, 1, True)
    sums_now((1, 1, 0), (2, 0, 0))
    for m in range(M):
        exchanged(DXB, m, s_dx[m])
        exchanged(GCB, m, s_gc[m])
        backward_top(m)
        if m == 0:
            sums_now((1, 1, 1))
        if m == M - 1:
            proj.put(b["ATTT"], N2)
            proj.sum_core()
            sums_now((1, 2, 1))
        backward_heads(m)
        if m == 0:
            sums_now((2, 0, 1), (2, 0, 2), (1, 1, 2), (2, 1, 0))
    sums_now((1, 2, 2))
    proj.sum_plane()
    qkv.put(b["N1T"], GJ)
    GB, SB1, SB2, SB3, SB4 = (b[k] for k in ("GB", "SB1", "SB2", "SB3", "SB4"))
    qkv.sum_core()
    lax.fori_loop(0, M, backward_end, 0)
    kept.append(fetch(b["IG"], igrad))
    GB[...] = GR[...].astype(BF16)
    r_b1 = one_send(GB, SB1, sibling)
    qkv.sum_plane()
    proj.sum_cross()
    arrived(SB1, r_b1)
    SB2[y] = GB[...] + SB1[...]
    s_b2, r_b2 = sends.take(G - 1) - 1, sems.take(G - 1) - 1
    for d in range(1, G):
        send(SB2.at[y], SB2.at[y], s_b2 + d, r_b2 + d, at(z, x, ((y + d) % G) * 2 + core))
        sent_later(s_b2 + d, SB2.at[y])
    sums_now((2, 1, 1), (2, 1, 2), (2, 2, 1), (1, 2, 0), (2, 2, 2))
    if nz == 4:

        @pl.when(at_end)
        def _():
            for k in first_ends:
                sums_end_in(k)

    for d in range(1, G):
        arrived(SB2.at[(y + G - d) % G], r_b2 + d)
    total = SB2[0].astype(F32)
    for j in range(1, G):
        total = total + SB2[j].astype(F32)
    SB3[x] = total.astype(BF16)
    r_b3 = one_send(SB3.at[x], SB3.at[x], across)
    qkv.sum_cross()
    proj.sum_z()
    if nz == 4:
        pl.when(at_end)(functools.partial(sums_end_out, False))
    sums_now((1, 3, 0), (1, 3, 1), (1, 3, 2), (2, 2, 0))
    qkv.sum_z()
    arrived(SB3.at[1 - x], r_b3)
    SB4[z] = SB3[0] + SB3[1]
    s_b4, r_b4 = sends.take(1), sems.take(1)
    for dz in orders:
        send(SB4.at[z], SB4.at[z], s_b4, r_b4, at((z + dz) % nz, x, e))
    sent_later(s_b4, SB4.at[0 : nz - 1])
    sums_begin(nz - 1, (4,))
    sums_rest()
    if nz != 4:
        sums_end_out(False)
    else:

        @pl.when(at_end)
        def _():
            for k in last_ends:
                sums_end_in(k)

        @pl.when(jnp.logical_not(at_end))
        def _():
            sums_end_out(False)
            for k in (0, nz - 1):
                sums_end_in(k)

    proj.hand_out()
    qkv.hand_out()
    if nz == 4:

        @pl.when(jnp.logical_not(at_end))
        def _():
            for k in range(1, nz - 1):
                sums_end_in(k)

    else:
        for k in range(nz):
            sums_end_in(k)
    for m in range(M):
        exchanged(YB, m, s_y[m])
        outputs(m)
    b["AO"][...] = b["AR"][...].astype(BF16)
    kept.append(fetch(b["AO"], act))
    arrived(SB4.at[0 : nz - 1], r_b4)
    total = SB4[0].astype(F32)
    for k in range(1, nz):
        total = total + SB4[k].astype(F32)
    mine = (
        lax.broadcasted_iota(jnp.int32, (D, RF), 0)
        == lax.broadcasted_iota(jnp.int32, (D, RF), 1) + f * RF
    ).astype(F32)
    b["GS"][...] = lax.dot_general(
        total,
        mine,
        (((1,), (0,)), ((), ())),
        precision=lax.Precision.HIGHEST,
        preferred_element_type=F32,
    )
    kept.append(fetch(b["GS"].at[0:NE], grouter))
    kept.append(fetch(b["GS"].at[NE : NE + 1], ggain1))
    kept.append(fetch(b["GS"].at[NE + 1 : NE + 2], ggain2))
    sums_end_out(True)
    sums_close()
    proj.leave(gout)
    qkv.leave(gqkv)
    for cond, copy in pending:
        when(cond, copy.wait_send)
    for copy in kept:
        copy.wait()
    used = (sends.used, sems.used, locals_.used)
    assert all(a <= b for a, b in zip(used, counts)), (used, counts)


def hand_over(*refs):
    source, target, held, sem = refs[:9], refs[9:18], refs[18:-1], refs[-1]
    cast = [k for k in range(9) if source[k].dtype != target[k].dtype]
    order = sorted(range(9), key=lambda k: -math.prod(target[k].shape))
    for k in order:
        pltpu.make_async_copy(source[k], held[k], sem.at[0, k]).start()
    for k in order:
        pltpu.make_async_copy(source[k], held[k], sem.at[0, k]).wait()
        ready = held[k]
        if k in cast:
            ready = held[9 + cast.index(k)]
            ready[...] = held[k][...].astype(ready.dtype)
        pltpu.make_async_copy(ready, target[k], sem.at[1, k]).start()
    for k in order:
        pltpu.make_async_copy(target[k], target[k], sem.at[1, k]).wait()


def body(
    mesh_shape,
    inputs,
    gain_attn,
    qkv_weight,
    out_weight,
    gain_moe,
    router_weight,
    expert_in,
    expert_out,
    routes,
    cotangent,
):
    micro, images, seq, width = inputs.shape
    c = layout(mesh_shape, micro, images * seq, width, expert_in.shape[2])
    rows = images * seq
    scratch = scratch_of(c)
    names = list(scratch)
    nz, G = c["nz"], c["G"]
    counts = (48 + 9 * (G - 1), 25 + 19 * nz + 2 * nz * nz + 9 * (G - 1), 19 + 2 * c["E"])
    shapes = (
        ((rows, micro, width), BF16),
        ((micro, rows, 1, width), F32),
        (qkv_weight.shape, F32),
        (out_weight.shape, F32),
        ((1, c["RF"]), F32),
        ((1, c["RF"]), F32),
        ((c["NE"], c["RF"]), F32),
        (expert_in.shape, F32),
        (expert_out.shape, F32),
    )
    shapes = [jax.ShapeDtypeStruct(s, t) for s, t in shapes]
    sums = (2, 3, 7, 8)
    halves = [
        jax.ShapeDtypeStruct(s.shape, BF16 if k in sums else s.dtype) for k, s in enumerate(shapes)
    ]
    anywhere = pl.BlockSpec(memory_space=pltpu.HBM)
    results = pl.pallas_call(
        functools.partial(kernel, c, names, counts),
        out_shape=halves,
        in_specs=[anywhere] * 10,
        out_specs=[anywhere] * 9,
        scratch_shapes=[pltpu.VMEM(s, t) for s, t in scratch.values()]
        + [pltpu.SemaphoreType.DMA((count,)) for count in counts],
        compiler_params=pltpu.CompilerParams(
            collective_id=0, has_side_effects=True, vmem_limit_bytes=60 * 1024 * 1024
        ),
    )(
        jnp.transpose(inputs, (1, 2, 0, 3)).reshape(rows, micro, width),
        jnp.transpose(cotangent, (1, 2, 0, 3)).reshape(rows, micro, width),
        jnp.transpose(routes, (0, 1, 3, 2)).reshape(micro, 2, rows),
        qkv_weight,
        out_weight,
        gain_attn[None, :],
        gain_moe[None, :],
        router_weight.T,
        expert_in,
        expert_out,
    )
    act, igrad, gqkv, gout, ggain1, ggain2, grouter, gein, geout = pl.pallas_call(
        hand_over,
        out_shape=shapes,
        in_specs=[anywhere] * 9,
        out_specs=[anywhere] * 9,
        scratch_shapes=[pltpu.VMEM(s.shape, s.dtype) for s in halves]
        + [pltpu.VMEM(shapes[k].shape, F32) for k in sums]
        + [pltpu.SemaphoreType.DMA((2, 9))],
        compiler_params=pltpu.CompilerParams(vmem_limit_bytes=60 * 1024 * 1024),
    )(*results)
    return (
        jnp.transpose(act.reshape(images, seq, micro, width), (2, 0, 1, 3)),
        igrad.reshape(inputs.shape),
        ggain1[0],
        gqkv,
        gout,
        ggain2[0],
        grouter.T,
        gein,
        geout,
    )


def solution(mesh):
    return jax.shard_map(
        functools.partial(body, dict(mesh.shape)),
        mesh=mesh,
        in_specs=(
            P(None, ("fsdp", "expert"), None, None),
            P("fsdp"),
            P("fsdp", None),
            P("fsdp", None),
            P("fsdp"),
            P("fsdp", None),
            P("expert", "fsdp", None),
            P("expert", "fsdp", None),
            P(None, ("fsdp", "expert"), None, None),
            P(None, ("fsdp", "expert"), None, None),
        ),
        out_specs=(
            P(None, ("fsdp", "expert"), None, None),
            P(None, ("fsdp", "expert"), None, None),
            P("fsdp"),
            P("fsdp", None),
            P("fsdp", None),
            P("fsdp"),
            P("fsdp", None),
            P("expert", "fsdp", None),
            P("expert", "fsdp", None),
        ),
        check_vma=False,
    )
```

```python
import functools
import math

import jax
import jax.numpy as jnp
from jax import lax
from jax.experimental import pallas as pl
from jax.experimental.pallas import tpu as pltpu
from jax.sharding import PartitionSpec as P

HEADS = 8
EPS = 1e-06
MESH = pl.DeviceIdType.MESH
F32 = jnp.float32
BF16 = jnp.bfloat16


def nn(a, b):
    return lax.dot_general(a, b, (((1,), (0,)), ((), ())), preferred_element_type=F32)


def nt(a, b):
    return lax.dot_general(a, b, (((1,), (1,)), ((), ())), preferred_element_type=F32)


def tn(a, b):
    return lax.dot_general(a, b, (((0,), (0,)), ((), ())), preferred_element_type=F32)


def normalize(values):
    center = jnp.mean(values, axis=-1, keepdims=True)
    shifted = values - center
    spread = jnp.mean(shifted * shifted, axis=-1, keepdims=True)
    rstd = lax.rsqrt(spread + EPS)
    return shifted * rstd, rstd


def normalize_back(grad, hat, rstd):
    return rstd * (
        grad
        - jnp.mean(grad, axis=-1, keepdims=True)
        - hat * jnp.mean(grad * hat, axis=-1, keepdims=True)
    )


class Semaphores:
    def __init__(self):
        self.used = 0

    def take(self, count):
        start = self.used
        self.used += count
        return start


SIZES = ("nz", "E", "G", "NE", "NR", "T", "TP", "CP", "S", "D", "FC", "RF", "CF", "M")


def layout(mesh_shape, micro, seq, width, ff_width):
    fsdp, peers = mesh_shape["fsdp"], mesh_shape["expert"]
    c = {}
    c["nz"] = fsdp // 2
    c["E"] = peers
    c["G"] = peers // 2
    c["NE"] = 2 * peers
    c["T"] = seq
    c["TP"] = -(-seq // 16) * 16
    c["CP"] = -(-max(2, 10 * seq // (4 * 2 * peers) + 1) // 16) * 16
    c["S"] = c["NE"] * c["CP"]
    c["NR"] = -(-(c["NE"] + 2) // 16) * 16
    c["D"] = width
    c["FF"] = ff_width
    c["RF"] = width // fsdp
    c["CF"] = ff_width // fsdp
    c["FC"] = 2 * c["CF"]
    c["WQ"] = 128 * -(-(3 * width // 128) // peers)
    c["WO"] = 128 * -(-(width // 128) // peers)
    c["M"] = micro
    return c


def scratch_of(c):
    nz, E, G, NE, NR, T, TP, CP, S, D, FC, RF, CF, M = (c[k] for k in SIZES)
    h = nz // 2
    v = {
        "XP": ((M, TP, D), BF16),
        "CT": ((M, TP, D), BF16),
        "XR": ((T, M, D), BF16),
        "CR": ((T, M, D), BF16),
        "AR": ((T, M, D), F32),
        "AO": ((T, M, D), BF16),
        "IG": ((M, T, 1, D), F32),
        "RR": ((M, 2, T), jnp.int32),
        "RT": ((M, TP, 128), F32),
        "SR": ((nz, 2, NR, RF), BF16),
        "G1": ((1, RF), BF16),
        "G2": ((1, RF), BF16),
        "RW": ((NE, RF), BF16),
        "GI": ((2, RF, nz * FC), BF16),
        "GT": ((2, CF, D), BF16),
        "GS": ((NR, RF), F32),
        "SM": ((nz, 2, RF, 128), BF16),
        "WIN": ((nz, nz, 2, RF, FC), BF16),
        "WOUT": ((nz, 2, CF, D), BF16),
        "N1": ((M, TP, D), BF16),
        "J": ((M, TP, 3 * D), BF16),
        "ATT": ((M, TP, D), BF16),
        "MID": ((M, TP, D), F32),
        "N2": ((M, TP, D), BF16),
        "GATES": ((M, TP, 128), F32),
        "PB": ((M, HEADS, TP, TP), BF16),
        "N1T": ((M, D, TP), BF16),
        "ATTT": ((M, D, TP), BF16),
        "PM": ((M, 2, TP, S), BF16),
        "XS": ((M, NE, CP, D), BF16),
        "XB": ((M, NE, CP, D), BF16),
        "GSS": ((M, NE, CP, D), BF16),
        "GRB": ((M, NE, CP, D), BF16),
        "CSS": ((M, NE, 8, 128), F32),
        "CSB": ((M, NE, 8, 128), F32),
        "CROW": ((8, S), F32),
        "GC": ((M, S, D), BF16),
        "YB": ((M, NE, CP, D), BF16),
        "DXB": ((M, NE, CP, D), BF16),
        "GCS": ((M, NE, 8, 128), F32),
        "GCB": ((M, NE, 8, 128), F32),
        "YACC": ((M, S, D), F32),
        "DXACC": ((M, S, D), F32),
        "AS": ((M, S, FC), BF16),
        "GHS": ((M, S, FC), BF16),
        "DWI": ((nz, nz, 2, RF, FC), BF16),
        "DWO": ((nz, 2, CF, D), BF16),
        "UPI": ((nz, nz, 2, RF, FC), BF16),
        "UPO": ((nz, 2, CF, D), BF16),
        "DNI": ((nz, nz, 2, RF, FC), BF16),
        "DNO": ((nz, 2, CF, D), BF16),
        "FXI": ((nz, RF, FC), BF16),
        "FXO": ((CF, D), BF16),
        "GM": ((M, TP, D), F32),
        "GA": ((M, TP, D), BF16),
        "GJ": ((M, TP, 3 * D), BF16),
        "GR": ((NR, D), F32),
        "GB": ((NR, D), BF16),
        "SB1": ((NR, D), BF16),
        "SB2": ((G, NR, D), BF16),
        "SB3": ((2, NR, D), BF16),
        "SB4": ((nz, NR, D), BF16),
    }
    for name, wide in (("Q", c["WQ"]), ("O", c["WO"])):
        for part, lead in (
            ("W", (E, nz, 2)),
            ("G", (E, nz, 2)),
            ("B1", (G, nz, 2)),
            ("Y1", (G, h, 2)),
            ("X1", (G, nz - h)),
            ("X2", (h,)),
            ("Y2", (G, nz - h)),
            ("Z", (nz,)),
            ("F", (E,)),
        ):
            v[name + part] = (lead + (RF, wide), BF16)
    return v


def kernel(c, names, counts, *refs):
    nz, E, G, NE, NR, T, TP, CP, S, D, FC, RF, CF, M = (c[k] for k in SIZES)
    (xin, cot, routes, qkv_s, out_s, gain1, gain2, router, ein, eout) = refs[:10]
    (act, igrad, gqkv, gout, ggain1, ggain2, grouter, gein, geout) = refs[10:19]
    b = dict(zip(names, refs[19:]))
    SS, RS, LS = refs[-3:]
    h = nz // 2
    head = D // HEADS
    pair = 2 * head
    scale = 1.0 / math.sqrt(head)
    sems, sends, locals_ = Semaphores(), Semaphores(), Semaphores()
    pending = []

    f = lax.axis_index("fsdp")
    e = lax.axis_index("expert")
    z, x = f // 2, f % 2
    y, core = e // 2, e % 2
    pme = 2 * e + x

    def at(zz, xx, ee):
        return (zz * 2 + xx, ee)

    sibling = at(z, x, y * 2 + (1 - core))
    across = at(z, 1 - x, e)

    def copy_of(src, dst, ssem, rsem, device):
        return pltpu.make_async_remote_copy(
            src_ref=src,
            dst_ref=dst,
            send_sem=SS.at[ssem],
            recv_sem=RS.at[rsem],
            device_id=device,
            device_id_type=MESH,
        )

    def when(cond, run):
        if cond is None:
            run()
        else:
            pl.when(cond)(run)

    def send(src, dst, ssem, rsem, device, cond=None):
        when(cond, copy_of(src, dst, ssem, rsem, device).start)

    def arrived(dst, rsem, cond=None):
        when(cond, copy_of(dst, dst, 0, rsem, sibling).wait_recv)

    def sent_later(ssem, src, cond=None):
        pending.append((cond, copy_of(src, src, ssem, 0, sibling)))

    def one_send(src, dst, device):
        ssem, rsem = sends.take(1), sems.take(1)
        send(src, dst, ssem, rsem, device)
        sent_later(ssem, src)
        return rsem

    barrier = pltpu.get_barrier_semaphore()
    for dz in range(1, nz):
        pl.semaphore_signal(
            barrier, inc=1, device_id=at((z + dz) % nz, x, e), device_id_type=MESH
        )

    def greet(d, carry):
        p = (pme + d) % NE
        pl.semaphore_signal(barrier, inc=1, device_id=at(z, p % 2, p // 2), device_id_type=MESH)
        return carry

    lax.fori_loop(1, NE, greet, 0)

    SM, WIN, WOUT = b["SM"], b["WIN"], b["WOUT"]
    UP, DN = (b["UPI"], b["UPO"]), (b["DNI"], b["DNO"])

    def fetch(src, dst):
        copy = pltpu.make_async_copy(src, dst, LS.at[locals_.take(1)])
        copy.start()
        return copy

    near_first = [d for k in range(1, nz) for d in (k, nz - k) if 2 * k <= nz]
    orders = list(dict.fromkeys(near_first))
    far_first = [j + (1 - z // h) * (nz - 2 * j) for j in range(1, nz)]

    class Dense:
        def __init__(self, name, shard, wide):
            self.name, self.shard, self.wide = name, shard, wide
            self.w, self.g = b[name + "W"], b[name + "G"]
            self.used = -(-shard.shape[1] // wide)
            self.own = locals_.take(1)
            for k in range(self.used):

                @pl.when(e == k)
                def _():
                    pltpu.make_async_copy(
                        self.columns(shard, k), self.w.at[k, z, x], LS.at[self.own]
                    ).start()

        def columns(self, ref, k):
            return ref.at[:, k * self.wide : (k + 1) * self.wide]

        def own_ready(self):
            copy = pltpu.make_async_copy(
                self.w.at[e, z, x], self.w.at[e, z, x], LS.at[self.own]
            )
            when(None if self.used == E else e < self.used, copy.wait)

        def along_z(self):
            w = self.w
            self.r_z, s_z = sems.take(nz - 1) - 1, sends.take(1)
            for dz in orders:
                to = at((z + dz) % nz, x, e)
                send(w.at[e, z, x], w.at[e, z, x], s_z, self.r_z + dz, to)
            sent_later(s_z, w.at[e, 0 : nz - 1, x])
            self.s_x, self.r_x = sends.take(1), sems.take(nz)
            self.s_y, self.r_y = sends.take(G - 1) - 1, sems.take(G - 1) - 1
            self.s_c, self.r_c = sends.take(1), sems.take(1)
            sent_later(self.s_x, w.at[e, :, x])
            for d in range(1, G):
                sent_later(self.s_y + d, w.at[e, :, x])
            sent_later(self.s_c, w.at[0:G])

        def spread(self, dz):
            zz = (z + nz - dz) % nz
            piece = self.w.at[e, zz, x]
            if dz > 0:
                arrived(piece, self.r_z + dz)
            send(piece, piece, self.s_x, self.r_x + dz, across)
            for d in range(1, G):
                to = at(z, x, ((y + d) % G) * 2 + core)
                send(piece, piece, self.s_y + d, self.r_y + d, to)
            send(piece, piece, self.s_c, self.r_c, sibling)

        def forward(self):
            w = self.w
            self.s_xy, self.r_xy = sends.take(G - 1) - 1, sems.take(G - 1) - 1
            for d in range(1, G):
                sent_later(self.s_xy + d, w.at[e, :, x])
            for dz in [0] + orders:
                piece = w.at[e, (z + nz - dz) % nz, 1 - x]
                arrived(piece, self.r_x + dz)
                for d in range(1, G):
                    to = at(z, x, ((y + d) % G) * 2 + core)
                    send(piece, piece, self.s_xy + d, self.r_xy + d, to)
                send(piece, piece, self.s_c, self.r_c, sibling)

        def corner(self):
            w = self.w
            for d in range(1, G):
                ee = ((y + G - d) % G) * 2 + core
                arrived(w.at[ee, :, x], self.r_y + d)
                send(w.at[ee, :, x], w.at[ee, :, x], self.s_c, self.r_c, sibling)
                arrived(w.at[ee, :, 1 - x], self.r_xy + d)
                send(w.at[ee, :, 1 - x], w.at[ee, :, 1 - x], self.s_c, self.r_c, sibling)

        def ready(self):
            arrived(self.w.at[0:G], self.r_c)

        def blocks(self):
            for k in range(self.used):
                cols = slice(k * self.wide, min((k + 1) * self.wide, self.shard.shape[1]))
                yield cols, self.w[k].reshape(D, self.wide)

        def put(self, left, right):
            for k in range(self.used):
                cols = slice(k * self.wide, (k + 1) * self.wide)
                part = nn(left[0], right[0, :, cols])
                for m in range(1, M):
                    part = part + nn(left[m], right[m, :, cols])
                self.g[k] = part.astype(BF16).reshape(nz, 2, RF, self.wide)

        def sum_core(self):
            s, self.r_1 = sends.take(1), sems.take(1)
            for j in range(G):
                send(self.g.at[2 * j + 1 - core], b[self.name + "B1"].at[j], s, self.r_1, sibling)
            sent_later(s, b[self.name + "B1"])

        def sum_plane(self):
            g, first = self.g, b[self.name + "B1"]
            arrived(first, self.r_1)
            for j in range(G):
                g[2 * j + core] = g[2 * j + core] + first[j]
            s, self.r_y1 = sends.take(G - 1) - 1, sems.take(G - 1) - 1
            for d in range(1, G):
                q = (y + d) % G
                piece = g.at[2 * q + core, 0:h]
                send(piece, b[self.name + "Y1"].at[y], s + d, self.r_y1 + d, at(z, x, 2 * q + core))
                sent_later(s + d, piece)
            s, self.r_x1 = sends.take(1), sems.take(1)
            for j in range(G):
                piece = g.at[2 * j + core, h:nz, 1 - x]
                send(piece, b[self.name + "X1"].at[j], s, self.r_x1, across)
            sent_later(s, b[self.name + "X1"])

        def sum_cross(self):
            g, from_y, from_x = self.g, b[self.name + "Y1"], b[self.name + "X1"]
            for d in range(1, G):
                q = (y + G - d) % G
                arrived(from_y.at[q], self.r_y1 + d)
                g[e, 0:h] = g[e, 0:h] + from_y[q]
            self.r_x2 = one_send(g.at[e, 0:h, 1 - x], b[self.name + "X2"], across)
            arrived(from_x, self.r_x1)
            for j in range(G):
                g[2 * j + core, h:nz, x] = g[2 * j + core, h:nz, x] + from_x[j]
            s, self.r_y2 = sends.take(G - 1) - 1, sems.take(G - 1) - 1
            for d in range(1, G):
                q = (y + d) % G
                piece = g.at[2 * q + core, h:nz, x]
                send(piece, b[self.name + "Y2"].at[y], s + d, self.r_y2 + d, at(z, x, 2 * q + core))
                sent_later(s + d, piece)

        def sum_z(self):
            g, from_x, from_y = self.g, b[self.name + "X2"], b[self.name + "Y2"]
            arrived(from_x, self.r_x2)
            g[e, 0:h, x] = g[e, 0:h, x] + from_x[...]
            for d in range(1, G):
                q = (y + G - d) % G
                arrived(from_y.at[q], self.r_y2 + d)
                g[e, h:nz, x] = g[e, h:nz, x] + from_y[q]
            s, self.r_z2 = sends.take(1), sems.take(1)
            parts = b[self.name + "Z"]
            for dz in far_first:
                zz = (z + dz) % nz
                send(g.at[e, zz, x], parts.at[z], s, self.r_z2, at(zz, x, e))
            sent_later(s, parts.at[0 : nz - 1])
            parts[z] = g[e, z, x]

        def hand_out(self):
            parts, done = b[self.name + "Z"], b[self.name + "F"]
            arrived(parts.at[0 : nz - 1], self.r_z2)
            total = parts[0].astype(F32)
            for k in range(1, nz):
                total = total + parts[k].astype(F32)
            done[e] = total.astype(BF16)
            s, self.r_f = sends.take(1), sems.take(1)

            def one(d, carry):
                send(done.at[e], done.at[e], s, self.r_f, at(z, x, (e + d) % E))
                return carry

            lax.fori_loop(1, E, one, 0)
            sent_later(s, done.at[0 : E - 1])

        def leave(self, out):
            done = b[self.name + "F"]
            arrived(done.at[0 : E - 1], self.r_f)
            for k in range(self.used):
                kept.append(fetch(done.at[k], self.columns(out, k)))

    qkv, proj = Dense("Q", qkv_s, c["WQ"]), Dense("O", out_s, c["WO"])
    kept = []

    SR = b["SR"]
    SR[z, x] = jnp.zeros((NR, RF), BF16)
    small_in = [
        fetch(gain1, b["G1"]),
        fetch(gain2, b["G2"]),
        fetch(router, b["RW"]),
    ]
    token_in = [fetch(routes, b["RR"]), fetch(xin, b["XR"]), fetch(cot, b["CR"])]
    own_in = locals_.take(1)
    for k in range(nz):
        pltpu.make_async_copy(
            ein.at[x, :, k * FC : (k + 1) * FC], WIN.at[k, z, x], LS.at[own_in]
        ).start()
    own_out = fetch(eout.at[x], WOUT.at[z, x])

    for copy in small_in:
        copy.wait()
    SR[z, x, 0:NE] = b["RW"][...]
    SR[z, x, NE : NE + 1] = b["G1"][...]
    SR[z, x, NE + 1 : NE + 2] = b["G2"][...]
    entry = lax.broadcasted_iota(jnp.int32, (NR, 128), 0)
    place = lax.broadcasted_iota(jnp.int32, (NR, 128), 1)
    pick = (
        ((entry < NE) & (entry == place))
        | ((entry >= NE) & (entry < NE + 2) & (place == entry - NE + 126))
    ).astype(BF16)
    qkv.own_ready()
    proj.own_ready()
    pl.semaphore_wait(barrier, nz - 1 + NE - 1)

    qkv.along_z()
    r_sz, s_sz = sems.take(1), sends.take(1)
    for dz in orders:
        send(SR.at[z, x], SR.at[z, x], s_sz, r_sz, at((z + dz) % nz, x, e))
    sent_later(s_sz, SR.at[0 : nz - 1, x])
    qkv.spread(0)

    s_xi, r_xi = sends.take(1), sems.take(1)
    for k in range(nz):
        send(ein.at[1 - x, :, k * FC : (k + 1) * FC], WIN.at[k, z, x], s_xi, r_xi, across)
    sent_later(s_xi, WIN.at[:, z, x])


    XP, CT, RT, PM = b["XP"], b["CT"], b["RT"], b["PM"]

    @pl.when(z == 0)
    def _():
        UP[0][:, 0] = jnp.zeros((nz, 2, RF, FC), BF16)
        UP[1][0] = jnp.zeros((2, CF, D), BF16)

    @pl.when(z == nz - 1)
    def _():
        DN[0][:, nz - 1] = jnp.zeros((nz, 2, RF, FC), BF16)
        DN[1][nz - 1] = jnp.zeros((2, CF, D), BF16)

    for copy in token_in:
        copy.wait()
    lane = lax.broadcasted_iota(jnp.int32, (TP, 128), 1)
    lane_f = lane.astype(F32)
    swap = (
        lax.broadcasted_iota(jnp.int32, (2, 128), 0) == lax.broadcasted_iota(jnp.int32, (2, 128), 1)
    ).astype(BF16)
    for m in range(M):
        XP[m] = jnp.zeros((TP, D), BF16)
        CT[m] = jnp.zeros((TP, D), BF16)
        RT[m] = jnp.full((TP, 128), -1.0, F32)
        XP[m, 0:T] = b["XR"][:, m, :]
        CT[m, 0:T] = b["CR"][:, m, :]
        RT[m, 0:T] = tn(b["RR"][m].astype(BF16), swap)

    def onehot(m, j):
        return RT[m][:, j : j + 1] == lane_f

    before = (
        lax.broadcasted_iota(jnp.int32, (TP, TP), 1) < lax.broadcasted_iota(jnp.int32, (TP, TP), 0)
    ).astype(BF16)
    spots = lax.broadcasted_iota(jnp.int32, (TP, S), 1).astype(F32)
    for m in range(M):
        first = onehot(m, 0).astype(F32)
        second = onehot(m, 1).astype(F32)
        rank0 = nn(before, first.astype(BF16))
        rank1 = nn(before, second.astype(BF16)) + jnp.sum(first, axis=0, keepdims=True)
        for j, (hot, rank) in enumerate(((first, rank0), (second, rank1))):
            slot = jnp.sum(hot * rank, axis=-1, keepdims=True)
            route = RT[m][:, j : j + 1]
            spot = jnp.where(route >= 0, route * CP + slot, -1.0)
            PM[m, j] = (spots == spot).astype(BF16)

    def turn_of(i):
        return 0 if i == 0 else i % (nz - 1) + 1

    groups = (range(0, 2), range(2, nz))
    s_zi = [[sends.take(1) for _ in groups] for _ in range(2)]
    s_zo = [sends.take(1) for _ in range(2)]
    r_zi = [[sems.take(nz) for _ in groups] for _ in range(2)]
    r_zo = [sems.take(2 * nz) for _ in range(2)]
    for zz in range(nz):
        for side in range(2):
            count = zz + 1 if side == 0 else nz - zz
            if count < nz:
                for g, turns in enumerate(groups):
                    sent_later(s_zi[side][g], WIN.at[0 : len(turns), 0:count], z == zz)
                sent_later(s_zo[side], WOUT.at[0:count], z == zz)

    def reach(side, d, some=None):
        begun = z - d if side == 0 else z + d
        there = (begun >= 0) if side == 0 else (begun < nz)
        last = (z == nz - 1) if side == 0 else (z == 0)
        if some is not None:
            there = there & some(begun)
        return begun, there, there & jnp.logical_not(last)

    def onward(side):
        return at((z + 1) % nz if side == 0 else (z + nz - 1) % nz, x, e)

    def pass_in(g, d, halves=(0, 1)):
        for side in range(2):
            begun, there, goes = reach(side, d)
            r = r_zi[side][g]
            if d > 0:
                arrived(WIN.at[0 : len(groups[g]), begun], r + d, there)
            if d < nz - 1:

                @pl.when(goes)
                def _():
                    for i in groups[g]:
                        k = turn_of(i) if side == 1 else nz - 1 - turn_of(i)
                        for half in halves:
                            piece = WIN.at[k, begun, x if half == 0 else 1 - x]
                            send(piece, piece, s_zi[side][g], r + d + 1, onward(side))

    def pass_out(d, half, late=None):
        xx = x if half == 0 else 1 - x
        for side in range(2):
            odd = nz - 2 if side == 0 else 1
            some = None
            if late is not None:
                some = (lambda begun: begun == odd) if late else (lambda begun: begun != odd)
            begun, there, goes = reach(side, d, some)
            r = r_zo[side] + 2 * d + half
            piece = WOUT.at[begun, xx]
            if d > 0:
                arrived(piece, r, there)
            if d < nz - 1:
                send(piece, piece, s_zo[side], r + 2, onward(side), goes)

    early, others = 0, 1
    GATES, XS, XB, GC, CROW = (b[k] for k in ("GATES", "XS", "XB", "GC", "CROW"))
    GSS, GRB, CSS, CSB = (b[k] for k in ("GSS", "GRB", "CSS", "CSB"))
    GCS, GCB, YB, DXB = (b[k] for k in ("GCS", "GCB", "YB", "DXB"))
    YS, DXS = XS, GSS

    def gone(src, m, sem):
        copy_of(src.at[m, 0 : NE - 1], src.at[m, 0 : NE - 1], sem[0], 0, sibling).wait_send()

    def exchange(src, dst, m, sem, later=True):
        rows = slice(0, 1 if src.shape[2] == 8 else src.shape[2])

        def one(d, carry):
            p = (pme + d) % NE
            send(src.at[m, p, rows], dst.at[m, pme, rows], *sem, at(z, p % 2, p // 2))
            return carry

        lax.fori_loop(1, NE, one, 0)
        if later:
            sent_later(sem[0], src.at[m, 0 : NE - 1, rows])
        dst[m, pme] = src[m, pme]

    def exchanged(dst, m, sem):
        rows = slice(0, 1 if dst.shape[2] == 8 else dst.shape[2])
        arrived(dst.at[m, 0 : NE - 1, rows], sem[1])

    def pairs():
        return [(sends.take(1), sems.take(1)) for _ in range(M)]

    s_x, s_cs, s_gr, s_dx, s_gc, s_y = (pairs() for _ in range(6))
    for m in range(M):
        GSS[m] = tn(PM[m, 0] + PM[m, 1], CT[m]).astype(BF16).reshape(NE, CP, D)

    for dz in orders[:2]:
        qkv.spread(dz)
    proj.along_z()
    proj.spread(0)
    pltpu.make_async_copy(WIN.at[:, z, x], WIN.at[:, z, x], LS.at[own_in]).wait()
    pass_in(early, 0, (0,))
    for dz in orders[2:]:
        qkv.spread(dz)
    arrived(SR.at[0 : nz - 1, x], r_sz)
    r_sx = one_send(SR.at[:, x], SR.at[:, x], across)
    own_out.wait()
    pass_out(0, 0)
    arrived(WIN.at[:, z, 1 - x], r_xi)
    pass_in(early, 0, (1,))
    qkv.forward()
    for dz in orders:
        proj.spread(dz)
    proj.forward()
    r_xo = one_send(eout.at[1 - x], WOUT.at[z, x], across)
    for m in range(M):
        exchange(GSS, GRB, m, s_gr[m], False)
    pass_in(others, 0, (0,))
    arrived(SR.at[:, 1 - x], r_sx)
    for zz in range(nz):
        for xx in range(2):
            SM[zz, xx] = tn(SR[zz, xx], pick).astype(BF16)
    qkv.corner()
    qkv.ready()

    small = SM[...].reshape(D, 128)
    gains = nt(pick, small)
    gain_one, gain_two = gains[NE : NE + 1], gains[NE + 1 : NE + 2]
    key_ok = lax.broadcasted_iota(jnp.int32, (1, TP), 1) < T
    low_half = lax.broadcasted_iota(jnp.int32, (1, pair), 1) < head
    N1, J, ATT, MID, N2 = b["N1"], b["J"], b["ATT"], b["MID"], b["N2"]
    def half_of(value, i):
        keep = low_half if i == 0 else jnp.logical_not(low_half)
        return jnp.where(keep, value, jnp.zeros_like(value))

    def softmax_scores(query, keys):
        scores = jnp.where(key_ok, nt(query, keys) * scale, -1e30)
        raised = jnp.exp(scores - jnp.max(scores, axis=-1, keepdims=True))
        return raised * (1.0 / jnp.sum(raised, axis=-1, keepdims=True))

    def columns(base, hp):
        return pl.ds(pl.multiple_of(base + hp * pair, 128), pair)

    def chosen_of(m, j):
        gates = GATES[m]
        return jnp.sum(jnp.where(onehot(m, j), gates, 0.0), axis=-1, keepdims=True)

    def forward(m):
        tokens = XP[m].astype(F32)
        hat, _ = normalize(tokens)
        N1[m] = (hat * gain_one).astype(BF16)
        for cols, block in qkv.blocks():
            J[m, :, cols] = nn(N1[m], block).astype(BF16)

        def attend(hp, carry):
            query, keys, values = (J[m, :, columns(i * D, hp)] for i in range(3))
            total = jnp.zeros((TP, pair), F32)
            for i in range(2):
                probs = softmax_scores(half_of(query, i), keys)
                probs = probs.astype(BF16)
                b["PB"][m, 2 * hp + i] = probs
                total = total + nn(probs, half_of(values, i))
            ATT[m, :, columns(0, hp)] = total.astype(BF16)
            return carry

        lax.fori_loop(0, D // pair, attend, 0)
        if m == 0:
            pass_in(early, 1)
            pass_in(others, 0, (1,))
            proj.corner()
            proj.ready()
        for cols, block in proj.blocks():
            MID[m, :, cols] = XP[m, :, cols].astype(F32) + nn(ATT[m], block)
        hat, _ = normalize(MID[m])
        N2[m] = (hat * gain_two).astype(BF16)
        logits = jnp.where(lane < NE, nn(N2[m], small), -1e30)
        raised = jnp.exp(logits - jnp.max(logits, axis=-1, keepdims=True))
        GATES[m] = raised / jnp.sum(raised, axis=-1, keepdims=True)
        XS[m] = tn(PM[m, 0] + PM[m, 1], N2[m]).astype(BF16).reshape(NE, CP, D)
        weight = PM[m, 0].astype(F32) * chosen_of(m, 0) + PM[m, 1].astype(F32) * chosen_of(m, 1)
        CROW[0:1] = jnp.sum(weight, axis=0, keepdims=True)
        for k in range(NE):
            CSS[m, k, 0:1, 0:CP] = CROW[0:1, k * CP : (k + 1) * CP]

    diagonal = lax.broadcasted_iota(jnp.int32, (CP, 128), 0) == lax.broadcasted_iota(
        jnp.int32, (CP, 128), 1
    )

    def scale_grads(m):
        for p in range(NE):
            by_lane = CSB[m, p, 0:1]
            weight = jnp.sum(jnp.where(diagonal, by_lane, 0.0), axis=1, keepdims=True)
            GC[m, p * CP : (p + 1) * CP] = (weight * GRB[m, p].astype(F32)).astype(BF16)

    for m in range(M):
        forward(m)
        exchange(XS, XB, m, s_x[m], False)
        exchange(CSS, CSB, m, s_cs[m])
        if m == 0:
            arrived(WOUT.at[z, 1 - x], r_xo)
            pass_out(0, 1, False)
    pass_in(early, 2)
    pass_out(1, 0)
    for d in range(3, nz):
        pass_in(early, d)
    pass_out(1, 1, False)
    pass_in(others, 1)

    same = (
        lax.broadcasted_iota(jnp.int32, (D, D), 0) == lax.broadcasted_iota(jnp.int32, (D, D), 1)
    ).astype(BF16)
    for m in range(M):
        b["N1T"][m] = nt(same, N1[m]).astype(BF16)
        b["ATTT"][m] = nt(same, ATT[m]).astype(BF16)
    YACC, DXACC, AS, GHS = b["YACC"], b["DXACC"], b["AS"], b["GHS"]
    DWI, DWO = b["DWI"], b["DWO"]
    YACC[...] = jnp.zeros_like(YACC)
    DXACC[...] = jnp.zeros_like(DXACC)
    c0, c1 = math.sqrt(2.0 / math.pi), 0.044715

    OWN = (DWI, DWO)
    s_up = [(sends.take(1), sends.take(1)) for _ in range(2)]
    r_up = [(sems.take(nz * nz), sems.take(2 * nz)) for _ in range(2)]

    def expert_part(k, m, loop=True):
        def half(xx, carry):
            cols = pl.ds(pl.multiple_of(xx * CF, 128), CF)
            w_in = WIN[k, :, :, :, cols].reshape(D, CF)
            w_out = WOUT[k, xx]
            hidden = nn(XB[m].reshape(S, D), w_in)
            grad_acted = nt(GC[m], w_out)
            square = hidden * hidden
            bent = jnp.tanh(c0 * hidden * (1.0 + c1 * square))
            acted = (0.5 * hidden * (1.0 + bent)).astype(BF16)
            slope = 0.5 * (1.0 + bent) + 0.5 * c0 * hidden * (1.0 - bent * bent) * (
                1.0 + 3.0 * c1 * square
            )
            grad_hidden = (grad_acted * slope).astype(BF16)
            AS[m, :, cols] = acted
            GHS[m, :, cols] = grad_hidden
            YACC[m] = YACC[m] + nn(acted, w_out)
            DXACC[m] = DXACC[m] + nt(grad_hidden, w_in)
            return carry

        if loop:
            lax.fori_loop(0, 2, half, 0)
        else:
            half(0, 0)
            half(1, 0)

    def expert_weights(k, first, second):
        def half(xx, carry):
            cols = pl.ds(pl.multiple_of(xx * CF, 128), CF)
            if second:
                grads = GC[...].reshape(M * S, D)
                DWO[k, xx] = tn(AS[:, :, cols].reshape(M * S, CF), grads).astype(BF16)
            if first:
                part = tn(XB[...].reshape(M * S, D), GHS[:, :, cols].reshape(M * S, CF))
                DWI[k, :, :, :, cols] = part.astype(BF16).reshape(nz, 2, RF, CF)
            return carry

        lax.fori_loop(0, 2, half, 0)

    def sum_step(side, i, begins, parts):
        far = z if side == 0 else nz - 1 - z
        GOT = UP if side == 0 else DN
        turn = ((i % (nz - 1)) + 1) * jnp.minimum(i, 1)
        k = turn if side == 0 else nz - 1 - turn

        def tokens_side(j, carry):
            goal = nz - 1 - j
            t = goal if side == 0 else nz - 1 - goal
            rsem = r_up[side][0] + k * nz + t

            @pl.when(goal > far)
            def _():
                if not begins:
                    arrived(GOT[0].at[k, t], rsem)
                    DWI[k, t] = DWI[k, t] + GOT[0][k, t]
                send(DWI.at[k, t], GOT[0].at[k, t], s_up[side][0], rsem, onward(side))

            return carry

        def results_side():
            for part, xx, rows in (
                (1, 1 - x, slice(0, CF)),
                (2, x, slice(0, CF)),
                (3, x, slice(0, CF // 2)),
                (4, x, slice(CF // 2, CF)),
            ):
                if part not in parts:
                    continue
                rsem = r_up[side][1] + 2 * k + xx
                if not begins:
                    arrived(GOT[1].at[k, xx], rsem)
                    DWO[k, xx] = DWO[k, xx] + GOT[1][k, xx]
                source, target = DWO.at[k, xx, rows], GOT[1].at[k, xx, rows]
                send(source, target, s_up[side][1], rsem, onward(side))

        if parts != (0,):
            pl.when(turn == nz - 1)(results_side)
        if 0 in parts:
            lax.fori_loop(0, nz - 1, tokens_side, 0)
        if parts != (0,):
            pl.when((turn > far) & (turn < nz - 1))(results_side)

    def sums_begin(i, parts=(0, 1, 2)):
        for side in range(2):
            far = z if side == 0 else nz - 1 - z
            step = functools.partial(sum_step, side, jnp.int32(i), True, parts)
            pl.when(far == 0)(step)

    def sums_pass(far_at, i, parts=(0, 1, 2)):
        for side in range(2):
            far = z if side == 0 else nz - 1 - z
            step = functools.partial(sum_step, side, jnp.int32(i), False, parts)
            pl.when(far == far_at)(step)

    passes = [(far, i, part) for far in range(1, nz - 1) for i in range(nz) for part in range(3)]

    def sums_now(*wanted):
        for step in wanted:
            if step in passes:
                passes.remove(step)
                sums_pass(step[0], step[1], (step[2],))

    def sums_rest():
        for far in range(1, nz - 1):
            left = [step for step in passes if step[0] == far]
            if nz <= 4:
                for _, i, part in left:
                    sums_pass(far, i, (part,))
            else:

                def one(i, carry, far=far):
                    sums_pass(far, i)
                    return carry

                lax.fori_loop(left[0][1], nz, one, 0)

    for zz in range(nz):
        for side in range(2):
            count = nz - 1 - zz if side == 0 else zz
            if count > 0:
                sent_later(s_up[side][0], DWI.at[:, 0:count], z == zz)
                sent_later(s_up[side][1], DWO.at[0:count], z == zz)

    def give_back(m):
        gone(GSS, m, s_gr[m])
        gone(XS, m, s_x[m])
        DXS[m] = DXACC[m].astype(BF16).reshape(NE, CP, D)
        exchange(DXS, DXB, m, s_dx[m])
        results = YACC[m].astype(BF16)
        YS[m] = results.reshape(NE, CP, D)
        for p in range(NE):
            rows = slice(p * CP, (p + 1) * CP)
            weight = jnp.sum(
                results[rows].astype(F32) * GRB[m, p].astype(F32), axis=1, keepdims=True
            )
            GCS[m, p, 0:1] = jnp.sum(jnp.where(diagonal, weight, 0.0), axis=0, keepdims=True)
        exchange(GCS, GCB, m, s_gc[m])

    r_fin, s_fin = (sems.take(nz), sems.take(1)), (sends.take(1), sends.take(1))
    FX = (b["FXI"], b["FXO"])
    GI, GT = b["GI"], b["GT"]
    sent_later(s_fin[0], FX[0])
    sent_later(s_fin[1], FX[1])

    def total_of(kind, place):
        return (
            OWN[kind][place].astype(F32)
            + UP[kind][place].astype(F32)
            + DN[kind][place].astype(F32)
        )

    def sums_end_in(k):
        cols = pl.ds(pl.multiple_of(k * FC, 128), FC)
        for side, ref, ok in ((0, UP, z > 0), (1, DN, z < nz - 1)):
            arrived(ref[0].at[k, z], r_up[side][0] + k * nz + z, ok)
        FX[0][k] = total_of(0, (k, z, 1 - x)).astype(BF16)
        send(FX[0].at[k], GI.at[x, :, cols], s_fin[0], r_fin[0] + k, across)
        GI[x, :, cols] = total_of(0, (k, z, x)).astype(BF16)

    def sums_end_out(mine):
        xx = x if mine else 1 - x
        for side, ref, ok in ((0, UP, z > 0), (1, DN, z < nz - 1)):
            arrived(ref[1].at[z, xx], r_up[side][1] + 2 * z + xx, ok)
        if mine:
            GT[x] = total_of(1, (z, xx)).astype(BF16)
        else:
            FX[1][...] = total_of(1, (z, xx)).astype(BF16)
            send(FX[1], GT.at[x], s_fin[1], r_fin[1], across)

    at_end = (z == 0) | (z == nz - 1)
    upper = z // h
    first_ends = [nz - 1 - upper * (nz - 1), 1 + upper * (nz - 3)]
    last_ends = [upper * (nz - 1), 2 - upper * (5 - nz)] if nz == 4 else []

    when_two, when_far, when_late = (1, 2, nz - 1) if nz <= 4 else (0, 0, 0)
    for i in range(nz):
        if i == when_two:
            pass_out(2, 0)
            pass_out(2, 1, False)
        if i == when_far:
            pass_in(others, 2)
            if nz > 4:
                pass_out(0, 1, True)
            for d in range(3, nz):
                pass_in(others, d)
                pass_out(d, 0)
                pass_out(d, 1, False)
        if i == when_late:
            for d in range(1, nz):
                pass_out(d, 1, True)
            sums_now((1, 0, 0), (1, 0, 1), (1, 0, 2))
        block = turn_of(i) + (z // h) * (nz - 1 - 2 * turn_of(i))
        for m in range(M):
            if i == 0:
                exchanged(GRB, m, s_gr[m])
                exchanged(XB, m, s_x[m])
                exchanged(CSB, m, s_cs[m])
                scale_grads(m)
            expert_part(block, m, i == 1)
            if i == nz - 1:
                give_back(m)
        if i == nz - 1:
            for m in range(M):
                exchange(YS, YB, m, s_y[m])
        expert_weights(block, True, i > 0)
        sums_begin(i, (0, 1, 2) if i < nz - 1 else (0, 1, 3))
        if i == 0:
            expert_weights(block, False, True)

    def sums_close():
        kept.append(fetch(GI.at[x], gein.at[x]))
        kept.append(fetch(GT.at[x], geout.at[x]))
        arrived(GT.at[1 - x], r_fin[1])
        kept.append(fetch(GT.at[1 - x], geout.at[1 - x]))
        for k in range(nz):
            arrived(GI.at[1 - x, :, k * FC : (k + 1) * FC], r_fin[0] + k)
        kept.append(fetch(GI.at[1 - x], gein.at[1 - x]))

    GM, GA, GJ, GR = b["GM"], b["GA"], b["GJ"], b["GR"]
    GR[...] = jnp.zeros_like(GR)

    def outputs(m):
        results = YB[m].reshape(S, D)
        out = MID[m] + chosen_of(m, 0) * nn(PM[m, 0], results)
        b["AR"][:, m, :] = (out + chosen_of(m, 1) * nn(PM[m, 1], results))[0:T]

    def backward_top(m):
        upstream = CT[m].astype(F32)
        for k in range(NE):
            CROW[0:1, k * CP : (k + 1) * CP] = GCB[m, k, 0:1, 0:CP]

        def grad_chosen(j):
            return jnp.sum(PM[m, j].astype(F32) * CROW[0:1], axis=-1, keepdims=True)

        gates = GATES[m]
        grad_gates = jnp.where(onehot(m, 0), grad_chosen(0), 0.0) + jnp.where(
            onehot(m, 1), grad_chosen(1), 0.0
        )
        grad_logits = (
            gates * (grad_gates - jnp.sum(grad_gates * gates, axis=-1, keepdims=True))
        ).astype(BF16)
        GR[0:NE] = GR[0:NE] + tn(grad_logits, N2[m])[0:NE]
        grad = nn(PM[m, 0] + PM[m, 1], DXB[m].reshape(S, D)) + nt(grad_logits, small)
        hat, rstd = normalize(MID[m])
        GR[NE + 1 : NE + 2] = GR[NE + 1 : NE + 2] + jnp.sum(grad * hat, axis=0, keepdims=True)
        grad_middle = upstream + normalize_back(grad * gain_two, hat, rstd)
        GM[m] = grad_middle
        branch = grad_middle.astype(BF16)
        N2[m] = branch
        back = None
        for cols, block in proj.blocks():
            term = nt(branch[:, cols], block)
            back = term if back is None else back + term
        GA[m] = back.astype(BF16)

    def backward_heads(m):
        def attend(hp, carry):
            query, keys, values = (J[m, :, columns(i * D, hp)] for i in range(3))
            grads = GA[m, :, columns(0, hp)]
            grad_query = jnp.zeros((TP, pair), F32)
            grad_keys = jnp.zeros((TP, pair), F32)
            grad_values = jnp.zeros((TP, pair), F32)
            for i in range(2):
                part = half_of(query, i)
                upstream = half_of(grads, i)
                probs_low = b["PB"][m, 2 * hp + i]
                probs = probs_low.astype(F32)
                grad_probs = nt(upstream, values)
                grad_values = grad_values + tn(probs_low, upstream)
                grad_scores = (
                    probs
                    * (grad_probs - jnp.sum(grad_probs * probs, axis=-1, keepdims=True))
                ).astype(BF16)
                grad_query = grad_query + nn(grad_scores, half_of(keys, i))
                grad_keys = grad_keys + tn(grad_scores, part)
            GJ[m, :, columns(0, hp)] = (grad_query * scale).astype(BF16)
            GJ[m, :, columns(D, hp)] = (grad_keys * scale).astype(BF16)
            GJ[m, :, columns(2 * D, hp)] = grad_values.astype(BF16)
            return carry

        lax.fori_loop(0, D // pair, attend, 0)

    def backward_end(m, carry):
        grad = None
        for cols, block in qkv.blocks():
            term = nt(GJ[m, :, cols], block)
            grad = term if grad is None else grad + term
        hat, rstd = normalize(XP[m].astype(F32))
        GR[NE : NE + 1] = GR[NE : NE + 1] + jnp.sum(grad * hat, axis=0, keepdims=True)
        full = GM[m] + normalize_back(grad * gain_one, hat, rstd)
        b["IG"][m, :, 0, :] = full[0:T]
        return carry

    if nz <= 4:
        pass_out(0, 1, True)
    sums_now((1, 1, 0), (2, 0, 0))
    for m in range(M):
        exchanged(DXB, m, s_dx[m])
        exchanged(GCB, m, s_gc[m])
        backward_top(m)
        if m == 0:
            sums_now((1, 1, 1))
        if m == M - 1:
            proj.put(b["ATTT"], N2)
            proj.sum_core()
            sums_now((1, 2, 1))
        backward_heads(m)
        if m == 0:
            sums_now((2, 0, 1), (2, 0, 2), (1, 1, 2), (2, 1, 0))
    sums_now((1, 2, 2))
    proj.sum_plane()
    qkv.put(b["N1T"], GJ)
    GB, SB1, SB2, SB3, SB4 = (b[k] for k in ("GB", "SB1", "SB2", "SB3", "SB4"))
    qkv.sum_core()
    lax.fori_loop(0, M, backward_end, 0)
    kept.append(fetch(b["IG"], igrad))
    GB[...] = GR[...].astype(BF16)
    r_b1 = one_send(GB, SB1, sibling)
    qkv.sum_plane()
    proj.sum_cross()
    arrived(SB1, r_b1)
    SB2[y] = GB[...] + SB1[...]
    s_b2, r_b2 = sends.take(G - 1) - 1, sems.take(G - 1) - 1
    for d in range(1, G):
        send(SB2.at[y], SB2.at[y], s_b2 + d, r_b2 + d, at(z, x, ((y + d) % G) * 2 + core))
        sent_later(s_b2 + d, SB2.at[y])
    sums_now((2, 1, 1), (2, 1, 2), (2, 2, 1), (1, 2, 0), (2, 2, 2))
    if nz == 4:

        @pl.when(at_end)
        def _():
            for k in first_ends:
                sums_end_in(k)

    for d in range(1, G):
        arrived(SB2.at[(y + G - d) % G], r_b2 + d)
    total = SB2[0].astype(F32)
    for j in range(1, G):
        total = total + SB2[j].astype(F32)
    SB3[x] = total.astype(BF16)
    r_b3 = one_send(SB3.at[x], SB3.at[x], across)
    qkv.sum_cross()
    proj.sum_z()
    if nz == 4:
        pl.when(at_end)(functools.partial(sums_end_out, False))
    sums_now((1, 3, 0), (1, 3, 1), (1, 3, 2), (2, 2, 0))
    qkv.sum_z()
    arrived(SB3.at[1 - x], r_b3)
    SB4[z] = SB3[0] + SB3[1]
    s_b4, r_b4 = sends.take(1), sems.take(1)
    for dz in far_first:
        send(SB4.at[z], SB4.at[z], s_b4, r_b4, at((z + dz) % nz, x, e))
    sent_later(s_b4, SB4.at[0 : nz - 1])
    sums_begin(nz - 1, (4,))
    sums_rest()
    if nz != 4:
        sums_end_out(False)
    else:

        @pl.when(at_end)
        def _():
            for k in last_ends:
                sums_end_in(k)

        @pl.when(jnp.logical_not(at_end))
        def _():
            sums_end_out(False)
            for k in (0, nz - 1):
                sums_end_in(k)

    proj.hand_out()
    qkv.hand_out()
    if nz == 4:

        @pl.when(jnp.logical_not(at_end))
        def _():
            for k in range(1, nz - 1):
                sums_end_in(k)

    else:
        for k in range(nz):
            sums_end_in(k)
    for m in range(M):
        exchanged(YB, m, s_y[m])
        outputs(m)
    b["AO"][...] = b["AR"][...].astype(BF16)
    kept.append(fetch(b["AO"], act))
    arrived(SB4.at[0 : nz - 1], r_b4)
    total = SB4[0].astype(F32)
    for k in range(1, nz):
        total = total + SB4[k].astype(F32)
    mine = (
        lax.broadcasted_iota(jnp.int32, (D, RF), 0)
        == lax.broadcasted_iota(jnp.int32, (D, RF), 1) + f * RF
    ).astype(F32)
    b["GS"][...] = lax.dot_general(
        total,
        mine,
        (((1,), (0,)), ((), ())),
        precision=lax.Precision.HIGHEST,
        preferred_element_type=F32,
    )
    kept.append(fetch(b["GS"].at[0:NE], grouter))
    kept.append(fetch(b["GS"].at[NE : NE + 1], ggain1))
    kept.append(fetch(b["GS"].at[NE + 1 : NE + 2], ggain2))
    sums_end_out(True)
    sums_close()
    proj.leave(gout)
    qkv.leave(gqkv)
    for cond, copy in pending:
        when(cond, copy.wait_send)
    for copy in kept:
        copy.wait()
    used = (sends.used, sems.used, locals_.used)
    assert all(a <= b for a, b in zip(used, counts)), (used, counts)


def hand_over(*refs):
    source, target, held, sem = refs[:9], refs[9:18], refs[18:-1], refs[-1]
    cast = [k for k in range(9) if source[k].dtype != target[k].dtype]
    order = sorted(range(9), key=lambda k: -math.prod(target[k].shape))
    for k in order:
        pltpu.make_async_copy(source[k], held[k], sem.at[0, k]).start()
    for k in order:
        pltpu.make_async_copy(source[k], held[k], sem.at[0, k]).wait()
        ready = held[k]
        if k in cast:
            ready = held[9 + cast.index(k)]
            ready[...] = held[k][...].astype(ready.dtype)
        pltpu.make_async_copy(ready, target[k], sem.at[1, k]).start()
    for k in order:
        pltpu.make_async_copy(target[k], target[k], sem.at[1, k]).wait()


def body(
    mesh_shape,
    inputs,
    gain_attn,
    qkv_weight,
    out_weight,
    gain_moe,
    router_weight,
    expert_in,
    expert_out,
    routes,
    cotangent,
):
    micro, images, seq, width = inputs.shape
    c = layout(mesh_shape, micro, images * seq, width, expert_in.shape[2])
    rows = images * seq
    scratch = scratch_of(c)
    names = list(scratch)
    nz, G = c["nz"], c["G"]
    counts = (48 + 9 * (G - 1), 25 + 19 * nz + 2 * nz * nz + 9 * (G - 1), 19 + 2 * c["E"])
    shapes = (
        ((rows, micro, width), BF16),
        ((micro, rows, 1, width), F32),
        (qkv_weight.shape, F32),
        (out_weight.shape, F32),
        ((1, c["RF"]), F32),
        ((1, c["RF"]), F32),
        ((c["NE"], c["RF"]), F32),
        (expert_in.shape, F32),
        (expert_out.shape, F32),
    )
    shapes = [jax.ShapeDtypeStruct(s, t) for s, t in shapes]
    sums = (2, 3, 7, 8)
    halves = [
        jax.ShapeDtypeStruct(s.shape, BF16 if k in sums else s.dtype) for k, s in enumerate(shapes)
    ]
    anywhere = pl.BlockSpec(memory_space=pltpu.HBM)
    results = pl.pallas_call(
        functools.partial(kernel, c, names, counts),
        out_shape=halves,
        in_specs=[anywhere] * 10,
        out_specs=[anywhere] * 9,
        scratch_shapes=[pltpu.VMEM(s, t) for s, t in scratch.values()]
        + [pltpu.SemaphoreType.DMA((count,)) for count in counts],
        compiler_params=pltpu.CompilerParams(
            collective_id=0, has_side_effects=True, vmem_limit_bytes=60 * 1024 * 1024
        ),
    )(
        jnp.transpose(inputs, (1, 2, 0, 3)).reshape(rows, micro, width),
        jnp.transpose(cotangent, (1, 2, 0, 3)).reshape(rows, micro, width),
        jnp.transpose(routes, (0, 1, 3, 2)).reshape(micro, 2, rows),
        qkv_weight,
        out_weight,
        gain_attn[None, :],
        gain_moe[None, :],
        router_weight.T,
        expert_in,
        expert_out,
    )
    act, igrad, gqkv, gout, ggain1, ggain2, grouter, gein, geout = pl.pallas_call(
        hand_over,
        out_shape=shapes,
        in_specs=[anywhere] * 9,
        out_specs=[anywhere] * 9,
        scratch_shapes=[pltpu.VMEM(s.shape, s.dtype) for s in halves]
        + [pltpu.VMEM(shapes[k].shape, F32) for k in sums]
        + [pltpu.SemaphoreType.DMA((2, 9))],
        compiler_params=pltpu.CompilerParams(vmem_limit_bytes=60 * 1024 * 1024),
    )(*results)
    return (
        jnp.transpose(act.reshape(images, seq, micro, width), (2, 0, 1, 3)),
        igrad.reshape(inputs.shape),
        ggain1[0],
        gqkv,
        gout,
        ggain2[0],
        grouter.T,
        gein,
        geout,
    )


def solution(mesh):
    return jax.shard_map(
        functools.partial(body, dict(mesh.shape)),
        mesh=mesh,
        in_specs=(
            P(None, ("fsdp", "expert"), None, None),
            P("fsdp"),
            P("fsdp", None),
            P("fsdp", None),
            P("fsdp"),
            P("fsdp", None),
            P("expert", "fsdp", None),
            P("expert", "fsdp", None),
            P(None, ("fsdp", "expert"), None, None),
            P(None, ("fsdp", "expert"), None, None),
        ),
        out_specs=(
            P(None, ("fsdp", "expert"), None, None),
            P(None, ("fsdp", "expert"), None, None),
            P("fsdp"),
            P("fsdp", None),
            P("fsdp", None),
            P("fsdp"),
            P("fsdp", None),
            P("expert", "fsdp", None),
            P("expert", "fsdp", None),
        ),
        check_vma=False,
    )
```

```python
import functools
import math

import jax
import jax.numpy as jnp
from jax import lax
from jax.experimental import pallas as pl
from jax.experimental.pallas import tpu as pltpu
from jax.sharding import PartitionSpec as P

HEADS = 8
EPS = 1e-06
MESH = pl.DeviceIdType.MESH
F32 = jnp.float32
BF16 = jnp.bfloat16


def nn(a, b):
    return lax.dot_general(a, b, (((1,), (0,)), ((), ())), preferred_element_type=F32)


def nt(a, b):
    return lax.dot_general(a, b, (((1,), (1,)), ((), ())), preferred_element_type=F32)


def tn(a, b):
    return lax.dot_general(a, b, (((0,), (0,)), ((), ())), preferred_element_type=F32)


def normalize(values):
    center = jnp.mean(values, axis=-1, keepdims=True)
    shifted = values - center
    spread = jnp.mean(shifted * shifted, axis=-1, keepdims=True)
    rstd = lax.rsqrt(spread + EPS)
    return shifted * rstd, rstd


def normalize_back(grad, hat, rstd):
    return rstd * (
        grad
        - jnp.mean(grad, axis=-1, keepdims=True)
        - hat * jnp.mean(grad * hat, axis=-1, keepdims=True)
    )


class Semaphores:
    def __init__(self):
        self.used = 0

    def take(self, count):
        start = self.used
        self.used += count
        return start


SIZES = ("nz", "E", "G", "NE", "NR", "T", "TP", "CP", "S", "D", "FC", "RF", "CF", "M")


def layout(mesh_shape, micro, seq, width, ff_width):
    fsdp, peers = mesh_shape["fsdp"], mesh_shape["expert"]
    c = {}
    c["nz"] = fsdp // 2
    c["E"] = peers
    c["G"] = peers // 2
    c["NE"] = 2 * peers
    c["T"] = seq
    c["TP"] = -(-seq // 16) * 16
    c["CP"] = -(-max(2, 10 * seq // (4 * 2 * peers) + 1) // 16) * 16
    c["S"] = c["NE"] * c["CP"]
    c["NR"] = -(-(c["NE"] + 2) // 16) * 16
    c["D"] = width
    c["FF"] = ff_width
    c["RF"] = width // fsdp
    c["CF"] = ff_width // fsdp
    c["FC"] = 2 * c["CF"]
    c["WQ"] = 128 * -(-(3 * width // 128) // peers)
    c["WO"] = 128 * -(-(width // 128) // peers)
    c["M"] = micro
    return c


def scratch_of(c):
    nz, E, G, NE, NR, T, TP, CP, S, D, FC, RF, CF, M = (c[k] for k in SIZES)
    h = nz // 2
    v = {
        "XP": ((M, TP, D), BF16),
        "CT": ((M, TP, D), BF16),
        "XR": ((TP, M, D), BF16),
        "CR": ((TP, M, D), BF16),
        "AR": ((TP, M, D), F32),
        "AO": ((TP, M, D), BF16),
        "IG": ((M, TP, 1, D), F32),
        "RR": ((M, 2, T), jnp.int32),
        "RT": ((M, TP, 128), F32),
        "SR": ((nz, 2, NR, RF), BF16),
        "G1": ((1, RF), BF16),
        "G2": ((1, RF), BF16),
        "RW": ((NE, RF), BF16),
        "GI": ((2, RF, nz * FC), BF16),
        "GT": ((2, CF, D), BF16),
        "GS": ((NR, RF), F32),
        "SM": ((nz, 2, RF, 128), BF16),
        "WIN": ((nz, nz, 2, RF, FC), BF16),
        "WOUT": ((nz, 2, CF, D), BF16),
        "N1": ((M, TP, D), BF16),
        "J": ((M, TP, 3 * D), BF16),
        "ATT": ((M, TP, D), BF16),
        "MID": ((M, TP, D), F32),
        "N2": ((M, TP, D), BF16),
        "GATES": ((M, TP, 128), F32),
        "PB": ((M, HEADS, TP, TP), BF16),
        "N1T": ((M, D, TP), BF16),
        "ATTT": ((M, D, TP), BF16),
        "PM": ((M, 2, TP, S), BF16),
        "XS": ((M, NE, CP, D), BF16),
        "XB": ((M, NE, CP, D), BF16),
        "GSS": ((M, NE, CP, D), BF16),
        "GRB": ((M, NE, CP, D), BF16),
        "CSS": ((M, NE, 8, 128), F32),
        "CSB": ((M, NE, 8, 128), F32),
        "CROW": ((8, S), F32),
        "GC": ((M, S, D), BF16),
        "YB": ((M, NE, CP, D), BF16),
        "DXB": ((M, NE, CP, D), BF16),
        "GCS": ((M, NE, 8, 128), F32),
        "GCB": ((M, NE, 8, 128), F32),
        "YACC": ((M, S, D), F32),
        "DXACC": ((M, S, D), F32),
        "AS": ((M, S, FC), BF16),
        "GHS": ((M, S, FC), BF16),
        "DWI": ((nz, nz, 2, RF, FC), BF16),
        "DWO": ((nz, 2, CF, D), BF16),
        "UPI": ((nz, nz, 2, RF, FC), BF16),
        "UPO": ((nz, 2, CF, D), BF16),
        "DNI": ((nz, nz, 2, RF, FC), BF16),
        "DNO": ((nz, 2, CF, D), BF16),
        "FXI": ((nz, RF, FC), BF16),
        "FXO": ((CF, D), BF16),
        "GM": ((M, TP, D), F32),
        "GA": ((M, TP, D), BF16),
        "GJ": ((M, TP, 3 * D), BF16),
        "GR": ((NR, D), F32),
        "GB": ((NR, D), BF16),
        "SB1": ((NR, D), BF16),
        "SB2": ((G, NR, D), BF16),
        "SB3": ((2, NR, D), BF16),
        "SB4": ((nz, NR, D), BF16),
    }
    for name, wide in (("Q", c["WQ"]), ("O", c["WO"])):
        for part, lead in (
            ("W", (E, nz, 2)),
            ("G", (E, nz, 2)),
            ("B1", (G, nz, 2)),
            ("Y1", (G, h, 2)),
            ("X1", (G, nz - h)),
            ("X2", (h,)),
            ("Y2", (G, nz - h)),
            ("Z", (nz,)),
            ("F", (E,)),
        ):
            v[name + part] = (lead + (RF, wide), BF16)
    return v


def kernel(c, names, counts, *refs):
    nz, E, G, NE, NR, T, TP, CP, S, D, FC, RF, CF, M = (c[k] for k in SIZES)
    (xin, cot, routes, qkv_s, out_s, gain1, gain2, router, ein, eout) = refs[:10]
    (act, igrad, gqkv, gout, ggain1, ggain2, grouter, gein, geout) = refs[10:19]
    b = dict(zip(names, refs[19:]))
    SS, RS, LS = refs[-3:]
    h = nz // 2
    head = D // HEADS
    pair = 2 * head
    scale = 1.0 / math.sqrt(head)
    sems, sends, locals_ = Semaphores(), Semaphores(), Semaphores()
    pending = []

    f = lax.axis_index("fsdp")
    e = lax.axis_index("expert")
    z, x = f // 2, f % 2
    y, core = e // 2, e % 2
    pme = 2 * e + x

    def at(zz, xx, ee):
        return (zz * 2 + xx, ee)

    sibling = at(z, x, y * 2 + (1 - core))
    across = at(z, 1 - x, e)

    def copy_of(src, dst, ssem, rsem, device):
        return pltpu.make_async_remote_copy(
            src_ref=src,
            dst_ref=dst,
            send_sem=SS.at[ssem],
            recv_sem=RS.at[rsem],
            device_id=device,
            device_id_type=MESH,
        )

    def when(cond, run):
        if cond is None:
            run()
        else:
            pl.when(cond)(run)

    def send(src, dst, ssem, rsem, device, cond=None):
        when(cond, copy_of(src, dst, ssem, rsem, device).start)

    def arrived(dst, rsem, cond=None):
        when(cond, copy_of(dst, dst, 0, rsem, sibling).wait_recv)

    def sent_later(ssem, src, cond=None):
        pending.append((cond, copy_of(src, src, ssem, 0, sibling)))

    def one_send(src, dst, device):
        ssem, rsem = sends.take(1), sems.take(1)
        send(src, dst, ssem, rsem, device)
        sent_later(ssem, src)
        return rsem

    barrier = pltpu.get_barrier_semaphore()
    for dz in range(1, nz):
        pl.semaphore_signal(
            barrier, inc=1, device_id=at((z + dz) % nz, x, e), device_id_type=MESH
        )

    def greet(d, carry):
        p = (pme + d) % NE
        pl.semaphore_signal(barrier, inc=1, device_id=at(z, p % 2, p // 2), device_id_type=MESH)
        return carry

    lax.fori_loop(1, NE, greet, 0)

    SM, WIN, WOUT = b["SM"], b["WIN"], b["WOUT"]
    UP, DN = (b["UPI"], b["UPO"]), (b["DNI"], b["DNO"])

    def fetch(src, dst):
        copy = pltpu.make_async_copy(src, dst, LS.at[locals_.take(1)])
        copy.start()
        return copy

    near_first = [d for k in range(1, nz) for d in (k, nz - k) if 2 * k <= nz]
    orders = list(dict.fromkeys(near_first))
    far_first = [j + (1 - z // h) * (nz - 2 * j) for j in range(1, nz)]

    class Dense:
        def __init__(self, name, shard, wide):
            self.name, self.shard, self.wide = name, shard, wide
            self.w, self.g = b[name + "W"], b[name + "G"]
            self.used = -(-shard.shape[1] // wide)
            self.own = locals_.take(1)
            for k in range(self.used):

                @pl.when(e == k)
                def _():
                    pltpu.make_async_copy(
                        self.columns(shard, k), self.w.at[k, z, x], LS.at[self.own]
                    ).start()

        def columns(self, ref, k):
            return ref.at[:, k * self.wide : (k + 1) * self.wide]

        def own_ready(self):
            copy = pltpu.make_async_copy(
                self.w.at[e, z, x], self.w.at[e, z, x], LS.at[self.own]
            )
            when(None if self.used == E else e < self.used, copy.wait)

        def along_z(self):
            w = self.w
            self.r_z, s_z = sems.take(nz - 1) - 1, sends.take(1)
            for dz in orders:
                to = at((z + dz) % nz, x, e)
                send(w.at[e, z, x], w.at[e, z, x], s_z, self.r_z + dz, to)
            sent_later(s_z, w.at[e, 0 : nz - 1, x])
            self.s_x, self.r_x = sends.take(1), sems.take(nz)
            self.s_y, self.r_y = sends.take(G - 1) - 1, sems.take(G - 1) - 1
            self.s_c, self.r_c = sends.take(1), sems.take(1)
            sent_later(self.s_x, w.at[e, :, x])
            for d in range(1, G):
                sent_later(self.s_y + d, w.at[e, :, x])
            sent_later(self.s_c, w.at[0:G])

        def spread(self, dz):
            zz = (z + nz - dz) % nz
            piece = self.w.at[e, zz, x]
            if dz > 0:
                arrived(piece, self.r_z + dz)
            send(piece, piece, self.s_x, self.r_x + dz, across)
            for d in range(1, G):
                to = at(z, x, ((y + d) % G) * 2 + core)
                send(piece, piece, self.s_y + d, self.r_y + d, to)
            send(piece, piece, self.s_c, self.r_c, sibling)

        def forward(self):
            w = self.w
            self.s_xy, self.r_xy = sends.take(G - 1) - 1, sems.take(G - 1) - 1
            for d in range(1, G):
                sent_later(self.s_xy + d, w.at[e, :, x])
            for dz in [0] + orders:
                piece = w.at[e, (z + nz - dz) % nz, 1 - x]
                arrived(piece, self.r_x + dz)
                for d in range(1, G):
                    to = at(z, x, ((y + d) % G) * 2 + core)
                    send(piece, piece, self.s_xy + d, self.r_xy + d, to)
                send(piece, piece, self.s_c, self.r_c, sibling)

        def corner(self):
            w = self.w
            for d in range(1, G):
                ee = ((y + G - d) % G) * 2 + core
                arrived(w.at[ee, :, x], self.r_y + d)
                send(w.at[ee, :, x], w.at[ee, :, x], self.s_c, self.r_c, sibling)
                arrived(w.at[ee, :, 1 - x], self.r_xy + d)
                send(w.at[ee, :, 1 - x], w.at[ee, :, 1 - x], self.s_c, self.r_c, sibling)

        def ready(self):
            arrived(self.w.at[0:G], self.r_c)

        def blocks(self):
            for k in range(self.used):
                cols = slice(k * self.wide, min((k + 1) * self.wide, self.shard.shape[1]))
                yield cols, self.w[k].reshape(D, self.wide)

        def put(self, left, right):
            for k in range(self.used):
                cols = slice(k * self.wide, (k + 1) * self.wide)
                part = nn(left[0], right[0, :, cols])
                for m in range(1, M):
                    part = part + nn(left[m], right[m, :, cols])
                self.g[k] = part.astype(BF16).reshape(nz, 2, RF, self.wide)

        def sum_core(self):
            s, self.r_1 = sends.take(1), sems.take(1)
            for j in range(G):
                send(self.g.at[2 * j + 1 - core], b[self.name + "B1"].at[j], s, self.r_1, sibling)
            sent_later(s, b[self.name + "B1"])

        def sum_plane(self):
            g, first = self.g, b[self.name + "B1"]
            arrived(first, self.r_1)
            for j in range(G):
                g[2 * j + core] = g[2 * j + core] + first[j]
            s, self.r_y1 = sends.take(G - 1) - 1, sems.take(G - 1) - 1
            for d in range(1, G):
                q = (y + d) % G
                piece = g.at[2 * q + core, 0:h]
                send(piece, b[self.name + "Y1"].at[y], s + d, self.r_y1 + d, at(z, x, 2 * q + core))
                sent_later(s + d, piece)
            s, self.r_x1 = sends.take(1), sems.take(1)
            for j in range(G):
                piece = g.at[2 * j + core, h:nz, 1 - x]
                send(piece, b[self.name + "X1"].at[j], s, self.r_x1, across)
            sent_later(s, b[self.name + "X1"])

        def sum_cross(self):
            g, from_y, from_x = self.g, b[self.name + "Y1"], b[self.name + "X1"]
            for d in range(1, G):
                q = (y + G - d) % G
                arrived(from_y.at[q], self.r_y1 + d)
                g[e, 0:h] = g[e, 0:h] + from_y[q]
            self.r_x2 = one_send(g.at[e, 0:h, 1 - x], b[self.name + "X2"], across)
            arrived(from_x, self.r_x1)
            for j in range(G):
                g[2 * j + core, h:nz, x] = g[2 * j + core, h:nz, x] + from_x[j]
            s, self.r_y2 = sends.take(G - 1) - 1, sems.take(G - 1) - 1
            for d in range(1, G):
                q = (y + d) % G
                piece = g.at[2 * q + core, h:nz, x]
                send(piece, b[self.name + "Y2"].at[y], s + d, self.r_y2 + d, at(z, x, 2 * q + core))
                sent_later(s + d, piece)

        def sum_z(self):
            g, from_x, from_y = self.g, b[self.name + "X2"], b[self.name + "Y2"]
            arrived(from_x, self.r_x2)
            g[e, 0:h, x] = g[e, 0:h, x] + from_x[...]
            for d in range(1, G):
                q = (y + G - d) % G
                arrived(from_y.at[q], self.r_y2 + d)
                g[e, h:nz, x] = g[e, h:nz, x] + from_y[q]
            s, self.r_z2 = sends.take(1), sems.take(1)
            parts = b[self.name + "Z"]
            for dz in far_first:
                zz = (z + dz) % nz
                send(g.at[e, zz, x], parts.at[z], s, self.r_z2, at(zz, x, e))
            sent_later(s, parts.at[0 : nz - 1])
            parts[z] = g[e, z, x]

        def hand_out(self):
            parts, done = b[self.name + "Z"], b[self.name + "F"]
            arrived(parts.at[0 : nz - 1], self.r_z2)
            total = parts[0].astype(F32)
            for k in range(1, nz):
                total = total + parts[k].astype(F32)
            done[e] = total.astype(BF16)
            s, self.r_f = sends.take(1), sems.take(1)

            def one(d, carry):
                send(done.at[e], done.at[e], s, self.r_f, at(z, x, (e + d) % E))
                return carry

            lax.fori_loop(1, E, one, 0)
            sent_later(s, done.at[0 : E - 1])

        def leave(self, out):
            done = b[self.name + "F"]
            arrived(done.at[0 : E - 1], self.r_f)
            for k in range(self.used):
                kept.append(fetch(done.at[k], self.columns(out, k)))

    qkv, proj = Dense("Q", qkv_s, c["WQ"]), Dense("O", out_s, c["WO"])
    kept = []

    SR = b["SR"]
    SR[z, x] = jnp.zeros((NR, RF), BF16)
    small_in = [
        fetch(gain1, b["G1"]),
        fetch(gain2, b["G2"]),
        fetch(router, b["RW"]),
    ]
    token_in = [fetch(routes, b["RR"]), fetch(xin, b["XR"].at[0:T]), fetch(cot, b["CR"].at[0:T])]
    own_in = locals_.take(1)
    for k in range(nz):
        pltpu.make_async_copy(
            ein.at[x, :, k * FC : (k + 1) * FC], WIN.at[k, z, x], LS.at[own_in]
        ).start()
    own_out = fetch(eout.at[x], WOUT.at[z, x])

    for copy in small_in:
        copy.wait()
    SR[z, x, 0:NE] = b["RW"][...]
    SR[z, x, NE : NE + 1] = b["G1"][...]
    SR[z, x, NE + 1 : NE + 2] = b["G2"][...]
    entry = lax.broadcasted_iota(jnp.int32, (NR, 128), 0)
    place = lax.broadcasted_iota(jnp.int32, (NR, 128), 1)
    pick = (
        ((entry < NE) & (entry == place))
        | ((entry >= NE) & (entry < NE + 2) & (place == entry - NE + 126))
    ).astype(BF16)
    qkv.own_ready()
    proj.own_ready()
    pl.semaphore_wait(barrier, nz - 1 + NE - 1)

    qkv.along_z()
    r_sz, s_sz = sems.take(1), sends.take(1)
    for dz in orders:
        send(SR.at[z, x], SR.at[z, x], s_sz, r_sz, at((z + dz) % nz, x, e))
    sent_later(s_sz, SR.at[0 : nz - 1, x])
    qkv.spread(0)

    s_xi, r_xi = sends.take(1), sems.take(1)
    for k in range(nz):
        send(ein.at[1 - x, :, k * FC : (k + 1) * FC], WIN.at[k, z, x], s_xi, r_xi, across)
    sent_later(s_xi, WIN.at[:, z, x])


    XP, CT, RT, PM = b["XP"], b["CT"], b["RT"], b["PM"]

    @pl.when(z == 0)
    def _():
        UP[0][:, 0] = jnp.zeros((nz, 2, RF, FC), BF16)
        UP[1][0] = jnp.zeros((2, CF, D), BF16)

    @pl.when(z == nz - 1)
    def _():
        DN[0][:, nz - 1] = jnp.zeros((nz, 2, RF, FC), BF16)
        DN[1][nz - 1] = jnp.zeros((2, CF, D), BF16)

    for copy in token_in:
        copy.wait()
    lane = lax.broadcasted_iota(jnp.int32, (TP, 128), 1)
    lane_f = lane.astype(F32)
    swap = (
        lax.broadcasted_iota(jnp.int32, (2, 128), 0) == lax.broadcasted_iota(jnp.int32, (2, 128), 1)
    ).astype(BF16)
    for ref in (b["XR"], b["CR"]):
        ref[T:TP] = jnp.zeros((TP - T, M, D), BF16)
    for m in range(M):
        RT[m] = jnp.full((TP, 128), -1.0, F32)
        XP[m] = b["XR"][:, m, :]
        CT[m] = b["CR"][:, m, :]
        RT[m, 0:T] = tn(b["RR"][m].astype(BF16), swap)

    def onehot(m, j):
        return RT[m][:, j : j + 1] == lane_f

    before = (
        lax.broadcasted_iota(jnp.int32, (TP, TP), 1) < lax.broadcasted_iota(jnp.int32, (TP, TP), 0)
    ).astype(BF16)
    spots = lax.broadcasted_iota(jnp.int32, (TP, S), 1).astype(F32)
    for m in range(M):
        first = onehot(m, 0).astype(F32)
        second = onehot(m, 1).astype(F32)
        rank0 = nn(before, first.astype(BF16))
        rank1 = nn(before, second.astype(BF16)) + jnp.sum(first, axis=0, keepdims=True)
        for j, (hot, rank) in enumerate(((first, rank0), (second, rank1))):
            slot = jnp.sum(hot * rank, axis=-1, keepdims=True)
            route = RT[m][:, j : j + 1]
            spot = jnp.where(route >= 0, route * CP + slot, -1.0)
            PM[m, j] = (spots == spot).astype(BF16)

    def turn_of(i):
        return 0 if i == 0 else i % (nz - 1) + 1

    groups = (range(0, 2), range(2, nz))
    s_zi = [[sends.take(1) for _ in groups] for _ in range(2)]
    s_zo = [sends.take(1) for _ in range(2)]
    r_zi = [[sems.take(nz) for _ in groups] for _ in range(2)]
    r_zo = [sems.take(2 * nz) for _ in range(2)]
    for zz in range(nz):
        for side in range(2):
            count = zz + 1 if side == 0 else nz - zz
            if count < nz:
                for g, turns in enumerate(groups):
                    sent_later(s_zi[side][g], WIN.at[0 : len(turns), 0:count], z == zz)
                sent_later(s_zo[side], WOUT.at[0:count], z == zz)

    def reach(side, d, some=None):
        begun = z - d if side == 0 else z + d
        there = (begun >= 0) if side == 0 else (begun < nz)
        last = (z == nz - 1) if side == 0 else (z == 0)
        if some is not None:
            there = there & some(begun)
        return begun, there, there & jnp.logical_not(last)

    def onward(side):
        return at((z + 1) % nz if side == 0 else (z + nz - 1) % nz, x, e)

    def pass_in(g, d, halves=(0, 1)):
        for side in range(2):
            begun, there, goes = reach(side, d)
            r = r_zi[side][g]
            if d > 0:
                arrived(WIN.at[0 : len(groups[g]), begun], r + d, there)
            if d < nz - 1:

                @pl.when(goes)
                def _():
                    for i in groups[g]:
                        k = turn_of(i) if side == 1 else nz - 1 - turn_of(i)
                        for half in halves:
                            piece = WIN.at[k, begun, x if half == 0 else 1 - x]
                            send(piece, piece, s_zi[side][g], r + d + 1, onward(side))

    def pass_out(d, half, late=None):
        xx = x if half == 0 else 1 - x
        for side in range(2):
            odd = nz - 2 if side == 0 else 1
            some = None
            if late is not None:
                some = (lambda begun: begun == odd) if late else (lambda begun: begun != odd)
            begun, there, goes = reach(side, d, some)
            r = r_zo[side] + 2 * d + half
            piece = WOUT.at[begun, xx]
            if d > 0:
                arrived(piece, r, there)
            if d < nz - 1:
                send(piece, piece, s_zo[side], r + 2, onward(side), goes)

    early, others = 0, 1
    GATES, XS, XB, GC, CROW = (b[k] for k in ("GATES", "XS", "XB", "GC", "CROW"))
    GSS, GRB, CSS, CSB = (b[k] for k in ("GSS", "GRB", "CSS", "CSB"))
    GCS, GCB, YB, DXB = (b[k] for k in ("GCS", "GCB", "YB", "DXB"))
    YS, DXS = XS, GSS

    def gone(src, m, sem):
        copy_of(src.at[m, 0 : NE - 1], src.at[m, 0 : NE - 1], sem[0], 0, sibling).wait_send()

    def exchange(src, dst, m, sem, later=True):
        rows = slice(0, 1 if src.shape[2] == 8 else src.shape[2])

        def one(d, carry):
            p = (pme + d) % NE
            send(src.at[m, p, rows], dst.at[m, pme, rows], *sem, at(z, p % 2, p // 2))
            return carry

        lax.fori_loop(1, NE, one, 0)
        if later:
            sent_later(sem[0], src.at[m, 0 : NE - 1, rows])
        dst[m, pme] = src[m, pme]

    def exchanged(dst, m, sem):
        rows = slice(0, 1 if dst.shape[2] == 8 else dst.shape[2])
        arrived(dst.at[m, 0 : NE - 1, rows], sem[1])

    def pairs():
        return [(sends.take(1), sems.take(1)) for _ in range(M)]

    s_x, s_cs, s_gr, s_dx, s_gc, s_y = (pairs() for _ in range(6))
    for m in range(M):
        GSS[m] = tn(PM[m, 0] + PM[m, 1], CT[m]).astype(BF16).reshape(NE, CP, D)

    for dz in orders[:2]:
        qkv.spread(dz)
    proj.along_z()
    proj.spread(0)
    pltpu.make_async_copy(WIN.at[:, z, x], WIN.at[:, z, x], LS.at[own_in]).wait()
    pass_in(early, 0, (0,))
    for dz in orders[2:]:
        qkv.spread(dz)
    arrived(SR.at[0 : nz - 1, x], r_sz)
    r_sx = one_send(SR.at[:, x], SR.at[:, x], across)
    own_out.wait()
    pass_out(0, 0)
    arrived(WIN.at[:, z, 1 - x], r_xi)
    pass_in(early, 0, (1,))
    qkv.forward()
    for dz in orders:
        proj.spread(dz)
    proj.forward()
    r_xo = one_send(eout.at[1 - x], WOUT.at[z, x], across)
    for m in range(M):
        exchange(GSS, GRB, m, s_gr[m], False)
    pass_in(others, 0, (0,))
    arrived(SR.at[:, 1 - x], r_sx)
    for zz in range(nz):
        for xx in range(2):
            SM[zz, xx] = tn(SR[zz, xx], pick).astype(BF16)
    qkv.corner()
    qkv.ready()

    small = SM[...].reshape(D, 128)
    gains = nt(pick, small)
    gain_one, gain_two = gains[NE : NE + 1], gains[NE + 1 : NE + 2]
    key_ok = lax.broadcasted_iota(jnp.int32, (1, TP), 1) < T
    low_half = lax.broadcasted_iota(jnp.int32, (1, pair), 1) < head
    N1, J, ATT, MID, N2 = b["N1"], b["J"], b["ATT"], b["MID"], b["N2"]
    def half_of(value, i):
        keep = low_half if i == 0 else jnp.logical_not(low_half)
        return jnp.where(keep, value, jnp.zeros_like(value))

    def softmax_scores(query, keys):
        scores = jnp.where(key_ok, nt(query, keys) * scale, -1e30)
        raised = jnp.exp(scores - jnp.max(scores, axis=-1, keepdims=True))
        return raised * (1.0 / jnp.sum(raised, axis=-1, keepdims=True))

    def columns(base, hp):
        return pl.ds(pl.multiple_of(base + hp * pair, 128), pair)

    def chosen_of(m, j):
        gates = GATES[m]
        return jnp.sum(jnp.where(onehot(m, j), gates, 0.0), axis=-1, keepdims=True)

    def forward(m):
        tokens = XP[m].astype(F32)
        hat, _ = normalize(tokens)
        N1[m] = (hat * gain_one).astype(BF16)
        for cols, block in qkv.blocks():
            J[m, :, cols] = nn(N1[m], block).astype(BF16)

        def attend(hp, carry):
            query, keys, values = (J[m, :, columns(i * D, hp)] for i in range(3))
            total = jnp.zeros((TP, pair), F32)
            for i in range(2):
                probs = softmax_scores(half_of(query, i), keys)
                probs = probs.astype(BF16)
                b["PB"][m, 2 * hp + i] = probs
                total = total + nn(probs, half_of(values, i))
            ATT[m, :, columns(0, hp)] = total.astype(BF16)
            return carry

        lax.fori_loop(0, D // pair, attend, 0)
        if m == 0:
            pass_in(early, 1)
            pass_in(others, 0, (1,))
            proj.corner()
            proj.ready()
        for cols, block in proj.blocks():
            MID[m, :, cols] = XP[m, :, cols].astype(F32) + nn(ATT[m], block)
        hat, _ = normalize(MID[m])
        N2[m] = (hat * gain_two).astype(BF16)
        logits = jnp.where(lane < NE, nn(N2[m], small), -1e30)
        raised = jnp.exp(logits - jnp.max(logits, axis=-1, keepdims=True))
        GATES[m] = raised / jnp.sum(raised, axis=-1, keepdims=True)
        XS[m] = tn(PM[m, 0] + PM[m, 1], N2[m]).astype(BF16).reshape(NE, CP, D)
        weight = PM[m, 0].astype(F32) * chosen_of(m, 0) + PM[m, 1].astype(F32) * chosen_of(m, 1)
        CROW[0:1] = jnp.sum(weight, axis=0, keepdims=True)
        for k in range(NE):
            CSS[m, k, 0:1, 0:CP] = CROW[0:1, k * CP : (k + 1) * CP]

    diagonal = lax.broadcasted_iota(jnp.int32, (CP, 128), 0) == lax.broadcasted_iota(
        jnp.int32, (CP, 128), 1
    )

    def scale_grads(m):
        for p in range(NE):
            by_lane = CSB[m, p, 0:1]
            weight = jnp.sum(jnp.where(diagonal, by_lane, 0.0), axis=1, keepdims=True)
            GC[m, p * CP : (p + 1) * CP] = (weight * GRB[m, p].astype(F32)).astype(BF16)

    for m in range(M):
        forward(m)
        exchange(XS, XB, m, s_x[m], False)
        exchange(CSS, CSB, m, s_cs[m])
        if m == 0:
            arrived(WOUT.at[z, 1 - x], r_xo)
            pass_out(0, 1, False)
    pass_in(early, 2)
    pass_out(1, 0)
    for d in range(3, nz):
        pass_in(early, d)
    pass_out(1, 1, False)
    pass_in(others, 1)

    same = (
        lax.broadcasted_iota(jnp.int32, (D, D), 0) == lax.broadcasted_iota(jnp.int32, (D, D), 1)
    ).astype(BF16)
    for m in range(M):
        b["N1T"][m] = nt(same, N1[m]).astype(BF16)
        b["ATTT"][m] = nt(same, ATT[m]).astype(BF16)
    YACC, DXACC, AS, GHS = b["YACC"], b["DXACC"], b["AS"], b["GHS"]
    DWI, DWO = b["DWI"], b["DWO"]
    YACC[...] = jnp.zeros_like(YACC)
    DXACC[...] = jnp.zeros_like(DXACC)
    c0, c1 = math.sqrt(2.0 / math.pi), 0.044715

    OWN = (DWI, DWO)
    s_up = [(sends.take(1), sends.take(1)) for _ in range(2)]
    r_up = [(sems.take(nz * nz), sems.take(2 * nz)) for _ in range(2)]

    def expert_part(k, m, loop=True):
        def half(xx, carry):
            cols = pl.ds(pl.multiple_of(xx * CF, 128), CF)
            w_in = WIN[k, :, :, :, cols].reshape(D, CF)
            w_out = WOUT[k, xx]
            hidden = nn(XB[m].reshape(S, D), w_in)
            grad_acted = nt(GC[m], w_out)
            square = hidden * hidden
            bent = jnp.tanh(c0 * hidden * (1.0 + c1 * square))
            acted = (0.5 * hidden * (1.0 + bent)).astype(BF16)
            slope = 0.5 * (1.0 + bent) + 0.5 * c0 * hidden * (1.0 - bent * bent) * (
                1.0 + 3.0 * c1 * square
            )
            grad_hidden = (grad_acted * slope).astype(BF16)
            AS[m, :, cols] = acted
            GHS[m, :, cols] = grad_hidden
            YACC[m] = YACC[m] + nn(acted, w_out)
            DXACC[m] = DXACC[m] + nt(grad_hidden, w_in)
            return carry

        if loop:
            lax.fori_loop(0, 2, half, 0)
        else:
            half(0, 0)
            half(1, 0)

    def expert_weights(k, first, second):
        def half(xx, carry):
            cols = pl.ds(pl.multiple_of(xx * CF, 128), CF)
            if second:
                grads = GC[...].reshape(M * S, D)
                DWO[k, xx] = tn(AS[:, :, cols].reshape(M * S, CF), grads).astype(BF16)
            if first:
                part = tn(XB[...].reshape(M * S, D), GHS[:, :, cols].reshape(M * S, CF))
                DWI[k, :, :, :, cols] = part.astype(BF16).reshape(nz, 2, RF, CF)
            return carry

        lax.fori_loop(0, 2, half, 0)

    def sum_step(side, i, begins, parts):
        far = z if side == 0 else nz - 1 - z
        GOT = UP if side == 0 else DN
        turn = ((i % (nz - 1)) + 1) * jnp.minimum(i, 1)
        k = turn if side == 0 else nz - 1 - turn

        def tokens_side(j, carry):
            goal = nz - 1 - j
            t = goal if side == 0 else nz - 1 - goal
            rsem = r_up[side][0] + k * nz + t

            @pl.when(goal > far)
            def _():
                if not begins:
                    arrived(GOT[0].at[k, t], rsem)
                    DWI[k, t] = DWI[k, t] + GOT[0][k, t]
                send(DWI.at[k, t], GOT[0].at[k, t], s_up[side][0], rsem, onward(side))

            return carry

        def results_side():
            for part, xx, rows in (
                (1, 1 - x, slice(0, CF)),
                (2, x, slice(0, CF)),
                (3, x, slice(0, CF // 2)),
                (4, x, slice(CF // 2, CF)),
            ):
                if part not in parts:
                    continue
                rsem = r_up[side][1] + 2 * k + xx
                if not begins:
                    arrived(GOT[1].at[k, xx], rsem)
                    DWO[k, xx] = DWO[k, xx] + GOT[1][k, xx]
                source, target = DWO.at[k, xx, rows], GOT[1].at[k, xx, rows]
                send(source, target, s_up[side][1], rsem, onward(side))

        if parts != (0,):
            pl.when(turn == nz - 1)(results_side)
        if 0 in parts:
            lax.fori_loop(0, nz - 1, tokens_side, 0)
        if parts != (0,):
            pl.when((turn > far) & (turn < nz - 1))(results_side)

    def sums_begin(i, parts=(0, 1, 2)):
        for side in range(2):
            far = z if side == 0 else nz - 1 - z
            step = functools.partial(sum_step, side, jnp.int32(i), True, parts)
            pl.when(far == 0)(step)

    def sums_pass(far_at, i, parts=(0, 1, 2)):
        for side in range(2):
            far = z if side == 0 else nz - 1 - z
            step = functools.partial(sum_step, side, jnp.int32(i), False, parts)
            pl.when(far == far_at)(step)

    passes = [(far, i, part) for far in range(1, nz - 1) for i in range(nz) for part in range(3)]

    def sums_now(*wanted):
        for step in wanted:
            if step in passes:
                passes.remove(step)
                sums_pass(step[0], step[1], (step[2],))

    def sums_rest():
        for far in range(1, nz - 1):
            left = [step for step in passes if step[0] == far]
            if nz <= 4:
                for _, i, part in left:
                    sums_pass(far, i, (part,))
            else:

                def one(i, carry, far=far):
                    sums_pass(far, i)
                    return carry

                lax.fori_loop(left[0][1], nz, one, 0)

    for zz in range(nz):
        for side in range(2):
            count = nz - 1 - zz if side == 0 else zz
            if count > 0:
                sent_later(s_up[side][0], DWI.at[:, 0:count], z == zz)
                sent_later(s_up[side][1], DWO.at[0:count], z == zz)

    def give_back(m):
        gone(GSS, m, s_gr[m])
        gone(XS, m, s_x[m])
        DXS[m] = DXACC[m].astype(BF16).reshape(NE, CP, D)
        exchange(DXS, DXB, m, s_dx[m])
        results = YACC[m].astype(BF16)
        YS[m] = results.reshape(NE, CP, D)
        for p in range(NE):
            rows = slice(p * CP, (p + 1) * CP)
            weight = jnp.sum(
                results[rows].astype(F32) * GRB[m, p].astype(F32), axis=1, keepdims=True
            )
            GCS[m, p, 0:1] = jnp.sum(jnp.where(diagonal, weight, 0.0), axis=0, keepdims=True)
        exchange(GCS, GCB, m, s_gc[m])

    r_fin, s_fin = (sems.take(nz), sems.take(1)), (sends.take(1), sends.take(1))
    FX = (b["FXI"], b["FXO"])
    GI, GT = b["GI"], b["GT"]
    sent_later(s_fin[0], FX[0])
    sent_later(s_fin[1], FX[1])

    def total_of(kind, place):
        return (
            OWN[kind][place].astype(F32)
            + UP[kind][place].astype(F32)
            + DN[kind][place].astype(F32)
        )

    def sums_end_in(k):
        cols = pl.ds(pl.multiple_of(k * FC, 128), FC)
        for side, ref, ok in ((0, UP, z > 0), (1, DN, z < nz - 1)):
            arrived(ref[0].at[k, z], r_up[side][0] + k * nz + z, ok)
        FX[0][k] = total_of(0, (k, z, 1 - x)).astype(BF16)
        send(FX[0].at[k], GI.at[x, :, cols], s_fin[0], r_fin[0] + k, across)
        GI[x, :, cols] = total_of(0, (k, z, x)).astype(BF16)

    def sums_end_out(mine):
        xx = x if mine else 1 - x
        for side, ref, ok in ((0, UP, z > 0), (1, DN, z < nz - 1)):
            arrived(ref[1].at[z, xx], r_up[side][1] + 2 * z + xx, ok)
        if mine:
            GT[x] = total_of(1, (z, xx)).astype(BF16)
        else:
            FX[1][...] = total_of(1, (z, xx)).astype(BF16)
            send(FX[1], GT.at[x], s_fin[1], r_fin[1], across)

    at_end = (z == 0) | (z == nz - 1)
    upper = z // h
    first_ends = [nz - 1 - upper * (nz - 1), 1 + upper * (nz - 3)]
    last_ends = [upper * (nz - 1), 2 - upper * (5 - nz)] if nz == 4 else []

    when_two, when_far, when_late = (1, 2, nz - 1) if nz <= 4 else (0, 0, 0)
    for i in range(nz):
        if i == when_two:
            pass_out(2, 0)
            pass_out(2, 1, False)
        if i == when_far:
            pass_in(others, 2)
            if nz > 4:
                pass_out(0, 1, True)
            for d in range(3, nz):
                pass_in(others, d)
                pass_out(d, 0)
                pass_out(d, 1, False)
        if i == when_late:
            for d in range(1, nz):
                pass_out(d, 1, True)
            sums_now((1, 0, 0), (1, 0, 1), (1, 0, 2))
        block = turn_of(i) + (z // h) * (nz - 1 - 2 * turn_of(i))
        for m in range(M):
            if i == 0:
                exchanged(GRB, m, s_gr[m])
                exchanged(XB, m, s_x[m])
                exchanged(CSB, m, s_cs[m])
                scale_grads(m)
            expert_part(block, m, i == 1)
            if i == nz - 1:
                give_back(m)
        if i == nz - 1:
            for m in range(M):
                exchange(YS, YB, m, s_y[m])
        expert_weights(block, True, i > 0)
        sums_begin(i, (0, 1, 2) if i < nz - 1 else (0, 1, 3))
        if i == 0:
            expert_weights(block, False, True)

    def sums_close():
        kept.append(fetch(GI.at[x], gein.at[x]))
        kept.append(fetch(GT.at[x], geout.at[x]))
        arrived(GT.at[1 - x], r_fin[1])
        kept.append(fetch(GT.at[1 - x], geout.at[1 - x]))
        for k in range(nz):
            arrived(GI.at[1 - x, :, k * FC : (k + 1) * FC], r_fin[0] + k)
        kept.append(fetch(GI.at[1 - x], gein.at[1 - x]))

    GM, GA, GJ, GR = b["GM"], b["GA"], b["GJ"], b["GR"]
    GR[...] = jnp.zeros_like(GR)

    def outputs(m):
        results = YB[m].reshape(S, D)
        out = MID[m] + chosen_of(m, 0) * nn(PM[m, 0], results)
        b["AR"][:, m, :] = out + chosen_of(m, 1) * nn(PM[m, 1], results)

    def backward_top(m):
        upstream = CT[m].astype(F32)
        for k in range(NE):
            CROW[0:1, k * CP : (k + 1) * CP] = GCB[m, k, 0:1, 0:CP]

        def grad_chosen(j):
            return jnp.sum(PM[m, j].astype(F32) * CROW[0:1], axis=-1, keepdims=True)

        gates = GATES[m]
        grad_gates = jnp.where(onehot(m, 0), grad_chosen(0), 0.0) + jnp.where(
            onehot(m, 1), grad_chosen(1), 0.0
        )
        grad_logits = (
            gates * (grad_gates - jnp.sum(grad_gates * gates, axis=-1, keepdims=True))
        ).astype(BF16)
        GR[0:NE] = GR[0:NE] + tn(grad_logits, N2[m])[0:NE]
        grad = nn(PM[m, 0] + PM[m, 1], DXB[m].reshape(S, D)) + nt(grad_logits, small)
        hat, rstd = normalize(MID[m])
        GR[NE + 1 : NE + 2] = GR[NE + 1 : NE + 2] + jnp.sum(grad * hat, axis=0, keepdims=True)
        grad_middle = upstream + normalize_back(grad * gain_two, hat, rstd)
        GM[m] = grad_middle
        branch = grad_middle.astype(BF16)
        N2[m] = branch
        back = None
        for cols, block in proj.blocks():
            term = nt(branch[:, cols], block)
            back = term if back is None else back + term
        GA[m] = back.astype(BF16)

    def backward_heads(m):
        def attend(hp, carry):
            query, keys, values = (J[m, :, columns(i * D, hp)] for i in range(3))
            grads = GA[m, :, columns(0, hp)]
            grad_query = jnp.zeros((TP, pair), F32)
            grad_keys = jnp.zeros((TP, pair), F32)
            grad_values = jnp.zeros((TP, pair), F32)
            for i in range(2):
                part = half_of(query, i)
                upstream = half_of(grads, i)
                probs_low = b["PB"][m, 2 * hp + i]
                probs = probs_low.astype(F32)
                grad_probs = nt(upstream, values)
                grad_values = grad_values + tn(probs_low, upstream)
                grad_scores = (
                    probs
                    * (grad_probs - jnp.sum(grad_probs * probs, axis=-1, keepdims=True))
                ).astype(BF16)
                grad_query = grad_query + nn(grad_scores, half_of(keys, i))
                grad_keys = grad_keys + tn(grad_scores, part)
            GJ[m, :, columns(0, hp)] = (grad_query * scale).astype(BF16)
            GJ[m, :, columns(D, hp)] = (grad_keys * scale).astype(BF16)
            GJ[m, :, columns(2 * D, hp)] = grad_values.astype(BF16)
            return carry

        lax.fori_loop(0, D // pair, attend, 0)

    def backward_end(m, carry):
        grad = None
        for cols, block in qkv.blocks():
            term = nt(GJ[m, :, cols], block)
            grad = term if grad is None else grad + term
        hat, rstd = normalize(XP[m].astype(F32))
        GR[NE : NE + 1] = GR[NE : NE + 1] + jnp.sum(grad * hat, axis=0, keepdims=True)
        full = GM[m] + normalize_back(grad * gain_one, hat, rstd)
        b["IG"][m, :, 0, :] = full
        return carry

    if nz <= 4:
        pass_out(0, 1, True)
    sums_now((1, 1, 0), (2, 0, 0))
    for m in range(M):
        exchanged(DXB, m, s_dx[m])
        exchanged(GCB, m, s_gc[m])
        backward_top(m)
        if m == 0:
            sums_now((1, 1, 1))
        if m == M - 1:
            proj.put(b["ATTT"], N2)
            proj.sum_core()
            sums_now((1, 2, 1))
        backward_heads(m)
        if m == 0:
            sums_now((2, 0, 1), (2, 0, 2), (1, 1, 2), (2, 1, 0))
    sums_now((1, 2, 2))
    proj.sum_plane()
    qkv.put(b["N1T"], GJ)
    GB, SB1, SB2, SB3, SB4 = (b[k] for k in ("GB", "SB1", "SB2", "SB3", "SB4"))
    qkv.sum_core()
    lax.fori_loop(0, M, backward_end, 0)
    kept.append(fetch(b["IG"].at[:, 0:T], igrad))
    GB[...] = GR[...].astype(BF16)
    r_b1 = one_send(GB, SB1, sibling)
    qkv.sum_plane()
    proj.sum_cross()
    arrived(SB1, r_b1)
    SB2[y] = GB[...] + SB1[...]
    s_b2, r_b2 = sends.take(G - 1) - 1, sems.take(G - 1) - 1
    for d in range(1, G):
        send(SB2.at[y], SB2.at[y], s_b2 + d, r_b2 + d, at(z, x, ((y + d) % G) * 2 + core))
        sent_later(s_b2 + d, SB2.at[y])
    sums_now((2, 1, 1), (2, 1, 2), (2, 2, 1), (1, 2, 0), (2, 2, 2))
    if nz == 4:

        @pl.when(at_end)
        def _():
            for k in first_ends:
                sums_end_in(k)

    for d in range(1, G):
        arrived(SB2.at[(y + G - d) % G], r_b2 + d)
    total = SB2[0].astype(F32)
    for j in range(1, G):
        total = total + SB2[j].astype(F32)
    SB3[x] = total.astype(BF16)
    r_b3 = one_send(SB3.at[x], SB3.at[x], across)
    qkv.sum_cross()
    proj.sum_z()
    if nz == 4:
        pl.when(at_end)(functools.partial(sums_end_out, False))
    sums_now((1, 3, 0), (1, 3, 1), (1, 3, 2), (2, 2, 0))
    qkv.sum_z()
    arrived(SB3.at[1 - x], r_b3)
    SB4[z] = SB3[0] + SB3[1]
    s_b4, r_b4 = sends.take(1), sems.take(1)
    for dz in far_first:
        send(SB4.at[z], SB4.at[z], s_b4, r_b4, at((z + dz) % nz, x, e))
    sent_later(s_b4, SB4.at[0 : nz - 1])
    sums_begin(nz - 1, (4,))
    sums_rest()
    if nz != 4:
        sums_end_out(False)
    else:

        @pl.when(at_end)
        def _():
            for k in last_ends:
                sums_end_in(k)

        @pl.when(jnp.logical_not(at_end))
        def _():
            sums_end_out(False)
            for k in (0, nz - 1):
                sums_end_in(k)

    proj.hand_out()
    qkv.hand_out()
    if nz == 4:

        @pl.when(jnp.logical_not(at_end))
        def _():
            for k in range(1, nz - 1):
                sums_end_in(k)

    else:
        for k in range(nz):
            sums_end_in(k)
    for m in range(M):
        exchanged(YB, m, s_y[m])
        outputs(m)
    b["AO"][...] = b["AR"][...].astype(BF16)
    kept.append(fetch(b["AO"].at[0:T], act))
    arrived(SB4.at[0 : nz - 1], r_b4)
    total = SB4[0].astype(F32)
    for k in range(1, nz):
        total = total + SB4[k].astype(F32)
    mine = (
        lax.broadcasted_iota(jnp.int32, (D, RF), 0)
        == lax.broadcasted_iota(jnp.int32, (D, RF), 1) + f * RF
    ).astype(F32)
    b["GS"][...] = lax.dot_general(
        total,
        mine,
        (((1,), (0,)), ((), ())),
        precision=lax.Precision.HIGHEST,
        preferred_element_type=F32,
    )
    kept.append(fetch(b["GS"].at[0:NE], grouter))
    kept.append(fetch(b["GS"].at[NE : NE + 1], ggain1))
    kept.append(fetch(b["GS"].at[NE + 1 : NE + 2], ggain2))
    sums_end_out(True)
    sums_close()
    proj.leave(gout)
    qkv.leave(gqkv)
    for cond, copy in pending:
        when(cond, copy.wait_send)
    for copy in kept:
        copy.wait()
    used = (sends.used, sems.used, locals_.used)
    assert all(a <= b for a, b in zip(used, counts)), (used, counts)


def hand_over(*refs):
    source, target, held, sem = refs[:9], refs[9:18], refs[18:-1], refs[-1]
    cast = [k for k in range(9) if source[k].dtype != target[k].dtype]
    order = sorted(range(9), key=lambda k: -math.prod(target[k].shape))
    for k in order:
        pltpu.make_async_copy(source[k], held[k], sem.at[0, k]).start()
    for k in order:
        pltpu.make_async_copy(source[k], held[k], sem.at[0, k]).wait()
        ready = held[k]
        if k in cast:
            ready = held[9 + cast.index(k)]
            ready[...] = held[k][...].astype(ready.dtype)
        pltpu.make_async_copy(ready, target[k], sem.at[1, k]).start()
    for k in order:
        pltpu.make_async_copy(target[k], target[k], sem.at[1, k]).wait()


def body(
    mesh_shape,
    inputs,
    gain_attn,
    qkv_weight,
    out_weight,
    gain_moe,
    router_weight,
    expert_in,
    expert_out,
    routes,
    cotangent,
):
    micro, images, seq, width = inputs.shape
    c = layout(mesh_shape, micro, images * seq, width, expert_in.shape[2])
    rows = images * seq
    scratch = scratch_of(c)
    names = list(scratch)
    nz, G = c["nz"], c["G"]
    counts = (48 + 9 * (G - 1), 25 + 19 * nz + 2 * nz * nz + 9 * (G - 1), 19 + 2 * c["E"])
    shapes = (
        ((rows, micro, width), BF16),
        ((micro, rows, 1, width), F32),
        (qkv_weight.shape, F32),
        (out_weight.shape, F32),
        ((1, c["RF"]), F32),
        ((1, c["RF"]), F32),
        ((c["NE"], c["RF"]), F32),
        (expert_in.shape, F32),
        (expert_out.shape, F32),
    )
    shapes = [jax.ShapeDtypeStruct(s, t) for s, t in shapes]
    sums = (2, 3, 7, 8)
    halves = [
        jax.ShapeDtypeStruct(s.shape, BF16 if k in sums else s.dtype) for k, s in enumerate(shapes)
    ]
    anywhere = pl.BlockSpec(memory_space=pltpu.HBM)
    results = pl.pallas_call(
        functools.partial(kernel, c, names, counts),
        out_shape=halves,
        in_specs=[anywhere] * 10,
        out_specs=[anywhere] * 9,
        scratch_shapes=[pltpu.VMEM(s, t) for s, t in scratch.values()]
        + [pltpu.SemaphoreType.DMA((count,)) for count in counts],
        compiler_params=pltpu.CompilerParams(
            collective_id=0, has_side_effects=True, vmem_limit_bytes=60 * 1024 * 1024
        ),
    )(
        jnp.transpose(inputs, (1, 2, 0, 3)).reshape(rows, micro, width),
        jnp.transpose(cotangent, (1, 2, 0, 3)).reshape(rows, micro, width),
        jnp.transpose(routes, (0, 1, 3, 2)).reshape(micro, 2, rows),
        qkv_weight,
        out_weight,
        gain_attn[None, :],
        gain_moe[None, :],
        router_weight.T,
        expert_in,
        expert_out,
    )
    act, igrad, gqkv, gout, ggain1, ggain2, grouter, gein, geout = pl.pallas_call(
        hand_over,
        out_shape=shapes,
        in_specs=[anywhere] * 9,
        out_specs=[anywhere] * 9,
        scratch_shapes=[pltpu.VMEM(s.shape, s.dtype) for s in halves]
        + [pltpu.VMEM(shapes[k].shape, F32) for k in sums]
        + [pltpu.SemaphoreType.DMA((2, 9))],
        compiler_params=pltpu.CompilerParams(vmem_limit_bytes=60 * 1024 * 1024),
    )(*results)
    return (
        jnp.transpose(act.reshape(images, seq, micro, width), (2, 0, 1, 3)),
        igrad.reshape(inputs.shape),
        ggain1[0],
        gqkv,
        gout,
        ggain2[0],
        grouter.T,
        gein,
        geout,
    )


def solution(mesh):
    return jax.shard_map(
        functools.partial(body, dict(mesh.shape)),
        mesh=mesh,
        in_specs=(
            P(None, ("fsdp", "expert"), None, None),
            P("fsdp"),
            P("fsdp", None),
            P("fsdp", None),
            P("fsdp"),
            P("fsdp", None),
            P("expert", "fsdp", None),
            P("expert", "fsdp", None),
            P(None, ("fsdp", "expert"), None, None),
            P(None, ("fsdp", "expert"), None, None),
        ),
        out_specs=(
            P(None, ("fsdp", "expert"), None, None),
            P(None, ("fsdp", "expert"), None, None),
            P("fsdp"),
            P("fsdp", None),
            P("fsdp", None),
            P("fsdp"),
            P("fsdp", None),
            P("expert", "fsdp", None),
            P("expert", "fsdp", None),
        ),
        check_vma=False,
    )
```
